32 devices in a mesh: dp: 4 (over z), seq: 8 (over y, x, core).
Axes of the slice: x: 2, y: 2, z: 4, core: 2. Of those that a mesh axis runs over, the one named last changes fastest.
Arguments:
- inputs: bfloat16 [4, 4096, 1536], P('dp', 'seq'), may hold values from -6 to 6
- segments: int32 [4, 4096], P('dp'), may hold values from 0 to 3, as said below
- attn_gain: bfloat16 [1536], P(('dp', 'seq')), may hold values from 0.5 to 1.5
- query_weight: bfloat16 [1536, 1536], P(('dp', 'seq')), may hold values from -0.15625 to 0.15625
- key_weight: bfloat16 [1536, 1536], P(('dp', 'seq')), may hold values from -0.15625 to 0.15625
- value_weight: bfloat16 [1536, 1536], P(('dp', 'seq')), may hold values from -0.15625 to 0.15625
- output_weight: bfloat16 [1536, 1536], P(('dp', 'seq')), may hold values from -2.5 to 2.5
- persistent: bfloat16 [1536, 64], P(('dp', 'seq')), may hold values from -6 to 6
- memory_first: bfloat16 [1536, 384], P(('dp', 'seq')), may hold values from -0.625 to 0.625
- memory_second: bfloat16 [1536, 384], P(('dp', 'seq')), may hold values from -0.3125 to 0.3125
- rate_weight: bfloat16 [1536, 16], P(('dp', 'seq')), may hold values from -0.15625 to 0.15625
- decay_logit: float32 [16], replicated, may hold values from -4 to -1.4
- momentum_logit: float32 [16], replicated, may hold values from 0 to 2.2
- ffn_gain: bfloat16 [1536], P(('dp', 'seq')), may hold values from 0.5 to 1.5
- gate_weight: bfloat16 [1536, 4096], P(('dp', 'seq')), may hold values from -0.15625 to 0.15625
- up_weight: bfloat16 [1536, 4096], P(('dp', 'seq')), may hold values from -0.15625 to 0.15625
- down_weight: bfloat16 [4096, 1536], P(('dp', 'seq')), may hold values from -0.09375 to 0.09375
- cotangent: bfloat16 [4, 4096, 1536], P('dp', 'seq'), may hold values from -6 to 6
Outputs:
- result: bfloat16 [4, 4096, 1536], P('dp', 'seq')
- grad_inputs: bfloat16 [4, 4096, 1536], P('dp', 'seq')
- grad_attn_gain: float32 [1536], P(('dp', 'seq'))
- grad_query_weight: float32 [1536, 1536], P(('dp', 'seq'))
- grad_key_weight: float32 [1536, 1536], P(('dp', 'seq'))
- grad_value_weight: float32 [1536, 1536], P(('dp', 'seq'))
- grad_output_weight: float32 [1536, 1536], P(('dp', 'seq'))
- grad_persistent: float32 [1536, 64], P(('dp', 'seq'))
- grad_memory_first: float32 [1536, 384], P(('dp', 'seq'))
- grad_memory_second: float32 [1536, 384], P(('dp', 'seq'))
- grad_rate_weight: float32 [1536, 16], P(('dp', 'seq'))
- grad_decay_logit: float32 [16], replicated
- grad_momentum_logit: float32 [16], replicated
- grad_ffn_gain: float32 [1536], P(('dp', 'seq'))
- grad_gate_weight: float32 [1536, 4096], P(('dp', 'seq'))
- grad_up_weight: float32 [1536, 4096], P(('dp', 'seq'))
- grad_down_weight: float32 [4096, 1536], P(('dp', 'seq'))
The draws below stay inside these ranges and needn't reach their ends.
Inputs may be any that keep to these rules, and one draw needn't show every extreme that they name: `segments`: ids never fall along a row and the first token of a row has id 0. In every row one document covers all tokens but some of the first 512 and some of the last 512; all other document boundaries lie inside those two blocks.
All inputs are finite; a program needn't handle non-finite values.
Results may differ from the reference program's by a relative error of at most 0.022.
Values may be sent and summed in bfloat16 or wider, within the bound.
No kernel may reach another device: no remote copies, remote signals or barrier semaphores. Data moves between devices by JAX's collectives and lax.ppermute only.
A program may use at most 576 MiB of HBM per device.

```python
from functools import partial
import jax
import jax.numpy as jnp
from jax import lax

D = 1536
H = 16
HD = 96
MH = 384
FF = 4096
NP = 64
GROUP = 512
ROWS = 4
SEQLEN = 4096


def draw_segments(key, part):
    key = jax.random.fold_in(key, 7)
    keys = jax.random.split(key, 3)
    start = jax.random.randint(keys[0], (ROWS, 1), 2, GROUP)
    early = 1 + jax.random.randint(keys[1], (ROWS, 1), 0, GROUP) % (start - 1)
    finish = jax.random.randint(keys[2], (ROWS, 1), SEQLEN - GROUP + 1, SEQLEN)
    order = jnp.arange(SEQLEN, dtype=jnp.int32)[None, :]
    ids = (order >= early).astype(jnp.int32) + (order >= start).astype(jnp.int32) + (order >= finish).astype(jnp.int32)
    return ids.astype(jnp.int32)


def shard_levels(key, shape, shards, least, largest):
    def one(axis_at, parts):
        steps = jax.random.uniform(jax.random.fold_in(jax.random.fold_in(key, 6), axis_at), (parts,), jnp.float32, least / len(shards), largest / len(shards))
        return jnp.repeat(jnp.exp(steps), shape[axis_at] // parts).reshape((-1,) + (1,) * (len(shape) - axis_at - 1))

    level = one(*shards[0])
    for cut in shards[1:]:
        level = level * one(*cut)
    return level


def scatter_about(key, extent, spread, reach, cuts=(), held_as=jnp.bfloat16):
    factor_of = shard_levels(key, extent, cuts, -0.22, 0.18) if cuts else 1.0
    array = jax.random.normal(key, extent, jnp.float32) * spread * factor_of
    return jnp.minimum(jnp.maximum(array, -reach), reach).astype(held_as)


def setup_inputs(seed: int = 0) -> dict:
    arg_keys = jax.random.split(jax.random.key(seed), 19)
    inputs = scatter_about(arg_keys[0], (ROWS, SEQLEN, D), 1.0, 6.0, ((0, 4), (1, 8)))
    segments = draw_segments(jax.random.fold_in(arg_keys[18], 71), 0)
    attn_gain = jnp.clip(1.0 + 0.1 * jax.random.normal(arg_keys[2], (D,), jnp.float32), 0.5, 1.5).astype(jnp.bfloat16)
    query_weight = scatter_about(arg_keys[3], (D, D), D ** -0.5, 0.15625, ((0, 32),))
    key_weight = scatter_about(arg_keys[4], (D, D), D ** -0.5, 0.15625, ((0, 32),))
    value_weight = scatter_about(arg_keys[5], (D, D), D ** -0.5, 0.15625, ((0, 32),))
    output_weight = scatter_about(arg_keys[6], (D, D), (max(D // 256, 1)) ** -0.5, 2.5, ((0, 32),))
    persistent = scatter_about(arg_keys[7], (D, NP), 1.0, 6.0, ((0, 32),))
    memory_first = scatter_about(arg_keys[8], (D, MH), HD ** -0.5, 0.625, ((0, 32),))
    memory_second = scatter_about(arg_keys[9], (D, MH), MH ** -0.5, 0.3125, ((0, 32),))
    rate_weight = scatter_about(arg_keys[10], (D, H), D ** -0.5, 0.15625, ((0, 32),))
    decay_logit = jnp.clip(jax.random.uniform(arg_keys[11], (H,), jnp.float32, -4.0, -1.4), -4.0, -1.4)
    momentum_logit = jnp.clip(jax.random.uniform(arg_keys[12], (H,), jnp.float32, 0.0, 2.2), 0.0, 2.2)
    ffn_gain = jnp.clip(1.0 + 0.1 * jax.random.normal(arg_keys[13], (D,), jnp.float32), 0.5, 1.5).astype(jnp.bfloat16)
    gate_weight = scatter_about(arg_keys[14], (D, FF), D ** -0.5, 0.15625, ((0, 32),))
    up_weight = scatter_about(arg_keys[15], (D, FF), D ** -0.5, 0.15625, ((0, 32),))
    down_weight = scatter_about(arg_keys[16], (FF, D), FF ** -0.5, 0.09375, ((0, 32),))
    cotangent = scatter_about(arg_keys[17], (ROWS, SEQLEN, D), 1.0, 6.0, ((0, 4), (1, 8)))
    return dict(inputs=inputs, segments=segments, attn_gain=attn_gain, query_weight=query_weight, key_weight=key_weight, value_weight=value_weight, output_weight=output_weight, persistent=persistent, memory_first=memory_first, memory_second=memory_second, rate_weight=rate_weight, decay_logit=decay_logit, momentum_logit=momentum_logit, ffn_gain=ffn_gain, gate_weight=gate_weight, up_weight=up_weight, down_weight=down_weight, cotangent=cotangent)


HIGH = lax.Precision.HIGHEST
norm_epsilon = 1e-06
rate_numerator = 2.0
masked_score = -1e+30

@jax.custom_vjp
def low(v):
    return lax.optimization_barrier(v.astype(jnp.bfloat16)).astype(jnp.float32)

@jax.custom_vjp
def low_back(v):
    return v

def low_keep(v):
    return (low(v), None)

def low_pass(kept, grad):
    return (grad,)

def back_keep(v):
    return (v, None)

def back_low(kept, grad):
    return (low(grad),)
low.defvjp(low_keep, low_pass)
low_back.defvjp(back_keep, back_low)

def high_dot(left, right):
    return jnp.dot(left, right, precision=HIGH, preferred_element_type=jnp.float32)

def rms_normed(values, gain):
    return values * lax.rsqrt(lax.optimization_barrier(jnp.mean(values * values, axis=-1, keepdims=True)) + norm_epsilon) * gain

def head_normed(values):
    return values * lax.rsqrt(lax.optimization_barrier(jnp.mean(values * values, axis=-1, keepdims=True)) + norm_epsilon)

def recall(first, second, probes):
    inner = jnp.einsum('chd,hdm->chm', probes, first, precision=HIGH)
    return jnp.einsum('chm,hdm->chd', jax.nn.silu(inner), second, precision=HIGH)

def recall_mix(state_first, state_second, init_first, init_second, probes, retain):
    kept = retain[:, None, None]
    return kept * recall(state_first, state_second, probes) + (1.0 - kept) * recall(init_first, init_second, probes)

def memory_step(state, first_init, second_init, keys, values, rates, update_mask, carry_flag, decay, momentum):
    base_first = carry_flag * state[0] + (1.0 - carry_flag) * first_init
    base_second = carry_flag * state[1] + (1.0 - carry_flag) * second_init
    weights = rates * update_mask[:, None]

    def inner_loss(first, second):
        error = recall(first, second, keys) - values
        return 0.5 * jnp.sum(weights[:, :, None] * error * error) / keys.shape[0]
    grad_first, grad_second = jax.grad(inner_loss, argnums=(0, 1))(base_first, base_second)
    speed_first = momentum[:, None, None] * carry_flag * state[2] - grad_first
    speed_second = momentum[:, None, None] * carry_flag * state[3] - grad_second
    keep = (1.0 - decay)[:, None, None]
    return jnp.stack([keep * base_first + speed_first, keep * base_second + speed_second, speed_first, speed_second])

def visible(ids):
    order = jnp.arange(GROUP)
    local = jnp.logical_and(order[None, :] <= order[:, None], ids[None, :] == ids[:, None])
    return jnp.concatenate([jnp.ones((GROUP, NP), bool), local, local], axis=1)

def group_flags(row_ids):
    ids = row_ids.reshape(-1, GROUP)
    count = ids.shape[0]
    first = ids[:, 0]
    last = ids[:, GROUP - 1]
    before = jnp.concatenate([first[:1], ids[:-1, GROUP - 1]])
    joined = jnp.logical_and(jnp.arange(count) > 0, first == before)
    carry_flag = jnp.logical_and(joined, first == last).astype(jnp.float32)
    retain = jnp.logical_and(joined[:, None], ids == first[:, None]).astype(jnp.float32)
    update_mask = (ids == last[:, None]).astype(jnp.float32)
    return (ids, retain, update_mask, carry_flag)

def group_forward(params, state, piece):
    attn_gain, query_weight, key_weight, value_weight, output_weight, persistent, memory_first, memory_second, rate_weight, decay_logit, momentum_logit, ffn_gain, gate_weight, up_weight, down_weight = params
    tokens, ids, retain, update_mask, carry_flag = piece
    first_init = memory_first.reshape(H, HD, MH)
    second_init = memory_second.reshape(H, HD, MH)
    normed = low(rms_normed(tokens, attn_gain))
    query = low_back(high_dot(normed, query_weight))
    local_keys = low_back(high_dot(normed, key_weight))
    local_values = low_back(high_dot(normed, value_weight))
    rates = rate_numerator / MH * jax.nn.sigmoid(low_back(high_dot(normed, rate_weight)))
    probes = head_normed(query.reshape(GROUP, H, HD))
    mem_keys = head_normed(local_keys.reshape(GROUP, H, HD))
    mem_values = local_values.reshape(GROUP, H, HD)
    recalled = low(recall_mix(state[0], state[1], first_init, second_init, probes, retain).reshape(GROUP, D))
    new_state = memory_step(state, first_init, second_init, mem_keys, mem_values, rates, update_mask, carry_flag, jax.nn.sigmoid(decay_logit), jax.nn.sigmoid(momentum_logit))
    context = jnp.concatenate([persistent.T, recalled], axis=0)
    keys_all = low(jnp.concatenate([low_back(high_dot(context, key_weight)), local_keys], axis=0))
    values_all = low(jnp.concatenate([low_back(high_dot(context, value_weight)), local_values], axis=0))
    scores = jnp.einsum('qhd,khd->hqk', low(query).reshape(GROUP, H, HD), keys_all.reshape(-1, H, HD), precision=HIGH) * HD ** (-0.5)
    scores = jnp.where(visible(ids)[None], low_back(scores), masked_score)
    chances = low(jax.nn.softmax(scores, axis=-1))
    mixed = jnp.einsum('hqk,khd->qhd', chances, values_all.reshape(-1, H, HD), precision=HIGH).reshape(GROUP, D)
    mixed = low(low_back(mixed))
    middle = tokens + low_back(high_dot(mixed, output_weight))
    normed_two = low(rms_normed(middle, ffn_gain))
    gate = low_back(high_dot(normed_two, gate_weight))
    up = low_back(high_dot(normed_two, up_weight))
    hidden = low(jax.nn.silu(gate) * up)
    return (new_state, middle + low_back(high_dot(hidden, down_weight)))

def layer_row(params, tokens_row, flags):
    ids, retain, update_mask, carry_flag = flags
    pieces = tokens_row.reshape(-1, GROUP, tokens_row.shape[-1])
    start = jnp.zeros((4, H, HD, MH), jnp.float32)
    stepper = jax.checkpoint(partial(group_forward, params))
    final, outs = lax.scan(stepper, start, (pieces, ids, retain, update_mask, carry_flag))
    return outs.reshape(tokens_row.shape)

def reference(inputs, segments, attn_gain, query_weight, key_weight, value_weight, output_weight, persistent, memory_first, memory_second, rate_weight, decay_logit, momentum_logit, ffn_gain, gate_weight, up_weight, down_weight, cotangent):
    params = tuple((p.astype(jnp.float32) for p in (attn_gain, query_weight, key_weight, value_weight, output_weight, persistent, memory_first, memory_second, rate_weight, decay_logit, momentum_logit, ffn_gain, gate_weight, up_weight, down_weight)))

    def row_turn(totals, row):
        tokens_row, row_ids, grad_row = row
        flags = group_flags(row_ids)
        outcome, pullback = jax.vjp(lambda p, t: layer_row(p, t, flags), params, tokens_row)
        gradients, grad_tokens = pullback(grad_row)
        return (jax.tree.map(jnp.add, totals, gradients), (outcome, grad_tokens))
    zeros = jax.tree.map(jnp.zeros_like, params)
    totals, (outcomes, grad_tokens) = lax.scan(row_turn, zeros, (inputs.astype(jnp.float32), segments, cotangent.astype(jnp.float32)))
    g_attn_gain, g_query, g_key, g_value, g_output, g_persistent, g_first, g_second, g_rate, g_decay, g_momentum, g_ffn_gain, g_gate, g_up, g_down = totals
    return (outcomes.astype(jnp.bfloat16), grad_tokens.astype(jnp.bfloat16), g_attn_gain, g_query, g_key, g_value, g_output, g_persistent, g_first, g_second, g_rate, g_decay, g_momentum, g_ffn_gain, g_gate, g_up, g_down)
```

```python
import jax
import jax.numpy as jnp
from jax import lax
from jax.experimental import pallas as pl
from jax.experimental.pallas import tpu as pltpu
from jax.sharding import PartitionSpec as P

D = 1536
H = 16
HD = 96
MH = 384
NP = 64
GROUP = 512
RATE_ROWS = 16
norm_epsilon = 1e-06
f32 = jnp.float32
bf16 = jnp.bfloat16


def dot_nn(left, right):
    return lax.dot_general(left, right, (((1,), (0,)), ((), ())), preferred_element_type=f32)


def dot_tn(left, right):
    return lax.dot_general(left, right, (((0,), (0,)), ((), ())), preferred_element_type=f32)


def dot_nt(left, right):
    return lax.dot_general(left, right, (((1,), (1,)), ((), ())), preferred_element_type=f32)


def inverse_root(values):
    return lax.rsqrt(jnp.mean(values * values, axis=0, keepdims=True) + norm_epsilon)


def memory_forward_kernel(
    heads,
    blocks,
    flags,
    keys_ref,
    values_ref,
    probes_ref,
    rates_ref,
    retain_ref,
    update_ref,
    first_ref,
    second_ref,
    scalars_ref,
    recalled_ref,
    saved_ref,
    state,
):
    turn = pl.program_id(0)

    @pl.when(turn == 0)
    def blank():
        state[...] = jnp.zeros_like(state)

    saved_ref[0] = state[...]
    retain = retain_ref[0]

    def recall_with(first, second, head):
        rows = slice(head * HD, (head + 1) * HD)
        raw = probes_ref[0, rows, :].astype(f32)
        probes = (raw * inverse_root(raw)).astype(bf16)
        inner = dot_tn(first[rows, :].astype(bf16), probes)
        return dot_nn(second[rows, :].astype(bf16), jax.nn.silu(inner).astype(bf16))

    only_state = flags[1, turn] * (1 - flags[2, turn])
    only_init = flags[2, turn] * (1 - flags[1, turn])

    @pl.when(only_state == 1)
    def from_state():
        for head in range(heads):
            recalled_ref[0, head * HD : (head + 1) * HD, :] = recall_with(
                state[0], state[1], head
            ).astype(bf16)

    @pl.when(only_init == 1)
    def from_init():
        for head in range(heads):
            recalled_ref[0, head * HD : (head + 1) * HD, :] = recall_with(
                first_ref[...], second_ref[...], head
            ).astype(bf16)

    @pl.when(only_state + only_init == 0)
    def from_both():
        for head in range(heads):
            recalled_ref[0, head * HD : (head + 1) * HD, :] = (
                retain * recall_with(state[0], state[1], head)
                + (1.0 - retain) * recall_with(first_ref[...], second_ref[...], head)
            ).astype(bf16)

    @pl.when(turn < blocks - 1)
    def step():
        carry = flags[0, turn].astype(f32)
        for head in range(heads):
            rows = slice(head * HD, (head + 1) * HD)
            keep = scalars_ref[0, head]
            push = scalars_ref[1, head] * carry
            base_first = jnp.where(carry > 0.5, state[0, rows, :], first_ref[rows, :])
            base_second = jnp.where(carry > 0.5, state[1, rows, :], second_ref[rows, :])
            raw = keys_ref[0, rows, :].astype(f32)
            keys = (raw * inverse_root(raw)).astype(bf16)
            second_low = base_second.astype(bf16)
            inner = dot_tn(base_first.astype(bf16), keys)
            gate = jax.nn.sigmoid(inner)
            active = inner * gate
            slope = gate + active * (1.0 - gate)
            active_low = active.astype(bf16)
            weight = rates_ref[0, head : head + 1, :].astype(f32) * update_ref[0] * (1.0 / GROUP)
            error = dot_nn(second_low, active_low) - values_ref[0, rows, :].astype(f32)
            pull = (error * weight).astype(bf16)
            inner_pull = (dot_tn(second_low, pull) * slope).astype(bf16)
            speed_first = push * state[2, rows, :] - dot_nt(keys, inner_pull)
            speed_second = push * state[3, rows, :] - dot_nt(pull, active_low)
            state[0, rows, :] = keep * base_first + speed_first
            state[1, rows, :] = keep * base_second + speed_second
            state[2, rows, :] = speed_first
            state[3, rows, :] = speed_second


def memory_forward(flags, packed, probes, retain, update, first, second, scalars):
    chips, rows, width = probes.shape
    heads = rows // HD
    blocks = chips * width // GROUP
    per = width // GROUP

    def block(turn, flags):
        return (turn // per, 0, (turn % per) ^ flags[3, 0])

    def by_turn(turn, flags):
        return (turn, 0, 0)

    def whole(turn, flags):
        return (0, 0)

    def value_block(turn, flags):
        return (turn // per, 1, (turn % per) ^ flags[3, 0])

    def rate_block(turn, flags):
        return (turn // per, 2 * rows // RATE_ROWS, (turn % per) ^ flags[3, 0])

    part = pl.BlockSpec((1, rows, GROUP), block)
    line = pl.BlockSpec((1, 1, GROUP), by_turn)
    return pl.pallas_call(
        lambda *refs: memory_forward_kernel(heads, blocks, *refs),
        grid_spec=pltpu.PrefetchScalarGridSpec(
            num_scalar_prefetch=1,
            grid=(blocks,),
            in_specs=[
                part,
                pl.BlockSpec((1, rows, GROUP), value_block),
                part,
                pl.BlockSpec((1, RATE_ROWS, GROUP), rate_block),
                line,
                line,
                pl.BlockSpec((rows, MH), whole),
                pl.BlockSpec((rows, MH), whole),
                pl.BlockSpec(memory_space=pltpu.SMEM),
            ],
            out_specs=[
                part,
                pl.BlockSpec((1, 4, rows, MH), lambda turn, flags: (turn, 0, 0, 0)),
            ],
            scratch_shapes=[pltpu.VMEM((4, rows, MH), f32)],
        ),
        out_shape=[
            jax.ShapeDtypeStruct(probes.shape, bf16),
            jax.ShapeDtypeStruct((blocks, 4, rows, MH), f32),
        ],
        compiler_params=pltpu.CompilerParams(vmem_limit_bytes=50 * 2**20),
        cost_estimate=pl.CostEstimate(
            flops=blocks * heads * 7 * 2 * GROUP * HD * MH * 4,
            bytes_accessed=blocks * 6 * rows * MH * 4,
            transcendentals=blocks * heads * 2 * MH * GROUP,
        ),
    )(flags, packed, packed, probes, packed, retain, update, first, second, scalars)


def memory_backward_kernel(
    heads,
    blocks,
    flags,
    keys_ref,
    values_ref,
    probes_ref,
    rates_ref,
    retain_ref,
    update_ref,
    first_ref,
    second_ref,
    scalars_ref,
    saved_ref,
    pull_ref,
    grads_ref,
    grad_first_ref,
    grad_second_ref,
    grad_scalars_ref,
    message,
):
    count = pl.program_id(0)
    turn = blocks - 1 - count

    @pl.when(count == 0)
    def blank():
        message[...] = jnp.zeros_like(message)
        grad_first_ref[...] = jnp.zeros_like(grad_first_ref)
        grad_second_ref[...] = jnp.zeros_like(grad_second_ref)
        grad_scalars_ref[...] = jnp.zeros_like(grad_scalars_ref)

    grads_ref[...] = jnp.zeros_like(grads_ref)
    size = heads * HD
    rate_row = 2 * size
    probe_row = 2 * size + RATE_ROWS

    @pl.when(count > 0)
    def step():
        carry = flags[0, turn].astype(f32)
        grad_rates = []
        for head in range(heads):
            rows = slice(head * HD, (head + 1) * HD)
            keep = scalars_ref[0, head]
            push = scalars_ref[1, head] * carry
            base_first = jnp.where(carry > 0.5, saved_ref[0, 0, rows, :], first_ref[rows, :])
            base_second = jnp.where(carry > 0.5, saved_ref[0, 1, rows, :], second_ref[rows, :])
            grad_a = message[0, rows, :]
            grad_b = message[1, rows, :]
            grad_sa = message[2, rows, :] + grad_a
            grad_sb = message[3, rows, :] + grad_b
            momentum_part = carry * (
                jnp.sum(saved_ref[0, 2, rows, :] * grad_sa, axis=0, keepdims=True)
                + jnp.sum(saved_ref[0, 3, rows, :] * grad_sb, axis=0, keepdims=True)
            )
            decay_part = -(
                jnp.sum(base_first * grad_a, axis=0, keepdims=True)
                + jnp.sum(base_second * grad_b, axis=0, keepdims=True)
            )
            grad_scalars_ref[2 * head : 2 * head + 1, :] += decay_part
            grad_scalars_ref[2 * head + 1 : 2 * head + 2, :] += momentum_part
            back_a = (-grad_sa).astype(bf16)
            back_b = (-grad_sb).astype(bf16)
            raw = keys_ref[0, rows, :].astype(f32)
            inverse = inverse_root(raw)
            normal = raw * inverse
            keys = normal.astype(bf16)
            first_low = base_first.astype(bf16)
            second_low = base_second.astype(bf16)
            inner = dot_tn(first_low, keys)
            gate = jax.nn.sigmoid(inner)
            active = inner * gate
            slope = gate + active * (1.0 - gate)
            bend = gate * (1.0 - gate) * (2.0 + inner - 2.0 * active)
            active_low = active.astype(bf16)
            weight = update_ref[0] * (1.0 / GROUP)
            rate = rates_ref[0, head : head + 1, :].astype(f32)
            error = dot_nn(second_low, active_low) - values_ref[0, rows, :].astype(f32)
            pull = (error * (rate * weight)).astype(bf16)
            spread = dot_tn(second_low, pull)
            inner_pull = (spread * slope).astype(bf16)
            back_inner = dot_tn(back_a, keys)
            back_spread = (back_inner * slope).astype(bf16)
            grad_pull = dot_nn(back_b, active_low) + dot_nn(second_low, back_spread)
            grad_rates.append(jnp.sum(grad_pull * error, axis=0, keepdims=True) * weight)
            grad_error = grad_pull * (rate * weight)
            grad_error_low = grad_error.astype(bf16)
            grads_ref[0, size + head * HD : size + (head + 1) * HD, :] = (-grad_error).astype(bf16)
            grad_active = dot_tn(back_b, pull) + dot_tn(second_low, grad_error_low)
            grad_inner = (back_inner * spread * bend + grad_active * slope).astype(bf16)
            grad_normal = dot_nn(back_a, inner_pull) + dot_nn(first_low, grad_inner)
            grads_ref[0, rows, :] = (
                inverse
                * (grad_normal - normal * jnp.mean(grad_normal * normal, axis=0, keepdims=True))
            ).astype(bf16)
            base_grad_a = keep * grad_a + dot_nt(keys, grad_inner)
            base_grad_b = (
                keep * grad_b + dot_nt(pull, back_spread) + dot_nt(grad_error_low, active_low)
            )
            message[0, rows, :] = carry * base_grad_a
            message[1, rows, :] = carry * base_grad_b
            message[2, rows, :] = push * grad_sa
            message[3, rows, :] = push * grad_sb
            grad_first_ref[rows, :] += (1.0 - carry) * base_grad_a
            grad_second_ref[rows, :] += (1.0 - carry) * base_grad_b
        grad_rates.append(jnp.zeros((RATE_ROWS - heads, GROUP), f32))
        grads_ref[0, rate_row : rate_row + RATE_ROWS, :] = jnp.concatenate(
            grad_rates, axis=0
        ).astype(bf16)

    retain = retain_ref[0]

    def recall_back(first, second, grad_recalled, head):
        rows = slice(head * HD, (head + 1) * HD)
        raw = probes_ref[0, rows, :].astype(f32)
        inverse = inverse_root(raw)
        normal = raw * inverse
        probes = normal.astype(bf16)
        first_low = first[rows, :].astype(bf16)
        inner = dot_tn(first_low, probes)
        gate = jax.nn.sigmoid(inner)
        active = inner * gate
        slope = gate + active * (1.0 - gate)
        grad_inner = (dot_tn(second[rows, :].astype(bf16), grad_recalled) * slope).astype(bf16)
        grad_second = dot_nt(grad_recalled, active.astype(bf16))
        grad_first = dot_nt(probes, grad_inner)
        grad_normal = dot_nn(first_low, grad_inner)
        grad_probes = inverse * (
            grad_normal - normal * jnp.mean(grad_normal * normal, axis=0, keepdims=True)
        )
        return grad_first, grad_second, grad_probes

    only_state = flags[1, turn] * (1 - flags[2, turn])
    only_init = flags[2, turn] * (1 - flags[1, turn])

    def from_state(whole, add):
        for head in range(heads):
            rows = slice(head * HD, (head + 1) * HD)
            grad_recalled = pull_ref[0, rows, :]
            if not whole:
                grad_recalled = (grad_recalled.astype(f32) * retain).astype(bf16)
            grad_first, grad_second, grad_probes = recall_back(
                saved_ref[0, 0], saved_ref[0, 1], grad_recalled, head
            )
            message[0, rows, :] += grad_first
            message[1, rows, :] += grad_second
            spot = slice(probe_row + head * HD, probe_row + (head + 1) * HD)
            grads_ref[0, spot, :] = grad_probes.astype(bf16)

    def from_init(whole, add):
        for head in range(heads):
            rows = slice(head * HD, (head + 1) * HD)
            grad_recalled = pull_ref[0, rows, :]
            if not whole:
                grad_recalled = (grad_recalled.astype(f32) * (1.0 - retain)).astype(bf16)
            grad_first, grad_second, grad_probes = recall_back(
                first_ref[...], second_ref[...], grad_recalled, head
            )
            grad_first_ref[rows, :] += grad_first
            grad_second_ref[rows, :] += grad_second
            spot = slice(probe_row + head * HD, probe_row + (head + 1) * HD)
            if add:
                grad_probes = grad_probes + grads_ref[0, spot, :].astype(f32)
            grads_ref[0, spot, :] = grad_probes.astype(bf16)

    @pl.when(only_state == 1)
    def state_alone():
        from_state(True, False)

    @pl.when(only_init == 1)
    def init_alone():
        from_init(True, False)

    @pl.when(only_state + only_init == 0)
    def both():
        from_state(False, False)
        from_init(False, True)


def memory_backward(
    flags, packed, probes, retain, update, first, second, scalars, saved, pull
):
    chips, rows, width = probes.shape
    heads = rows // HD
    blocks = chips * width // GROUP
    per = width // GROUP
    all_rows = 3 * rows + RATE_ROWS

    def block(count, flags):
        turn = blocks - 1 - count
        return (turn // per, 0, (turn % per) ^ flags[3, 0])

    def by_turn(count, flags):
        return (blocks - 1 - count, 0, 0)

    def whole(count, flags):
        return (0, 0)

    def value_block(count, flags):
        turn = blocks - 1 - count
        return (turn // per, 1, (turn % per) ^ flags[3, 0])

    def rate_block(count, flags):
        turn = blocks - 1 - count
        return (turn // per, 2 * rows // RATE_ROWS, (turn % per) ^ flags[3, 0])

    part = pl.BlockSpec((1, rows, GROUP), block)
    line = pl.BlockSpec((1, 1, GROUP), by_turn)
    matrix = pl.BlockSpec((rows, MH), whole)
    return pl.pallas_call(
        lambda *refs: memory_backward_kernel(heads, blocks, *refs),
        grid_spec=pltpu.PrefetchScalarGridSpec(
            num_scalar_prefetch=1,
            grid=(blocks,),
            in_specs=[
                part,
                pl.BlockSpec((1, rows, GROUP), value_block),
                part,
                pl.BlockSpec((1, RATE_ROWS, GROUP), rate_block),
                line,
                line,
                matrix,
                matrix,
                pl.BlockSpec(memory_space=pltpu.SMEM),
                pl.BlockSpec(
                    (1, 4, rows, MH), lambda count, flags: (blocks - 1 - count, 0, 0, 0)
                ),
                part,
            ],
            out_specs=[
                pl.BlockSpec((1, all_rows, GROUP), block),
                matrix,
                matrix,
                pl.BlockSpec((8, MH), whole),
            ],
            scratch_shapes=[pltpu.VMEM((4, rows, MH), f32)],
        ),
        out_shape=[
            jax.ShapeDtypeStruct((chips, all_rows, width), bf16),
            jax.ShapeDtypeStruct((rows, MH), f32),
            jax.ShapeDtypeStruct((rows, MH), f32),
            jax.ShapeDtypeStruct((8, MH), f32),
        ],
        compiler_params=pltpu.CompilerParams(vmem_limit_bytes=56 * 2**20),
        cost_estimate=pl.CostEstimate(
            flops=blocks * heads * 19 * 2 * GROUP * HD * MH * 4,
            bytes_accessed=blocks * 8 * rows * MH * 4,
            transcendentals=blocks * heads * 2 * MH * GROUP,
        ),
    )(flags, packed, packed, probes, packed, retain, update, first, second, scalars, saved, pull)


QUERIES = 256


def visible_bias(bias_ref, row_ref, col_ref):
    shape = bias_ref.shape[1:]
    key = lax.broadcasted_iota(jnp.int32, shape, 0)
    query = lax.broadcasted_iota(jnp.int32, shape, 1)
    for block in range(bias_ref.shape[0]):
        seen = jnp.logical_and(key <= query, col_ref[block] == row_ref[block])
        bias_ref[block] = jnp.where(seen, 0.0, -1e30)


def attention_forward_kernel(
    scale,
    q_ref,
    k_ref,
    v_ref,
    kr_ref,
    vr_ref,
    kp_ref,
    vp_ref,
    row_ref,
    col_ref,
    mixed_ref,
    total_ref,
    bias_ref,
):
    @pl.when(jnp.logical_and(pl.program_id(0) == 0, pl.program_id(1) == 0))
    def fill():
        visible_bias(bias_ref, row_ref, col_ref)

    block = pl.program_id(1)
    for part in range(GROUP // QUERIES):
        lanes = slice(part * QUERIES, (part + 1) * QUERIES)
        upto = (part + 1) * QUERIES
        query = q_ref[:, lanes]
        bias = bias_ref[block, :upto, lanes]
        s_p = dot_tn(kp_ref[...], query) * scale
        s_r = dot_tn(kr_ref[:, :upto], query) * scale + bias
        s_l = dot_tn(k_ref[:, :upto], query) * scale + bias
        top = jnp.maximum(
            jnp.max(s_p, axis=0, keepdims=True),
            jnp.maximum(
                jnp.max(s_r, axis=0, keepdims=True), jnp.max(s_l, axis=0, keepdims=True)
            ),
        )
        e_p = jnp.exp(s_p - top)
        e_r = jnp.exp(s_r - top)
        e_l = jnp.exp(s_l - top)
        total = (
            jnp.sum(e_p, axis=0, keepdims=True)
            + jnp.sum(e_r, axis=0, keepdims=True)
            + jnp.sum(e_l, axis=0, keepdims=True)
        )
        mixed = (
            dot_nn(vp_ref[...], e_p.astype(bf16))
            + dot_nn(vr_ref[:, :upto], e_r.astype(bf16))
            + dot_nn(v_ref[:, :upto], e_l.astype(bf16))
        )
        mixed_ref[:, lanes] = (mixed / total).astype(bf16)
        total_ref[0, :, lanes] = top + jnp.log(total)


def attention_specs(width):
    main = pl.BlockSpec((HD, GROUP), lambda head, block: (head, block))
    side = pl.BlockSpec((HD, NP), lambda head, block: (head, 0))
    count = width // GROUP
    row = pl.BlockSpec((count, 1, GROUP), lambda head, block: (0, 0, 0))
    col = pl.BlockSpec((count, GROUP, 1), lambda head, block: (0, 0, 0))
    line = pl.BlockSpec((1, 1, GROUP), lambda head, block: (head, 0, block))
    return main, side, row, col, line


def attention_forward(scale, q, k, v, kr, vr, kp, vp, row, col):
    rows, width = q.shape
    main, side, row_spec, col_spec, line = attention_specs(width)
    heads, count = rows // HD, width // GROUP
    return pl.pallas_call(
        lambda *refs: attention_forward_kernel(scale, *refs),
        grid=(heads, count),
        in_specs=[main, main, main, main, main, side, side, row_spec, col_spec],
        out_specs=[main, line],
        out_shape=[
            jax.ShapeDtypeStruct((rows, width), bf16),
            jax.ShapeDtypeStruct((heads, 1, width), f32),
        ],
        scratch_shapes=[pltpu.VMEM((count, GROUP, GROUP), f32)],
        compiler_params=pltpu.CompilerParams(vmem_limit_bytes=50 * 2**20),
        cost_estimate=pl.CostEstimate(
            flops=heads * count * 4 * GROUP * 1088 * HD * 4,
            bytes_accessed=6 * rows * width * 2,
            transcendentals=heads * count * GROUP * 1088,
        ),
    )(q, k, v, kr, vr, kp, vp, row, col)


def attention_backward_kernel(
    scale,
    q_ref,
    k_ref,
    v_ref,
    kr_ref,
    vr_ref,
    kp_ref,
    vp_ref,
    row_ref,
    col_ref,
    mixed_ref,
    total_ref,
    grad_ref,
    gq_ref,
    gk_ref,
    gv_ref,
    gkr_ref,
    gvr_ref,
    gkp_ref,
    gvp_ref,
    bias_ref,
):
    @pl.when(jnp.logical_and(pl.program_id(0) == 0, pl.program_id(1) == 0))
    def fill():
        visible_bias(bias_ref, row_ref, col_ref)

    block = pl.program_id(1)

    @pl.when(block == 0)
    def blank():
        gkp_ref[...] = jnp.zeros_like(gkp_ref)
        gvp_ref[...] = jnp.zeros_like(gvp_ref)

    parts = GROUP // QUERIES
    sums = {}
    for part in reversed(range(parts)):
        lanes = slice(part * QUERIES, (part + 1) * QUERIES)
        upto = (part + 1) * QUERIES
        query = q_ref[:, lanes]
        grad = grad_ref[:, lanes]
        bias = bias_ref[block, :upto, lanes] - total_ref[0, :, lanes]
        mean = jnp.sum(
            grad.astype(f32) * mixed_ref[:, lanes].astype(f32), axis=0, keepdims=True
        )
        grad_query = jnp.zeros((HD, QUERIES), f32)
        for name, keys, values, extra in (
            ("p", kp_ref[...], vp_ref[...], -total_ref[0, :, lanes]),
            ("r", kr_ref[:, :upto], vr_ref[:, :upto], bias),
            ("l", k_ref[:, :upto], v_ref[:, :upto], bias),
        ):
            chances = jnp.exp(dot_tn(keys, query) * scale + extra)
            slope = (chances * (dot_tn(values, grad) - mean)).astype(bf16)
            grad_query += dot_nn(keys, slope)
            grad_keys = dot_nt(query, slope)
            grad_values = dot_nt(grad, chances.astype(bf16))
            if name in sums:
                old_keys, old_values = sums[name]
                if name == "p":
                    sums[name] = (old_keys + grad_keys, old_values + grad_values)
                else:
                    sums[name] = (
                        jnp.concatenate([old_keys[:, :upto] + grad_keys, old_keys[:, upto:]], axis=1),
                        jnp.concatenate(
                            [old_values[:, :upto] + grad_values, old_values[:, upto:]], axis=1
                        ),
                    )
            else:
                sums[name] = (grad_keys, grad_values)
        gq_ref[:, lanes] = grad_query * scale
    gkp_ref[...] += sums["p"][0] * scale
    gvp_ref[...] += sums["p"][1]
    gkr_ref[...] = (sums["r"][0] * scale).astype(bf16)
    gvr_ref[...] = sums["r"][1].astype(bf16)
    gk_ref[...] = sums["l"][0] * scale
    gv_ref[...] = sums["l"][1]


def attention_backward(scale, q, k, v, kr, vr, kp, vp, row, col, mixed, total, grad):
    rows, width = q.shape
    main, side, row_spec, col_spec, line = attention_specs(width)
    heads, count = rows // HD, width // GROUP
    wide = jax.ShapeDtypeStruct((rows, width), f32)
    low = jax.ShapeDtypeStruct((rows, width), bf16)
    return pl.pallas_call(
        lambda *refs: attention_backward_kernel(scale, *refs),
        grid=(heads, count),
        in_specs=[main, main, main, main, main, side, side, row_spec, col_spec, main, line, main],
        out_specs=[main, main, main, main, main, side, side],
        out_shape=[
            wide,
            wide,
            wide,
            low,
            low,
            jax.ShapeDtypeStruct((rows, NP), f32),
            jax.ShapeDtypeStruct((rows, NP), f32),
        ],
        scratch_shapes=[pltpu.VMEM((count, GROUP, GROUP), f32)],
        compiler_params=pltpu.CompilerParams(vmem_limit_bytes=50 * 2**20),
        cost_estimate=pl.CostEstimate(
            flops=heads * count * 10 * GROUP * 1088 * HD * 4,
            bytes_accessed=14 * rows * width * 2,
            transcendentals=heads * count * GROUP * 1088,
        ),
    )(q, k, v, kr, vr, kp, vp, row, col, mixed, total, grad)


rate_numerator = 2.0


def matmul(left, right, left_dim, right_dim, out=f32):
    return lax.dot_general(
        left, right, (((left_dim,), (right_dim,)), ((), ())), preferred_element_type=f32
    ).astype(out)


def core_swap(value):
    return lax.ppermute(value, "core", [(0, 1), (1, 0)])


def gather_chips(value):
    return lax.all_gather(value, ("dp", "chip"), axis=0, tiled=True)


def scatter_chips(value):
    return lax.psum_scatter(value, ("dp", "chip"), scatter_dimension=0, tiled=True)


def by_core(core, mine, other, axis=0):
    return jnp.where(
        core == 0,
        jnp.concatenate([mine, other], axis=axis),
        jnp.concatenate([other, mine], axis=axis),
    )


def inverse_rms(values):
    return lax.rsqrt(jnp.mean(values * values, axis=-1, keepdims=True) + norm_epsilon)


def norm_back(grad_normed, values, inverse, gain):
    normal = values * inverse
    scaled = grad_normed * gain
    grad_gain = jnp.sum(grad_normed * normal, axis=0)
    grad_values = inverse * (scaled - normal * jnp.mean(scaled * normal, axis=-1, keepdims=True))
    return (grad_values, grad_gain)


def on_device(
    inputs,
    segments,
    attn_gain,
    query_weight,
    key_weight,
    value_weight,
    output_weight,
    persistent,
    memory_first,
    memory_second,
    rate_weight,
    decay_logit,
    momentum_logit,
    ffn_gain,
    gate_weight,
    up_weight,
    down_weight,
    cotangent,
):
    groups, chips, core_count = (lax.axis_size("dp"), lax.axis_size("chip"), 2)
    core = lax.axis_index("core")
    chip = lax.axis_index("chip")
    position = chip * core_count + core
    chain = chips * core_count
    devices = groups * chain
    scale = HD ** (-0.5)
    rate_scale = rate_numerator / MH
    half = D // 2
    core_heads = H // core_count
    heads = core_heads // chips
    rows = heads * HD
    width = 2 * GROUP
    shard = query_weight.shape[0]
    ff_shard = down_weight.shape[0]
    ff_half = gate_weight.shape[1] // 2

    def columns_of(which):
        def cut(weight):
            return lax.dynamic_slice_in_dim(weight, which * (weight.shape[1] // 2), weight.shape[1] // 2, 1)

        rate = cut(rate_weight)
        tail = jnp.concatenate([rate, persistent, attn_gain[:, None]], axis=1)
        tail = jnp.pad(tail, ((0, 0), (0, 128 - tail.shape[1])))
        return jnp.concatenate([cut(key_weight), cut(value_weight), cut(query_weight), tail], axis=1)

    w_one = gather_chips(by_core(core, columns_of(core), core_swap(columns_of(1 - core))))

    tokens = inputs[0]
    tokens_other = core_swap(tokens)
    grad_out = cotangent[0]
    grad_out_pair = jnp.concatenate([grad_out, core_swap(grad_out)], axis=0)

    mem_all = lax.all_gather(
        jnp.concatenate([memory_first, memory_second], axis=1),
        ("dp", "chip", "core"),
        axis=0,
        tiled=True,
    )
    mem_mine = lax.dynamic_slice_in_dim(mem_all, core * half + chip * rows, rows, 0).astype(f32)
    first_init, second_init = mem_mine[:, :MH], mem_mine[:, MH:]

    out_order = [(s, 2 * (s % (devices // 2)) + s // (devices // 2)) for s in range(devices)]
    w_output = gather_chips(lax.ppermute(output_weight, ("dp", "chip", "core"), out_order))

    def ff_columns(which):
        def cut(weight):
            parts = weight.reshape(shard, devices // 2, 2, ff_shard)
            return lax.dynamic_index_in_dim(parts, which, 2, keepdims=False).reshape(shard, ff_half)

        return jnp.concatenate([cut(gate_weight), cut(up_weight)], axis=1)

    w_gate_up = gather_chips(by_core(core, ff_columns(core), core_swap(ff_columns(1 - core))))
    w_down = gather_chips(down_weight)
    gain_two = lax.all_gather(ffn_gain, ("dp", "chip", "core"), axis=0, tiled=True).astype(f32)

    ids = segments[0].reshape(chain, GROUP)
    first_id, last_id = ids[:, 0], ids[:, GROUP - 1]
    before = jnp.concatenate([first_id[:1], ids[:-1, GROUP - 1]])
    joined = jnp.logical_and(jnp.arange(chain) > 0, first_id == before)
    carry = jnp.logical_and(joined, first_id == last_id)
    kept = jnp.logical_and(joined[:, None], ids == first_id[:, None])
    retain = kept.astype(f32)[:, None, :]
    update = (ids == last_id[:, None]).astype(f32)[:, None, :]
    flags = jnp.stack(
        [
            carry.astype(jnp.int32),
            jnp.any(kept, axis=1).astype(jnp.int32),
            jnp.logical_not(jnp.all(kept, axis=1)).astype(jnp.int32),
            jnp.full((chain,), core, jnp.int32),
        ]
    )
    pair_ids = jnp.stack(
        [
            lax.dynamic_index_in_dim(ids, position, keepdims=False),
            lax.dynamic_index_in_dim(ids, chip * core_count + 1 - core, keepdims=False),
        ]
    )
    id_row, id_col = pair_ids[:, None, :], pair_ids[:, :, None]
    decay = jax.nn.sigmoid(decay_logit)
    momentum = jax.nn.sigmoid(momentum_logit)
    head_at = core * core_heads + chip * heads
    scalars = jnp.stack(
        [
            lax.dynamic_slice_in_dim(1.0 - decay, head_at, heads),
            lax.dynamic_slice_in_dim(momentum, head_at, heads),
        ]
    )

    gain_at = 3 * half + core_heads + NP
    gain_one = w_one[:, gain_at].astype(f32)
    tokens_pair = jnp.concatenate([tokens, tokens_other], axis=0).astype(f32)
    inverse_one = inverse_rms(tokens_pair)
    normed = (tokens_pair * inverse_one * gain_one).astype(bf16)
    low = matmul(w_one[:, : 3 * half], normed, 0, 1, bf16)
    keys, values, query = low[:half], low[half : 2 * half], low[2 * half :]
    rate_sigmoid = jax.nn.sigmoid(matmul(w_one[:, 3 * half :], normed, 0, 1)[:core_heads])
    rates = (rate_scale * rate_sigmoid).astype(bf16).reshape(chips, heads, width)
    packed = jnp.concatenate(
        [
            keys.reshape(chips, rows, width),
            values.reshape(chips, rows, width),
            jnp.pad(rates, ((0, 0), (0, RATE_ROWS - heads), (0, 0))),
        ],
        axis=1,
    )
    packed = lax.all_to_all(packed, "chip", 0, 0, tiled=True)
    probes = lax.all_to_all(query.reshape(chips, rows, width), "chip", 0, 0, tiled=True)
    recalled, saved = memory_forward(
        flags, packed, probes, retain, update, first_init, second_init, scalars
    )
    recalled = lax.all_to_all(recalled, "chip", 0, 0, tiled=True).reshape(half, width)

    def flip(value):
        return jnp.concatenate([value[:, GROUP:], value[:, :GROUP]], axis=1)

    recalled_other = core_swap(flip(recalled))
    persist = w_one[:, gain_at - NP : gain_at]
    context = jnp.concatenate([by_core(core, recalled, recalled_other), persist], axis=1)
    low_context = matmul(w_one[:, : 2 * half], context, 0, 0, bf16)
    keys_r, values_r = low_context[:half, :width], low_context[half:, :width]
    keys_p, values_p = low_context[:half, width:], low_context[half:, width:]
    mixed, total = attention_forward(
        scale, query, keys, values, keys_r, values_r, keys_p, values_p, id_row, id_col
    )

    def pair_sum(partial):
        return partial[:GROUP] + core_swap(partial[GROUP:].astype(bf16)).astype(f32)

    def pair_rows(own):
        return jnp.concatenate([own, core_swap(own)], axis=0)

    middle = tokens.astype(f32) + pair_sum(matmul(mixed, w_output, 0, 0))
    inverse_two = inverse_rms(middle)
    normed_two = pair_rows((middle * inverse_two * gain_two).astype(bf16))
    gate = matmul(normed_two, w_gate_up[:, :ff_half], 1, 0)
    up = matmul(normed_two, w_gate_up[:, ff_half:], 1, 0)
    gate_sigmoid = jax.nn.sigmoid(gate)
    gate_silu = gate * gate_sigmoid
    hidden = (gate_silu * up).astype(bf16)
    result = (middle + pair_sum(matmul(hidden, w_down, 1, 0))).astype(bf16)

    grad_down_w = matmul(hidden, grad_out_pair, 0, 0, bf16)
    grad_hidden = matmul(grad_out_pair, w_down, 1, 1)
    grad_gate = (grad_hidden * up * gate_sigmoid * (1.0 + gate * (1.0 - gate_sigmoid))).astype(bf16)
    grad_up = (grad_hidden * gate_silu).astype(bf16)
    grad_gate_up = jnp.concatenate([grad_gate, grad_up], axis=1)
    grad_gate_up_w = matmul(normed_two, grad_gate_up, 0, 0, bf16)
    grad_normed_two = pair_sum(matmul(grad_gate_up, w_gate_up, 1, 1))
    grad_middle_norm, grad_gain_two = norm_back(grad_normed_two, middle, inverse_two, gain_two)
    grad_middle = grad_out.astype(f32) + grad_middle_norm
    down_part = scatter_chips(grad_down_w).astype(f32)
    gate_up_part = scatter_chips(grad_gate_up_w)

    grad_attended = pair_rows(grad_middle.astype(bf16))
    grad_output_w = matmul(mixed, grad_attended, 1, 0, bf16)
    output_part = scatter_chips(grad_output_w)
    grad_mixed = matmul(w_output, grad_attended, 1, 1, bf16)
    (
        grad_query_att,
        grad_keys_att,
        grad_values_att,
        grad_keys_r,
        grad_values_r,
        grad_keys_p,
        grad_values_p,
    ) = attention_backward(
        scale,
        query,
        keys,
        values,
        keys_r,
        values_r,
        keys_p,
        values_p,
        id_row,
        id_col,
        mixed,
        total,
        grad_mixed,
    )
    grad_low_context = jnp.concatenate(
        [
            jnp.concatenate([grad_keys_r, grad_keys_p.astype(bf16)], axis=1),
            jnp.concatenate([grad_values_r, grad_values_p.astype(bf16)], axis=1),
        ],
        axis=0,
    )
    grad_context = matmul(w_one[:, : 2 * half], grad_low_context, 1, 0)
    grad_persist = grad_context[:, width:]
    pull = (
        lax.dynamic_slice_in_dim(grad_context, core * half, half, 0)[:, :width]
        + core_swap(
            flip(
                lax.dynamic_slice_in_dim(grad_context, (1 - core) * half, half, 0)[:, :width]
            ).astype(bf16)
        ).astype(f32)
    ).astype(bf16)
    pull = lax.all_to_all(pull.reshape(chips, rows, width), "chip", 0, 0, tiled=True)
    grad_context_w = matmul(context, grad_low_context, 1, 1)
    grads, grad_first, grad_second, grad_scalars = memory_backward(
        flags, packed, probes, retain, update, first_init, second_init, scalars, saved, pull
    )
    grads = lax.all_to_all(grads, "chip", 0, 0, tiled=True)
    cuts = (rows, 2 * rows, 2 * rows + RATE_ROWS)
    grad_keys = grad_keys_att + grads[:, : cuts[0]].reshape(half, width).astype(f32)
    grad_values = grad_values_att + grads[:, cuts[0] : cuts[1]].reshape(half, width).astype(f32)
    grad_query = grad_query_att + grads[:, cuts[2] :].reshape(half, width).astype(f32)
    grad_rates = grads[:, cuts[1] : cuts[1] + heads].reshape(core_heads, width).astype(f32)
    grad_rate_logits = grad_rates * rate_scale * rate_sigmoid * (1.0 - rate_sigmoid)
    grad_low = jnp.concatenate(
        [
            grad_keys.astype(bf16),
            grad_values.astype(bf16),
            grad_query.astype(bf16),
            jnp.pad(grad_rate_logits.astype(bf16), ((0, 128 - core_heads), (0, 0))),
        ],
        axis=0,
    )
    grad_one_w = matmul(normed, grad_low, 0, 1)
    grad_normed = matmul(grad_low, w_one, 0, 1)
    grad_normed_own = pair_sum(grad_normed)
    grad_tokens_one, grad_gain_one = norm_back(
        grad_normed_own, tokens.astype(f32), inverse_one[:GROUP], gain_one
    )
    grad_inputs = (grad_middle + grad_tokens_one).astype(bf16)
    one_part = scatter_chips(
        jnp.concatenate(
            [
                grad_one_w[:, : 2 * half] + grad_context_w,
                grad_one_w[:, 2 * half : 3 * half],
                grad_one_w[:, 3 * half : 3 * half + core_heads],
                grad_persist,
                jnp.zeros((D, 128 - core_heads - NP), f32),
            ],
            axis=1,
        ).astype(bf16)
    )
    zeros = jnp.zeros((D, 2 * MH), bf16)
    mem_part = lax.psum_scatter(
        lax.dynamic_update_slice_in_dim(
            zeros,
            jnp.concatenate([grad_first, grad_second], axis=1).astype(bf16),
            core * half + chip * rows,
            0,
        ),
        ("dp", "chip", "core"),
        scatter_dimension=0,
        tiled=True,
    ).astype(f32)
    scalar_sums = jnp.sum(grad_scalars, axis=1)[: 2 * heads].reshape(heads, 2)
    spots = jnp.zeros((2, H), f32)
    spots = lax.dynamic_update_slice(spots, scalar_sums.T, (0, head_at))
    sums = lax.psum(
        jnp.concatenate([grad_gain_one, grad_gain_two, spots.reshape(-1)]), ("dp", "chip", "core")
    )
    index = (lax.axis_index("dp") * chips + chip) * core_count + core
    gain_one_part = lax.dynamic_slice_in_dim(sums, index * shard, shard)
    gain_two_part = lax.dynamic_slice_in_dim(sums, D + index * shard, shard)
    grad_decay = sums[2 * D : 2 * D + H] * decay * (1.0 - decay)
    grad_momentum = sums[2 * D + H :] * momentum * (1.0 - momentum)

    def own_rows(part):
        mine = lax.dynamic_slice_in_dim(part, core * shard, shard, 0)
        other = core_swap(lax.dynamic_slice_in_dim(part, (1 - core) * shard, shard, 0))
        return mine, other

    mine, other = own_rows(one_part)
    mine, other = mine.astype(f32), other.astype(f32)

    def whole_columns(start, size):
        return by_core(core, mine[:, start : start + size], other[:, start : start + size], 1)

    rate_at = 3 * half
    persist_part = (mine + other)[:, rate_at + core_heads : rate_at + core_heads + NP]

    def ff_rows(mine, other):
        pair = jnp.stack([mine, other]).reshape(2, shard, devices // 2, ff_shard).astype(f32)
        pair = jnp.where(core == 0, pair, pair[::-1])
        return pair.transpose(1, 2, 0, 3).reshape(shard, 2 * ff_half)

    mine_ff, other_ff = own_rows(gate_up_part)
    gate_part = ff_rows(mine_ff[:, :ff_half], other_ff[:, :ff_half])
    up_part = ff_rows(mine_ff[:, ff_half:], other_ff[:, ff_half:])
    output_own = lax.ppermute(
        output_part, ("dp", "chip", "core"), [(d, s) for s, d in out_order]
    ).astype(f32)
    return (
        result[None],
        grad_inputs[None],
        gain_one_part,
        whole_columns(2 * half, half),
        whole_columns(0, half),
        whole_columns(half, half),
        output_own,
        persist_part,
        mem_part[:, :MH],
        mem_part[:, MH:],
        whole_columns(rate_at, core_heads),
        grad_decay,
        grad_momentum,
        gain_two_part,
        gate_part,
        up_part,
        down_part,
    )


def solution(mesh):
    split = jax.sharding.Mesh(
        mesh.devices.reshape(mesh.shape["dp"], mesh.shape["seq"] // 2, 2), ("dp", "chip", "core")
    )
    row = P("dp", ("chip", "core"), None)
    vector = P(("dp", "chip", "core"))
    matrix = P(("dp", "chip", "core"), None)
    in_specs = (
        row,
        P("dp", None),
        vector,
        matrix,
        matrix,
        matrix,
        matrix,
        matrix,
        matrix,
        matrix,
        matrix,
        P(),
        P(),
        vector,
        matrix,
        matrix,
        matrix,
        row,
    )
    out_specs = (
        row,
        row,
        vector,
        matrix,
        matrix,
        matrix,
        matrix,
        matrix,
        matrix,
        matrix,
        matrix,
        P(),
        P(),
        vector,
        matrix,
        matrix,
        matrix,
    )
    return jax.shard_map(
        on_device, mesh=split, in_specs=in_specs, out_specs=out_specs, check_vma=False
    )
```

```python
import jax
import jax.numpy as jnp
from jax import lax
from jax.experimental import pallas as pl
from jax.experimental.pallas import tpu as pltpu
from jax.sharding import PartitionSpec as P

D = 1536
H = 16
HD = 96
MH = 384
NP = 64
GROUP = 512
RATE_ROWS = 16
RATE_SCALE = 2.0 / 384
norm_epsilon = 1e-06
f32 = jnp.float32
bf16 = jnp.bfloat16


def dot_nn(left, right):
    return lax.dot_general(left, right, (((1,), (0,)), ((), ())), preferred_element_type=f32)


def dot_tn(left, right):
    return lax.dot_general(left, right, (((0,), (0,)), ((), ())), preferred_element_type=f32)


def dot_nt(left, right):
    return lax.dot_general(left, right, (((1,), (1,)), ((), ())), preferred_element_type=f32)


def inverse_root(values):
    return lax.rsqrt(jnp.mean(values * values, axis=0, keepdims=True) + norm_epsilon)


def spot(heads, head, which):
    at = 2 * head + which if which < 2 else 2 * heads + head
    return slice(at * HD, (at + 1) * HD)


def memory_forward_kernel(
    heads,
    blocks,
    flags,
    main_ref,
    retain_ref,
    update_ref,
    first_ref,
    second_ref,
    scalars_ref,
    recalled_ref,
    saved_ref,
    state,
):
    turn = pl.program_id(0)

    @pl.when(turn == 0)
    def blank():
        state[...] = jnp.zeros_like(state)

    saved_ref[0] = state[...]
    retain = retain_ref[0]

    def recall_with(first, second, head):
        rows = slice(head * HD, (head + 1) * HD)
        raw = main_ref[spot(heads, head, 2), :].astype(f32)
        probes = (raw * inverse_root(raw)).astype(bf16)
        inner = dot_tn(first[rows, :].astype(bf16), probes)
        return dot_nn(second[rows, :].astype(bf16), jax.nn.silu(inner).astype(bf16))

    only_state = flags[1, turn] * (1 - flags[2, turn])
    only_init = flags[2, turn] * (1 - flags[1, turn])

    @pl.when(only_state == 1)
    def from_state():
        for head in range(heads):
            recalled_ref[0, head * HD : (head + 1) * HD, :] = recall_with(
                state[0], state[1], head
            ).astype(bf16)

    @pl.when(only_init == 1)
    def from_init():
        for head in range(heads):
            recalled_ref[0, head * HD : (head + 1) * HD, :] = recall_with(
                first_ref[...], second_ref[...], head
            ).astype(bf16)

    @pl.when(only_state + only_init == 0)
    def from_both():
        for head in range(heads):
            recalled_ref[0, head * HD : (head + 1) * HD, :] = (
                retain * recall_with(state[0], state[1], head)
                + (1.0 - retain) * recall_with(first_ref[...], second_ref[...], head)
            ).astype(bf16)

    @pl.when(turn < blocks - 1)
    def step():
        carry = flags[0, turn].astype(f32)
        for head in range(heads):
            rows = slice(head * HD, (head + 1) * HD)
            keep = scalars_ref[0, head]
            push = scalars_ref[1, head] * carry
            base_first = jnp.where(carry > 0.5, state[0, rows, :], first_ref[rows, :])
            base_second = jnp.where(carry > 0.5, state[1, rows, :], second_ref[rows, :])
            raw = main_ref[spot(heads, head, 0), :].astype(f32)
            keys = (raw * inverse_root(raw)).astype(bf16)
            second_low = base_second.astype(bf16)
            inner = dot_tn(base_first.astype(bf16), keys)
            gate = jax.nn.sigmoid(inner)
            active = inner * gate
            slope = gate + active * (1.0 - gate)
            active_low = active.astype(bf16)
            at = 3 * heads * HD + head
            rate = RATE_SCALE * jax.nn.sigmoid(main_ref[at : at + 1, :].astype(f32))
            weight = rate * update_ref[0] * (1.0 / GROUP)
            error = dot_nn(second_low, active_low) - main_ref[spot(heads, head, 1), :].astype(f32)
            pull = (error * weight).astype(bf16)
            inner_pull = (dot_tn(second_low, pull) * slope).astype(bf16)
            speed_first = push * state[2, rows, :] - dot_nt(keys, inner_pull)
            speed_second = push * state[3, rows, :] - dot_nt(pull, active_low)
            state[0, rows, :] = keep * base_first + speed_first
            state[1, rows, :] = keep * base_second + speed_second
            state[2, rows, :] = speed_first
            state[3, rows, :] = speed_second


def memory_forward(flags, main, retain, update, first, second, scalars, chips):
    rows = (main.shape[0] - RATE_ROWS) // 3
    heads = rows // HD
    width = main.shape[1] // chips
    blocks = main.shape[1] // GROUP
    per = width // GROUP

    def block(turn, flags):
        return (0, ((turn // per) ^ flags[4, 0]) * per + ((turn % per) ^ flags[3, 0]))

    def by_chip(turn, flags):
        return (turn // per, 0, turn % per)

    def by_turn(turn, flags):
        return (turn, 0, 0)

    def whole(turn, flags):
        return (0, 0)

    line = pl.BlockSpec((1, 1, GROUP), by_turn)
    return pl.pallas_call(
        lambda *refs: memory_forward_kernel(heads, blocks, *refs),
        grid_spec=pltpu.PrefetchScalarGridSpec(
            num_scalar_prefetch=1,
            grid=(blocks,),
            in_specs=[
                pl.BlockSpec((3 * rows + RATE_ROWS, GROUP), block),
                line,
                line,
                pl.BlockSpec((rows, MH), whole),
                pl.BlockSpec((rows, MH), whole),
                pl.BlockSpec(memory_space=pltpu.SMEM),
            ],
            out_specs=[
                pl.BlockSpec((1, rows, GROUP), by_chip),
                pl.BlockSpec((1, 4, rows, MH), lambda turn, flags: (turn, 0, 0, 0)),
            ],
            scratch_shapes=[pltpu.VMEM((4, rows, MH), f32)],
        ),
        out_shape=[
            jax.ShapeDtypeStruct((chips, rows, width), bf16),
            jax.ShapeDtypeStruct((blocks, 4, rows, MH), f32),
        ],
        compiler_params=pltpu.CompilerParams(vmem_limit_bytes=50 * 2**20),
        cost_estimate=pl.CostEstimate(
            flops=blocks * heads * 7 * 2 * GROUP * HD * MH * 4,
            bytes_accessed=blocks * 6 * rows * MH * 4,
            transcendentals=blocks * heads * 2 * MH * GROUP,
        ),
    )(flags, main, retain, update, first, second, scalars)


def memory_backward_kernel(
    heads,
    blocks,
    flags,
    main_ref,
    retain_ref,
    update_ref,
    first_ref,
    second_ref,
    scalars_ref,
    saved_ref,
    pull_ref,
    grads_ref,
    grad_first_ref,
    grad_second_ref,
    grad_scalars_ref,
    message,
):
    count = pl.program_id(0)
    turn = blocks - 1 - count

    @pl.when(count == 0)
    def blank():
        message[...] = jnp.zeros_like(message)
        grad_first_ref[...] = jnp.zeros_like(grad_first_ref)
        grad_second_ref[...] = jnp.zeros_like(grad_second_ref)
        grad_scalars_ref[...] = jnp.zeros_like(grad_scalars_ref)

    rate_row = 3 * heads * HD

    @pl.when(count == 0)
    def last():
        for head in range(heads):
            grads_ref[spot(heads, head, 0), :] = jnp.zeros((HD, GROUP), bf16)
            grads_ref[spot(heads, head, 1), :] = jnp.zeros((HD, GROUP), bf16)
        grads_ref[rate_row:, :] = jnp.zeros((RATE_ROWS, GROUP), bf16)

    @pl.when(count > 0)
    def step():
        carry = flags[0, turn].astype(f32)
        grad_rates = []
        for head in range(heads):
            rows = slice(head * HD, (head + 1) * HD)
            keep = scalars_ref[0, head]
            push = scalars_ref[1, head] * carry
            base_first = jnp.where(carry > 0.5, saved_ref[0, 0, rows, :], first_ref[rows, :])
            base_second = jnp.where(carry > 0.5, saved_ref[0, 1, rows, :], second_ref[rows, :])
            grad_a = message[0, rows, :]
            grad_b = message[1, rows, :]
            grad_sa = message[2, rows, :] + grad_a
            grad_sb = message[3, rows, :] + grad_b
            momentum_part = carry * (
                jnp.sum(saved_ref[0, 2, rows, :] * grad_sa, axis=0, keepdims=True)
                + jnp.sum(saved_ref[0, 3, rows, :] * grad_sb, axis=0, keepdims=True)
            )
            decay_part = -(
                jnp.sum(base_first * grad_a, axis=0, keepdims=True)
                + jnp.sum(base_second * grad_b, axis=0, keepdims=True)
            )
            grad_scalars_ref[2 * head : 2 * head + 1, :] += decay_part
            grad_scalars_ref[2 * head + 1 : 2 * head + 2, :] += momentum_part
            back_a = (-grad_sa).astype(bf16)
            back_b = (-grad_sb).astype(bf16)
            raw = main_ref[spot(heads, head, 0), :].astype(f32)
            inverse = inverse_root(raw)
            normal = raw * inverse
            keys = normal.astype(bf16)
            first_low = base_first.astype(bf16)
            second_low = base_second.astype(bf16)
            inner = dot_tn(first_low, keys)
            gate = jax.nn.sigmoid(inner)
            active = inner * gate
            slope = gate + active * (1.0 - gate)
            bend = gate * (1.0 - gate) * (2.0 + inner - 2.0 * active)
            active_low = active.astype(bf16)
            weight = update_ref[0] * (1.0 / GROUP)
            at = rate_row + head
            rate_sigmoid = jax.nn.sigmoid(main_ref[at : at + 1, :].astype(f32))
            rate = RATE_SCALE * rate_sigmoid
            error = dot_nn(second_low, active_low) - main_ref[spot(heads, head, 1), :].astype(f32)
            pull = (error * (rate * weight)).astype(bf16)
            spread = dot_tn(second_low, pull)
            inner_pull = (spread * slope).astype(bf16)
            back_inner = dot_tn(back_a, keys)
            back_spread = (back_inner * slope).astype(bf16)
            grad_pull = dot_nn(back_b, active_low) + dot_nn(second_low, back_spread)
            grad_rates.append(
                jnp.sum(grad_pull * error, axis=0, keepdims=True)
                * weight
                * rate
                * (1.0 - rate_sigmoid)
            )
            grad_error = grad_pull * (rate * weight)
            grad_error_low = grad_error.astype(bf16)
            grads_ref[spot(heads, head, 1), :] = (-grad_error).astype(bf16)
            grad_active = dot_tn(back_b, pull) + dot_tn(second_low, grad_error_low)
            grad_inner = (back_inner * spread * bend + grad_active * slope).astype(bf16)
            grad_normal = dot_nn(back_a, inner_pull) + dot_nn(first_low, grad_inner)
            grads_ref[spot(heads, head, 0), :] = (
                inverse
                * (grad_normal - normal * jnp.mean(grad_normal * normal, axis=0, keepdims=True))
            ).astype(bf16)
            base_grad_a = keep * grad_a + dot_nt(keys, grad_inner)
            base_grad_b = (
                keep * grad_b + dot_nt(pull, back_spread) + dot_nt(grad_error_low, active_low)
            )
            message[0, rows, :] = carry * base_grad_a
            message[1, rows, :] = carry * base_grad_b
            message[2, rows, :] = push * grad_sa
            message[3, rows, :] = push * grad_sb
            grad_first_ref[rows, :] += (1.0 - carry) * base_grad_a
            grad_second_ref[rows, :] += (1.0 - carry) * base_grad_b
        grad_rates.append(jnp.zeros((RATE_ROWS - heads, GROUP), f32))
        grads_ref[rate_row:, :] = jnp.concatenate(
            grad_rates, axis=0
        ).astype(bf16)

    retain = retain_ref[0]

    def recall_back(first, second, grad_recalled, head):
        rows = slice(head * HD, (head + 1) * HD)
        raw = main_ref[spot(heads, head, 2), :].astype(f32)
        inverse = inverse_root(raw)
        normal = raw * inverse
        probes = normal.astype(bf16)
        first_low = first[rows, :].astype(bf16)
        inner = dot_tn(first_low, probes)
        gate = jax.nn.sigmoid(inner)
        active = inner * gate
        slope = gate + active * (1.0 - gate)
        grad_inner = (dot_tn(second[rows, :].astype(bf16), grad_recalled) * slope).astype(bf16)
        grad_second = dot_nt(grad_recalled, active.astype(bf16))
        grad_first = dot_nt(probes, grad_inner)
        grad_normal = dot_nn(first_low, grad_inner)
        grad_probes = inverse * (
            grad_normal - normal * jnp.mean(grad_normal * normal, axis=0, keepdims=True)
        )
        return grad_first, grad_second, grad_probes

    only_state = flags[1, turn] * (1 - flags[2, turn])
    only_init = flags[2, turn] * (1 - flags[1, turn])

    def from_state(whole):
        for head in range(heads):
            rows = slice(head * HD, (head + 1) * HD)
            grad_recalled = pull_ref[0, rows, :]
            if not whole:
                grad_recalled = (grad_recalled.astype(f32) * retain).astype(bf16)
            grad_first, grad_second, grad_probes = recall_back(
                saved_ref[0, 0], saved_ref[0, 1], grad_recalled, head
            )
            message[0, rows, :] += grad_first
            message[1, rows, :] += grad_second
            grads_ref[spot(heads, head, 2), :] = grad_probes.astype(bf16)

    def from_init(whole):
        for head in range(heads):
            rows = slice(head * HD, (head + 1) * HD)
            grad_recalled = pull_ref[0, rows, :]
            if not whole:
                grad_recalled = (grad_recalled.astype(f32) * (1.0 - retain)).astype(bf16)
            grad_first, grad_second, grad_probes = recall_back(
                first_ref[...], second_ref[...], grad_recalled, head
            )
            grad_first_ref[rows, :] += grad_first
            grad_second_ref[rows, :] += grad_second
            if not whole:
                grad_probes = grad_probes + grads_ref[spot(heads, head, 2), :].astype(f32)
            grads_ref[spot(heads, head, 2), :] = grad_probes.astype(bf16)

    @pl.when(only_state == 1)
    def state_alone():
        from_state(True)

    @pl.when(only_init == 1)
    def init_alone():
        from_init(True)

    @pl.when(only_state + only_init == 0)
    def both():
        from_state(False)
        from_init(False)


def memory_backward(
    flags, main, retain, update, first, second, scalars, saved, pull
):
    chips, rows, width = pull.shape
    heads = rows // HD
    blocks = chips * width // GROUP
    per = width // GROUP
    all_rows = 3 * rows + RATE_ROWS

    def block(count, flags):
        turn = blocks - 1 - count
        return (0, ((turn // per) ^ flags[4, 0]) * per + ((turn % per) ^ flags[3, 0]))

    def by_chip(count, flags):
        turn = blocks - 1 - count
        return (turn // per, 0, turn % per)

    def by_turn(count, flags):
        return (blocks - 1 - count, 0, 0)

    def whole(count, flags):
        return (0, 0)

    line = pl.BlockSpec((1, 1, GROUP), by_turn)
    matrix = pl.BlockSpec((rows, MH), whole)
    return pl.pallas_call(
        lambda *refs: memory_backward_kernel(heads, blocks, *refs),
        grid_spec=pltpu.PrefetchScalarGridSpec(
            num_scalar_prefetch=1,
            grid=(blocks,),
            in_specs=[
                pl.BlockSpec((3 * rows + RATE_ROWS, GROUP), block),
                line,
                line,
                matrix,
                matrix,
                pl.BlockSpec(memory_space=pltpu.SMEM),
                pl.BlockSpec(
                    (1, 4, rows, MH), lambda count, flags: (blocks - 1 - count, 0, 0, 0)
                ),
                pl.BlockSpec((1, rows, GROUP), by_chip),
            ],
            out_specs=[
                pl.BlockSpec((all_rows, GROUP), block),
                matrix,
                matrix,
                pl.BlockSpec((8, MH), whole),
            ],
            scratch_shapes=[pltpu.VMEM((4, rows, MH), f32)],
        ),
        out_shape=[
            jax.ShapeDtypeStruct((all_rows, chips * width), bf16),
            jax.ShapeDtypeStruct((rows, MH), f32),
            jax.ShapeDtypeStruct((rows, MH), f32),
            jax.ShapeDtypeStruct((8, MH), f32),
        ],
        compiler_params=pltpu.CompilerParams(vmem_limit_bytes=56 * 2**20),
        cost_estimate=pl.CostEstimate(
            flops=blocks * heads * 19 * 2 * GROUP * HD * MH * 4,
            bytes_accessed=blocks * 8 * rows * MH * 4,
            transcendentals=blocks * heads * 2 * MH * GROUP,
        ),
    )(flags, main, retain, update, first, second, scalars, saved, pull)


QUERIES = 256


def visible_bias(bias_ref, row_ref, col_ref):
    shape = bias_ref.shape[1:]
    key = lax.broadcasted_iota(jnp.int32, shape, 0)
    query = lax.broadcasted_iota(jnp.int32, shape, 1)
    for block in range(bias_ref.shape[0]):
        seen = jnp.logical_and(key <= query, col_ref[block] == row_ref[block])
        bias_ref[block] = jnp.where(seen, 0.0, -1e30)


def attention_forward_kernel(
    scale, core, low_ref, query_ref, far_ref, side_ref, row_ref, col_ref, mixed_ref, total_ref, bias_ref
):
    @pl.when(jnp.logical_and(pl.program_id(0) == 0, pl.program_id(1) == 0))
    def fill():
        visible_bias(bias_ref, row_ref, col_ref)

    block = pl.program_id(1)
    for part in range(GROUP // QUERIES):
        lanes = slice(part * QUERIES, (part + 1) * QUERIES)
        upto = (part + 1) * QUERIES
        query = query_ref[:, lanes]
        bias = bias_ref[block, :upto, lanes]
        s_p = dot_tn(side_ref[:HD], query) * scale
        s_r = dot_tn(far_ref[:HD, :upto], query) * scale + bias
        s_l = dot_tn(low_ref[:HD, :upto], query) * scale + bias
        top = jnp.maximum(
            jnp.max(s_p, axis=0, keepdims=True),
            jnp.maximum(
                jnp.max(s_r, axis=0, keepdims=True), jnp.max(s_l, axis=0, keepdims=True)
            ),
        )
        e_p = jnp.exp(s_p - top)
        e_r = jnp.exp(s_r - top)
        e_l = jnp.exp(s_l - top)
        total = (
            jnp.sum(e_p, axis=0, keepdims=True)
            + jnp.sum(e_r, axis=0, keepdims=True)
            + jnp.sum(e_l, axis=0, keepdims=True)
        )
        mixed = (
            dot_nn(side_ref[HD:], e_p.astype(bf16))
            + dot_nn(far_ref[HD:, :upto], e_r.astype(bf16))
            + dot_nn(low_ref[HD:, :upto], e_l.astype(bf16))
        )
        mixed_ref[:, lanes] = (mixed / total).astype(bf16)
        total_ref[0, :, lanes] = top + jnp.log(total)


def attention_specs(rows, width):
    count = width // GROUP
    heads = rows // HD
    low = pl.BlockSpec((2 * HD, GROUP), lambda head, block, core: (head, block))
    query = pl.BlockSpec((HD, GROUP), lambda head, block, core: (2 * heads + head, block))
    far = pl.BlockSpec((2 * HD, GROUP), lambda head, block, core: (head, block ^ core[0]))
    side = pl.BlockSpec((2 * HD, NP), lambda head, block, core: (head, 0))
    row = pl.BlockSpec((count, 1, GROUP), lambda head, block, core: (0, 0, 0))
    col = pl.BlockSpec((count, GROUP, 1), lambda head, block, core: (0, 0, 0))
    main = pl.BlockSpec((HD, GROUP), lambda head, block, core: (head, block))
    line = pl.BlockSpec((1, 1, GROUP), lambda head, block, core: (head, 0, block))
    return low, query, far, side, row, col, main, line


def attention_forward(scale, core, low, far, side, row, col):
    rows, width = low.shape[0] // 3, low.shape[1]
    low_spec, query_spec, far_spec, side_spec, row_spec, col_spec, main, line = attention_specs(
        rows, width
    )
    heads, count = rows // HD, width // GROUP
    return pl.pallas_call(
        lambda *refs: attention_forward_kernel(scale, *refs),
        grid_spec=pltpu.PrefetchScalarGridSpec(
            num_scalar_prefetch=1,
            grid=(heads, count),
            in_specs=[low_spec, query_spec, far_spec, side_spec, row_spec, col_spec],
            out_specs=[main, line],
            scratch_shapes=[pltpu.VMEM((count, GROUP, GROUP), f32)],
        ),
        out_shape=[
            jax.ShapeDtypeStruct((rows, width), bf16),
            jax.ShapeDtypeStruct((heads, 1, width), f32),
        ],
        compiler_params=pltpu.CompilerParams(vmem_limit_bytes=50 * 2**20),
        cost_estimate=pl.CostEstimate(
            flops=heads * count * 4 * GROUP * 1088 * HD * 4,
            bytes_accessed=6 * rows * width * 2,
            transcendentals=heads * count * GROUP * 1088,
        ),
    )(core, low, low, far, side, row, col)


def attention_backward_kernel(
    scale,
    core,
    low_ref,
    query_ref,
    far_ref,
    side_ref,
    row_ref,
    col_ref,
    mixed_ref,
    total_ref,
    grad_ref,
    grads_ref,
    grad_far_ref,
    grad_side_ref,
    bias_ref,
):
    @pl.when(jnp.logical_and(pl.program_id(0) == 0, pl.program_id(1) == 0))
    def fill():
        visible_bias(bias_ref, row_ref, col_ref)

    block = pl.program_id(1)

    @pl.when(block == 0)
    def blank():
        grad_side_ref[...] = jnp.zeros_like(grad_side_ref)

    parts = GROUP // QUERIES
    sums = {}
    for part in reversed(range(parts)):
        lanes = slice(part * QUERIES, (part + 1) * QUERIES)
        upto = (part + 1) * QUERIES
        query = query_ref[:, lanes]
        grad = grad_ref[:, lanes]
        bias = bias_ref[block, :upto, lanes] - total_ref[0, :, lanes]
        mean = jnp.sum(
            grad.astype(f32) * mixed_ref[:, lanes].astype(f32), axis=0, keepdims=True
        )
        grad_query = jnp.zeros((HD, QUERIES), f32)
        for name, keys, values, extra in (
            ("p", side_ref[:HD], side_ref[HD:], -total_ref[0, :, lanes]),
            ("r", far_ref[:HD, :upto], far_ref[HD:, :upto], bias),
            ("l", low_ref[:HD, :upto], low_ref[HD:, :upto], bias),
        ):
            chances = jnp.exp(dot_tn(keys, query) * scale + extra)
            slope = (chances * (dot_tn(values, grad) - mean)).astype(bf16)
            grad_query += dot_nn(keys, slope)
            grad_keys = dot_nt(query, slope)
            grad_values = dot_nt(grad, chances.astype(bf16))
            if name in sums:
                old_keys, old_values = sums[name]
                if name == "p":
                    sums[name] = (old_keys + grad_keys, old_values + grad_values)
                else:
                    sums[name] = (
                        jnp.concatenate([old_keys[:, :upto] + grad_keys, old_keys[:, upto:]], axis=1),
                        jnp.concatenate(
                            [old_values[:, :upto] + grad_values, old_values[:, upto:]], axis=1
                        ),
                    )
            else:
                sums[name] = (grad_keys, grad_values)
        grads_ref[2 * HD :, lanes] = (grad_query * scale).astype(bf16)
    grad_side_ref[:HD] += sums["p"][0] * scale
    grad_side_ref[HD:] += sums["p"][1]
    grad_far_ref[:HD] = (sums["r"][0] * scale).astype(bf16)
    grad_far_ref[HD:] = sums["r"][1].astype(bf16)
    grads_ref[:HD] = (sums["l"][0] * scale).astype(bf16)
    grads_ref[HD : 2 * HD] = sums["l"][1].astype(bf16)


def attention_backward(scale, core, low, far, side, row, col, mixed, total, grad):
    rows, width = low.shape[0] // 3, low.shape[1]
    low_spec, query_spec, far_spec, side_spec, row_spec, col_spec, main, line = attention_specs(
        rows, width
    )
    heads, count = rows // HD, width // GROUP
    return pl.pallas_call(
        lambda *refs: attention_backward_kernel(scale, *refs),
        grid_spec=pltpu.PrefetchScalarGridSpec(
            num_scalar_prefetch=1,
            grid=(heads, count),
            in_specs=[
                low_spec,
                query_spec,
                far_spec,
                side_spec,
                row_spec,
                col_spec,
                main,
                line,
                main,
            ],
            out_specs=[
                pl.BlockSpec((3 * HD, GROUP), lambda head, block, core: (head, block)),
                far_spec,
                side_spec,
            ],
            scratch_shapes=[pltpu.VMEM((count, GROUP, GROUP), f32)],
        ),
        out_shape=[
            jax.ShapeDtypeStruct((3 * rows, width), bf16),
            jax.ShapeDtypeStruct((2 * rows, width), bf16),
            jax.ShapeDtypeStruct((2 * rows, NP), f32),
        ],
        compiler_params=pltpu.CompilerParams(vmem_limit_bytes=50 * 2**20),
        cost_estimate=pl.CostEstimate(
            flops=heads * count * 10 * GROUP * 1088 * HD * 4,
            bytes_accessed=14 * rows * width * 2,
            transcendentals=heads * count * GROUP * 1088,
        ),
    )(core, low, low, far, side, row, col, mixed, total, grad)


def head_of(core, chip, turn, chips, heads):
    return core * chips * heads + turn * chips + chip


def pack_weights(chips, heads, key, value, query, rate, gains, side):
    shard = key.shape[0]

    def kernel(key_ref, value_ref, query_ref, rate_ref, gains_ref, side_ref, out_ref):
        for core in range(2):
            order = [
                head_of(core, chip, turn, chips, heads)
                for chip in range(chips)
                for turn in range(heads)
            ]
            end = 3 * D // 2
            out_ref[core, :, end:] = jnp.zeros((shard, 128), bf16)
            out_ref[core, :, end : end + NP] = side_ref[...]
            out_ref[core, :, end + NP : end + NP + 2] = gains_ref[...]
            for at, head in enumerate(order):
                columns = slice(head * HD, (head + 1) * HD)
                low = 2 * at * HD
                out_ref[core, :, low : low + HD] = key_ref[:, columns]
                out_ref[core, :, low + HD : low + 2 * HD] = value_ref[:, columns]
                low = D + at * HD
                out_ref[core, :, low : low + HD] = query_ref[:, columns]
                low = end + NP + 2 + at
                out_ref[core, :, low : low + 1] = rate_ref[:, head : head + 1]

    return pl.pallas_call(
        kernel, out_shape=jax.ShapeDtypeStruct((2, shard, 3 * D // 2 + 128), bf16)
    )(key, value, query, rate, gains, side)


def pack_columns(chain, gate, up):
    shard, whole = gate.shape
    own = whole // chain

    def kernel(gate_ref, up_ref, out_ref):
        groups = out_ref.shape[2] // (2 * size)
        for place in range(chain):
            for which, ref in enumerate((gate_ref, up_ref)):
                for group in range(groups):
                    at = which * own + group * size
                    start = (group * chain + place) * size
                    out_ref[place, :, at : at + size] = ref[:, start : start + size]

    size = whole // (D // shard)
    return pl.pallas_call(
        kernel, out_shape=jax.ShapeDtypeStruct((chain, shard, 2 * own), bf16)
    )(gate, up)


def unpack_columns(parts, gate, up, gain):
    chain, shard, both = parts.shape
    own = both // 2
    whole = gate.shape[1]
    size = whole // (D // shard)

    def kernel(parts_ref, gate_ref, up_ref, gain_ref, gate_out, up_out, gain_out):
        total = jnp.zeros((shard, 1), f32)
        for which, (ref, out) in enumerate(((gate_ref, gate_out), (up_ref, up_out))):
            for place in range(chain):
                for group in range(own // size):
                    at = which * own + group * size
                    start = (group * chain + place) * size
                    out[:, start : start + size] = parts_ref[place, :, at : at + size].astype(f32)
            total += jnp.sum(out[...] * ref[...].astype(f32), axis=1, keepdims=True)
        gain_out[...] = total / gain_ref[...].astype(f32)

    return pl.pallas_call(
        kernel,
        out_shape=[
            jax.ShapeDtypeStruct((shard, whole), f32),
            jax.ShapeDtypeStruct((shard, whole), f32),
            jax.ShapeDtypeStruct((shard, 1), f32),
        ],
    )(parts, gate, up, gain)


def unpack_weights(chips, heads, parts, context, key, value, query, rate, gain):
    shard = key.shape[0]

    def kernel(parts_ref, context_ref, key_ref, value_ref, query_ref, rate_ref, gain_ref, *outs):
        key_out, value_out, query_out, rate_out, gain_out = outs
        total = jnp.zeros((shard, 1), f32)
        for core in range(2):
            for chip in range(chips):
                place = chip * 2 + core
                for turn in range(heads):
                    head = head_of(core, chip, turn, chips, heads)
                    rate_out[:, head : head + 1] = parts_ref[
                        place, :, 3 * heads * HD + turn : 3 * heads * HD + turn + 1
                    ].astype(f32)
                    columns = slice(head * HD, (head + 1) * HD)
                    for which, (weight, out) in enumerate(
                        ((key_ref, key_out), (value_ref, value_out), (query_ref, query_out))
                    ):
                        grad = parts_ref[place, :, spot(heads, turn, which)].astype(f32)
                        total += jnp.sum(
                            grad * weight[:, columns].astype(f32), axis=1, keepdims=True
                        )
                        if which < 2:
                            near = (2 * (chip * heads + turn) + which) * HD
                            grad += context_ref[core, :, near : near + HD].astype(f32)
                        out[:, columns] = grad
        total += jnp.sum(rate_out[...] * rate_ref[...].astype(f32), axis=1, keepdims=True)
        gain_out[...] = total / gain_ref[...].astype(f32)

    wide = jax.ShapeDtypeStruct((shard, D), f32)
    return pl.pallas_call(
        kernel,
        out_shape=[
            wide,
            wide,
            wide,
            jax.ShapeDtypeStruct((shard, H), f32),
            jax.ShapeDtypeStruct((shard, 1), f32),
        ],
    )(parts, context, key, value, query, rate, gain)


def project_blocks(first, blocks, tokens, gain, weight, old=()):
    columns = weight.shape[0]
    count = len(tokens)

    def kernel(*refs):
        gain_ref, weight_ref = refs[count : count + 2]
        normed_ref, main_ref = refs[-2:]
        for at in range(count):

            @pl.when(pl.program_id(0) == at)
            def one(tokens_ref=refs[at]):
                wide = tokens_ref[...].astype(f32)
                scale = lax.rsqrt(jnp.mean(wide * wide, axis=1, keepdims=True) + norm_epsilon)
                low = (wide * scale * gain_ref[...]).astype(bf16)
                normed_ref[...] = low
                main_ref[...] = dot_nt(weight_ref[...], low).astype(bf16)

    return pl.pallas_call(
        kernel,
        grid=(count,),
        in_specs=[pl.BlockSpec((GROUP, D), lambda i: (0, 0))] * count
        + [
            pl.BlockSpec((1, D), lambda i: (0, 0)),
            pl.BlockSpec((columns, D), lambda i: (0, 0)),
        ]
        + [pl.BlockSpec(memory_space=pl.ANY)] * len(old),
        out_specs=[
            pl.BlockSpec((GROUP, D), lambda i: (first + i, 0)),
            pl.BlockSpec((columns, GROUP), lambda i: (0, first + i)),
        ],
        out_shape=[
            jax.ShapeDtypeStruct((blocks * GROUP, D), bf16),
            jax.ShapeDtypeStruct((columns, blocks * GROUP), bf16),
        ],
        input_output_aliases={count + 2: 0, count + 3: 1} if old else {},
        compiler_params=pltpu.CompilerParams(vmem_limit_bytes=52 * 2**20),
        cost_estimate=pl.CostEstimate(
            flops=count * 2 * GROUP * D * columns * 2,
            bytes_accessed=count * (GROUP * D * 4 + columns * GROUP * 2) + columns * D * 2,
            transcendentals=0,
        ),
    )(*tokens, gain, weight, *old)


def merge_blocks(chip, groups, grads, grad_part, normed, weight):
    columns, tokens = grads.shape
    chips, part_rows, width = grad_part.shape
    heads = part_rows // (3 * HD)
    blocks = tokens // GROUP
    per = width // GROUP
    cut = D // groups

    def kernel(
        chip_ref, grads_ref, part_ref, normed_ref, weight_ref, out_ref, weight_out, total, held
    ):
        at = pl.program_id(0)
        for head in range(heads):
            for which in range(3):
                low = (3 * head + which) * HD
                there = spot(heads, head, which)
                held[there, :] = (
                    grads_ref[there, :].astype(f32) + part_ref[0, low : low + HD, :].astype(f32)
                ).astype(bf16)
        held[part_rows:, :] = grads_ref[part_rows:, :]
        merged = held[...]
        out_ref[...] = dot_tn(merged, weight_ref[...]).astype(bf16)
        part = dot_nn(merged, normed_ref[...])

        @pl.when(at == 0)
        def first():
            total[...] = part

        @pl.when(at > 0)
        def more():
            total[...] += part

        @pl.when(at == blocks - 1)
        def last():
            for group in range(groups):
                weight_out[group] = total[:, group * cut : (group + 1) * cut].astype(bf16)

    def spread(at, chip_ref):
        return ((at // per) ^ chip_ref[0], 0, at % per)

    return pl.pallas_call(
        kernel,
        grid_spec=pltpu.PrefetchScalarGridSpec(
            num_scalar_prefetch=1,
            grid=(blocks,),
            in_specs=[
                pl.BlockSpec((columns, GROUP), lambda at, chip_ref: (0, at)),
                pl.BlockSpec((1, part_rows, GROUP), spread),
                pl.BlockSpec((GROUP, D), lambda at, chip_ref: (at, 0)),
                pl.BlockSpec((columns, D), lambda at, chip_ref: (0, 0)),
            ],
            out_specs=[
                pl.BlockSpec((GROUP, D), lambda at, chip_ref: (at, 0)),
                pl.BlockSpec((groups, columns, cut), lambda at, chip_ref: (0, 0, 0)),
            ],
            scratch_shapes=[pltpu.VMEM((columns, D), f32), pltpu.VMEM((columns, GROUP), bf16)],
        ),
        out_shape=[
            jax.ShapeDtypeStruct((tokens, D), bf16),
            jax.ShapeDtypeStruct((groups, columns, cut), bf16),
        ],
        compiler_params=pltpu.CompilerParams(vmem_limit_bytes=50 * 2**20),
        cost_estimate=pl.CostEstimate(
            flops=blocks * 4 * GROUP * D * columns * 2,
            bytes_accessed=blocks * GROUP * (D * 4 + columns * 4),
            transcendentals=0,
        ),
    )(chip, grads, grad_part, normed, weight)


def ffn_chunk(place, chunks, normed, grad, w_gate_up, w_down, old=()):
    own = w_down.shape[0]

    def kernel(*refs):
        w_gate_up_ref, w_down_ref = refs[4:6]
        all_normed, all_grad, all_hidden, all_grads, out_ref, back_ref = refs[-6:]
        for at in range(2):

            @pl.when(pl.program_id(0) == at)
            def one(normed_ref=refs[at], grad_ref=refs[2 + at]):
                low = normed_ref[...]
                grad_low = grad_ref[...]
                all_normed[...] = low
                all_grad[...] = grad_low
                gate = dot_nn(low, w_gate_up_ref[:, :own])
                up = dot_nn(low, w_gate_up_ref[:, own:])
                gate_sigmoid = jax.nn.sigmoid(gate)
                gate_silu = gate * gate_sigmoid
                hidden = (gate_silu * up).astype(bf16)
                all_hidden[...] = hidden
                out_ref[0] = dot_nn(hidden, w_down_ref[...]).astype(bf16)
                grad_hidden = dot_nt(grad_low, w_down_ref[...])
                slope = gate_sigmoid * (1.0 + gate * (1.0 - gate_sigmoid))
                all_grads[:, :own] = (grad_hidden * up * slope).astype(bf16)
                all_grads[:, own:] = (grad_hidden * gate_silu).astype(bf16)
                back_ref[0] = dot_nt(all_grads[...], w_gate_up_ref[...]).astype(bf16)

    tokens = chunks * 2 * GROUP
    whole = pl.BlockSpec((GROUP, D), lambda i: (0, 0))
    return pl.pallas_call(
        kernel,
        grid=(2,),
        in_specs=[whole] * 4
        + [
            pl.BlockSpec((D, 2 * own), lambda i: (0, 0)),
            pl.BlockSpec((own, D), lambda i: (0, 0)),
        ]
        + [pl.BlockSpec(memory_space=pl.ANY)] * len(old),
        out_specs=[
            pl.BlockSpec((GROUP, D), lambda i: (2 * place + i, 0)),
            pl.BlockSpec((GROUP, D), lambda i: (2 * place + i, 0)),
            pl.BlockSpec((GROUP, own), lambda i: (2 * place + i, 0)),
            pl.BlockSpec((GROUP, 2 * own), lambda i: (2 * place + i, 0)),
            pl.BlockSpec((1, GROUP, D), lambda i: (i, 0, 0)),
            pl.BlockSpec((1, GROUP, D), lambda i: (i, 0, 0)),
        ],
        out_shape=[
            jax.ShapeDtypeStruct((tokens, D), bf16),
            jax.ShapeDtypeStruct((tokens, D), bf16),
            jax.ShapeDtypeStruct((tokens, own), bf16),
            jax.ShapeDtypeStruct((tokens, 2 * own), bf16),
            jax.ShapeDtypeStruct((2, GROUP, D), bf16),
            jax.ShapeDtypeStruct((2, GROUP, D), bf16),
        ],
        input_output_aliases={6 + at: at for at in range(len(old))},
        compiler_params=pltpu.CompilerParams(vmem_limit_bytes=56 * 2**20),
        cost_estimate=pl.CostEstimate(
            flops=2 * GROUP * D * own * 12, bytes_accessed=20 * GROUP * D, transcendentals=2 * GROUP * own
        ),
    )(*normed, *grad, w_gate_up, w_down, *old)


def tokens_product(left, right):
    tokens, rows = left.shape
    columns = right.shape[1]
    steps = tokens // GROUP

    def kernel(left_ref, right_ref, out_ref, total):
        at = pl.program_id(0)
        part = dot_tn(left_ref[...], right_ref[...])

        @pl.when(at == 0)
        def first():
            total[...] = part

        @pl.when(at > 0)
        def more():
            total[...] += part

        @pl.when(at == steps - 1)
        def last():
            out_ref[...] = total[...].astype(bf16)

    return pl.pallas_call(
        kernel,
        grid=(steps,),
        in_specs=[
            pl.BlockSpec((GROUP, rows), lambda at: (at, 0)),
            pl.BlockSpec((GROUP, columns), lambda at: (at, 0)),
        ],
        out_specs=pl.BlockSpec((rows, columns), lambda at: (0, 0)),
        out_shape=jax.ShapeDtypeStruct((rows, columns), bf16),
        scratch_shapes=[pltpu.VMEM((rows, columns), f32)],
        compiler_params=pltpu.CompilerParams(vmem_limit_bytes=50 * 2**20),
        cost_estimate=pl.CostEstimate(
            flops=2 * tokens * rows * columns,
            bytes_accessed=2 * tokens * (rows + columns),
            transcendentals=0,
        ),
    )(left, right)


def matmul(left, right, left_dim, right_dim, out=f32):
    return lax.dot_general(
        left, right, (((left_dim,), (right_dim,)), ((), ())), preferred_element_type=f32
    ).astype(out)


def core_swap(value):
    return lax.ppermute(value, "core", [(0, 1), (1, 0)])


def gather_chips(value):
    return lax.all_gather(value, ("dp", "chip"), axis=0, tiled=True)


def scatter_chips(value):
    return lax.psum_scatter(value, ("dp", "chip"), scatter_dimension=0, tiled=True)


def after(value, *events):
    return lax.optimization_barrier((value, *events))[0]


def chip_swap(value, step):
    count = lax.axis_size("chip")
    return lax.ppermute(value, "chip", [(index, index ^ step) for index in range(count)])


def chip_parts(value):
    count = lax.axis_size("chip")
    if count != 4:
        return [value] + [chip_swap(value, step) for step in range(1, count)]
    middle = value.shape[0] // 2
    along = chip_swap(value, 1)
    across = chip_swap(value, 2)
    corner = jnp.concatenate([chip_swap(along[:middle], 2), chip_swap(across[middle:], 1)], axis=0)
    return [value, along, across, corner]


def corner_sums(corner, parts, *events):
    middle = corner.shape[0] // 2
    from_along = chip_swap(corner[:middle], 1)
    from_across = chip_swap(corner[middle:], 2)
    if events:
        from_along, from_across = after(from_along, *events), after(from_across, *events)
    from_along, from_across = from_along.astype(f32), from_across.astype(f32)
    first = jnp.concatenate(
        [parts[1][:middle].astype(f32), parts[1][middle:].astype(f32) + from_across], axis=0
    )
    second = jnp.concatenate(
        [parts[2][:middle].astype(f32) + from_along, parts[2][middle:].astype(f32)], axis=0
    )
    return first.astype(bf16), second.astype(bf16)


def side_sums(own, first, second, *events):
    first, second = chip_swap(first, 1), chip_swap(second, 2)
    if events:
        first, second = after(first, *events), after(second, *events)
    return own.astype(f32) + first.astype(f32) + second.astype(f32)


def chip_sums(parts):
    count = lax.axis_size("chip")
    if count != 4:
        total = parts[0].astype(f32)
        for step in range(1, count):
            total = total + chip_swap(parts[step].astype(bf16), step).astype(f32)
        return total
    return side_sums(parts[0], *corner_sums(parts[3].astype(bf16), parts))


def line_gather(value):
    count = lax.axis_size("dp")
    index = lax.axis_index("dp")
    up = down = value
    found = [value] * count
    for step in range(1, count):
        up = lax.ppermute(up, "dp", [(at, at + 1) for at in range(count - 1)])
        down = lax.ppermute(down, "dp", [(at + 1, at) for at in range(count - 1)])
        for at in range(count):
            found[at] = jnp.where(
                index - at == step, up, jnp.where(at - index == step, down, found[at])
            )
    return jnp.stack(found)


def sum_everywhere(value, marks):
    steps = [("core", 1)]
    for axis in ("chip", "dp"):
        step = 1
        while step < lax.axis_size(axis):
            steps.append((axis, step))
            step *= 2
    for at, (axis, step) in enumerate(steps):
        pairs = [(index, index ^ step) for index in range(lax.axis_size(axis))]
        other = lax.ppermute(value, axis, pairs)
        value = value + (after(other, marks[at]) if at < len(marks) else other)
    return value


def by_core(core, mine, other, axis=0):
    return jnp.where(
        core == 0,
        jnp.concatenate([mine, other], axis=axis),
        jnp.concatenate([other, mine], axis=axis),
    )


def inverse_rms(values):
    return lax.rsqrt(jnp.mean(values * values, axis=-1, keepdims=True) + norm_epsilon)


def norm_back(grad_normed, values, inverse, gain):
    normal = values * inverse
    scaled = grad_normed * gain
    return inverse * (scaled - normal * jnp.mean(scaled * normal, axis=-1, keepdims=True))


def on_device(
    inputs,
    segments,
    attn_gain,
    query_weight,
    key_weight,
    value_weight,
    output_weight,
    persistent,
    memory_first,
    memory_second,
    rate_weight,
    decay_logit,
    momentum_logit,
    ffn_gain,
    gate_weight,
    up_weight,
    down_weight,
    cotangent,
):
    groups, chips, core_count = (lax.axis_size("dp"), lax.axis_size("chip"), 2)
    core = lax.axis_index("core")
    chip = lax.axis_index("chip")
    position = chip * core_count + core
    chain = chips * core_count
    devices = groups * chain
    scale = HD ** (-0.5)
    half = D // 2
    core_heads = H // core_count
    heads = core_heads // chips
    rows = heads * HD
    width = 2 * GROUP
    all_rows = 3 * rows + RATE_ROWS
    shard = query_weight.shape[0]
    ff_own = gate_weight.shape[1] // chain
    pieces = devices // 2
    per_head = max(HD // shard, 1)
    near = 2 * shard == HD and core_heads == heads * chips

    tokens = inputs[0]
    grad_out = cotangent[0]

    if chips == 4:
        along, across = chip_swap(tokens, 1), chip_swap(tokens, 2)
    w_sides = pack_weights(
        chips,
        heads,
        key_weight,
        value_weight,
        query_weight,
        rate_weight,
        jnp.stack([attn_gain, ffn_gain], axis=1),
        persistent,
    )
    w_side = lax.dynamic_index_in_dim(w_sides, core, 0, keepdims=False)
    w_side_other = core_swap(lax.dynamic_index_in_dim(w_sides, 1 - core, 0, keepdims=False))
    w_pair = gather_chips(by_core(core, w_side, w_side_other))
    w_context = w_pair[:, : 2 * half]
    w_tail = w_pair[:, 3 * half :]
    persist = w_tail[:, :NP]
    mem_shard = jnp.concatenate([memory_first, memory_second], axis=1)
    if near:
        mem_pair = by_core(core, mem_shard, core_swap(mem_shard))
        mem_line = line_gather(mem_pair).reshape(groups * 2 * shard, 2 * MH)
        mem_mine = lax.dynamic_slice_in_dim(mem_line, core * rows, rows, 0)
    else:
        mem_all = lax.all_gather(mem_shard, ("dp", "chip", "core"), axis=0, tiled=True)
        mem_all = lax.dynamic_slice_in_dim(mem_all, core * half, half, 0)
        mem_all = mem_all.reshape(heads, chips, HD, 2 * MH)
        mem_mine = lax.dynamic_index_in_dim(mem_all, chip, 1, keepdims=False).reshape(rows, 2 * MH)
    mem_mine = mem_mine.astype(f32)
    first_init, second_init = mem_mine[:, :MH], mem_mine[:, MH:]
    if chips == 4:
        cut = GROUP // 2
        corner = jnp.concatenate(
            [chip_swap(along[:cut], 2), chip_swap(across[cut:], 1)], axis=0
        )
        token_halves = [tokens, along, across, corner]
    else:
        token_halves = chip_parts(tokens)
    w_gate_up = lax.all_to_all(
        pack_columns(chain, gate_weight, up_weight), ("chip", "core"), 0, 0, tiled=True
    ).reshape(chain * shard, 2 * ff_own)
    w_main = jnp.concatenate(
        [
            lax.dynamic_slice_in_dim(w_pair, chip * 2 * rows, 2 * rows, 1),
            lax.dynamic_slice_in_dim(w_pair, 2 * half + chip * rows, rows, 1),
            lax.dynamic_slice_in_dim(w_tail, NP + 2 + chip * heads, heads, 1),
            jnp.zeros((D, RATE_ROWS - heads), bf16),
        ],
        axis=1,
    )
    w_flat = after(w_main, w_gate_up).T
    gains = w_tail[:, NP : NP + 2].astype(f32).T
    gain_one, gain_two = gains[:1], gains[1:]

    ids = segments[0].reshape(chain, GROUP)
    first_id, last_id = ids[:, 0], ids[:, GROUP - 1]
    before = jnp.concatenate([first_id[:1], ids[:-1, GROUP - 1]])
    joined = jnp.logical_and(jnp.arange(chain) > 0, first_id == before)
    carry = jnp.logical_and(joined, first_id == last_id)
    kept = jnp.logical_and(joined[:, None], ids == first_id[:, None])
    retain = kept.astype(f32)[:, None, :]
    update = (ids == last_id[:, None]).astype(f32)[:, None, :]
    flags = jnp.stack(
        [
            carry.astype(jnp.int32),
            jnp.any(kept, axis=1).astype(jnp.int32),
            jnp.logical_not(jnp.all(kept, axis=1)).astype(jnp.int32),
            jnp.full((chain,), core, jnp.int32),
            jnp.full((chain,), chip, jnp.int32),
        ]
    )
    pair_ids = jnp.stack(
        [
            lax.dynamic_index_in_dim(ids, position, keepdims=False),
            lax.dynamic_index_in_dim(ids, chip * core_count + 1 - core, keepdims=False),
        ]
    )
    id_row, id_col = pair_ids[:, None, :], pair_ids[:, :, None]
    core_index = core.astype(jnp.int32)[None]
    decay = jax.nn.sigmoid(decay_logit)
    momentum = jax.nn.sigmoid(momentum_logit)

    def own_heads(value):
        return lax.dynamic_index_in_dim(
            value.reshape(core_count, heads, chips)[core], chip, 1, keepdims=False
        )

    scalars = jnp.stack([own_heads(1.0 - decay), own_heads(momentum)])

    token_blocks = []
    for part in token_halves:
        token_blocks += [part, core_swap(part)]
    placed = ()
    for start in range(0, chain, 8):
        placed = project_blocks(
            start, chain, token_blocks[start : start + 8], gain_one, w_flat, placed
        )
    normed_all, main = placed

    out_order = []
    for side in range(2):
        for piece in range(pieces):
            spot_, part = divmod(piece, per_head)
            at_chip, turn = divmod(spot_, heads)
            source = side * pieces + (turn * chips + at_chip) * per_head + part
            out_order.append((source, 2 * piece + side))
    out_moved = lax.ppermute(output_weight, ("dp", "chip", "core"), out_order)
    w_output = gather_chips(after(out_moved, token_halves[3]))

    w_gate_up = lax.all_gather(w_gate_up, "dp", axis=0, tiled=True)
    w_down = lax.all_gather(down_weight, "dp", axis=0, tiled=True)

    def pair_rows(own):
        return jnp.concatenate([own, core_swap(own)], axis=0)

    if chips == 4:
        grad_along, grad_across = [chip_swap(after(grad_out, main), step) for step in (1, 2)]
    recalled, saved = memory_forward(
        flags, main, retain, update, first_init, second_init, scalars, chips
    )
    normed = normed_all[:width]
    low = matmul(w_pair[:, : 3 * half], normed, 0, 1, bf16)
    side = matmul(w_context, persist, 0, 0, bf16)
    recalled = after(lax.all_to_all(recalled, "chip", 0, 0, tiled=True), low, side)
    recalled = recalled.reshape(chips, heads, HD, width).swapaxes(0, 1).reshape(half, width)
    context = by_core(core, recalled, core_swap(recalled))
    if chips == 4:
        grad_along, grad_across = after(grad_along, context), after(grad_across, context)
        grad_corner = (chip_swap(grad_along[:cut], 2), chip_swap(grad_across[cut:], 1))
        grad_halves = [grad_out, grad_along, grad_across, grad_corner]
    else:
        grad_halves = chip_parts(after(grad_out, context))

    far = matmul(w_context, context, 0, 0, bf16)
    mixed, total = attention_forward(scale, core_index, low, far, side, id_row, id_col)

    def pair_sum(left, right, left_dim, right_dim):
        def block(which):
            return lax.slice_in_dim(
                left, which * GROUP, (which + 1) * GROUP, axis=1 - left_dim
            )

        other = core_swap(matmul(block(1), right, left_dim, right_dim, bf16))
        return matmul(block(0), right, left_dim, right_dim) + other.astype(f32)

    middle = tokens.astype(f32) + pair_sum(mixed, w_output, 0, 0)
    inverse_two = inverse_rms(middle)
    normed_own = (middle * inverse_two * gain_two).astype(bf16)
    if chips == 4:
        normed_halves = [normed_own, chip_swap(normed_own, 1), chip_swap(normed_own, 2), None]
    else:
        normed_halves = chip_parts(normed_own)

    outs, grad_normeds, arrays = [], [], ()
    for step in range(chips):
        normed_half, grad_half = normed_halves[step], grad_halves[step]
        if chips == 4 and 0 < step < 3:
            normed_half = after(normed_half, outs[0])
            normed_halves[step] = normed_half
        elif chips == 4 and step == 3:
            normed_half = jnp.concatenate([after(part, outs[2]) for part in normed_corner], axis=0)
            grad_half = jnp.concatenate([after(part, outs[2]) for part in grad_half], axis=0)
        if chips == 4 and step == 2:
            normed_corner = (
                chip_swap(normed_halves[1][:cut], 2),
                chip_swap(normed_halves[2][cut:], 1),
            )
        *arrays, out, grad_normed = ffn_chunk(
            step,
            chips,
            (normed_half, core_swap(normed_half)),
            (grad_half, core_swap(grad_half)),
            w_gate_up,
            w_down,
            arrays,
        )
        outs.append(out)
        grad_normeds.append(grad_normed)
    all_normed, all_grad, all_hidden, all_grad_gate_up = arrays

    def pair_sums(parts, *events):
        return [
            part[0].astype(f32) + core_swap(after(part, *events)[1]).astype(f32) for part in parts
        ]

    grad_normeds = pair_sums(grad_normeds)
    if chips == 4:
        corner_low = grad_normeds[3].astype(bf16)
        grad_down_w = tokens_product(after(all_hidden, corner_low), all_grad)
        first_sum, second_sum = corner_sums(corner_low, grad_normeds, grad_down_w)
        grad_gate_up_w = tokens_product(
            after(all_normed, first_sum, second_sum), all_grad_gate_up
        )
        grad_normed_two = side_sums(grad_normeds[0], first_sum, second_sum, grad_gate_up_w)
        outs = pair_sums(outs, grad_gate_up_w)
    else:
        grad_normed_two = chip_sums(grad_normeds)
        grad_down_w = tokens_product(all_hidden, all_grad)
        grad_gate_up_w = tokens_product(all_normed, all_grad_gate_up)
        outs = pair_sums(outs)
    grad_middle = grad_out.astype(f32) + norm_back(grad_normed_two, middle, inverse_two, gain_two)
    down_part = lax.psum_scatter(grad_down_w, "dp", scatter_dimension=0, tiled=True).astype(f32)
    gate_up_scattered = lax.psum_scatter(grad_gate_up_w, "dp", scatter_dimension=0, tiled=True)

    grad_attended = pair_rows(grad_middle.astype(bf16))
    grad_output_w = matmul(mixed, grad_attended, 1, 0, bf16)
    grad_mixed = matmul(w_output, grad_attended, 1, 1, bf16)
    if chips == 4:
        out_corner = after(outs[3].astype(bf16), grad_normed_two)
        out_first, out_second = corner_sums(out_corner, outs, grad_mixed, grad_output_w)
        events = (out_first, out_second)
    else:
        events = ()
    grad_part, grad_far, grad_side = attention_backward(
        scale,
        core_index,
        low,
        far,
        side,
        id_row,
        id_col,
        mixed,
        total,
        after(grad_mixed, grad_output_w, *events),
    )
    grad_side = grad_side.astype(bf16)
    if chips == 4:
        out_sum = side_sums(outs[0], out_first, out_second, grad_far)
    else:
        out_sum = chip_sums(outs)
    result = (middle + out_sum).astype(bf16)

    def half_rows(which):
        return lax.dynamic_slice_in_dim(w_context, which * half, half, 0)

    pull_other = core_swap(matmul(half_rows(1 - core), grad_far, 1, 0, bf16))
    pull = (matmul(half_rows(core), grad_far, 1, 0) + pull_other.astype(f32)).astype(bf16)
    pull = pull.reshape(heads, chips, HD, width).swapaxes(0, 1).reshape(chips, rows, width)
    pull = lax.all_to_all(after(pull, out_sum), "chip", 0, 0, tiled=True)
    grad_part = lax.all_to_all(
        after(grad_part.reshape(chips, 3 * rows, width), pull), "chip", 0, 0, tiled=True
    )
    grad_context_w = jnp.concatenate(
        [
            (matmul(context, grad_far, 1, 1) + matmul(persist, grad_side, 1, 1)).astype(bf16),
            matmul(w_context, grad_side, 1, 0, bf16),
            jnp.zeros((D, 128 - NP), bf16),
        ],
        axis=1,
    )
    context_part = lax.psum_scatter(grad_context_w, "dp", scatter_dimension=0, tiled=True)
    context_part = context_part.reshape(chips, 2 * shard, 2 * half + 128)
    grads, grad_first, grad_second, grad_scalars = memory_backward(
        flags,
        main,
        retain,
        update,
        first_init,
        second_init,
        scalars,
        saved,
        after(pull, down_part, grad_context_w),
    )
    grad_tokens, grad_heads_w = merge_blocks(
        chip.astype(jnp.int32)[None],
        groups,
        grads,
        after(grad_part, grads),
        normed_all,
        w_flat,
    )
    grad_blocks = grad_tokens.reshape(chips, 2, GROUP, D)
    grad_normeds = [
        grad_blocks[step, 0].astype(f32) + core_swap(grad_blocks[step, 1]).astype(f32)
        for step in range(chips)
    ]
    grad_mem = jnp.concatenate([grad_first, grad_second], axis=1).astype(bf16)
    if near and MH == D // groups:
        spread = jnp.zeros((groups, 4 * shard, MH), bf16)
        spread = lax.dynamic_update_slice_in_dim(
            spread,
            jnp.concatenate(
                [grad_first.reshape(heads, HD, MH), grad_second.reshape(heads, HD, MH)], axis=1
            ).astype(bf16),
            core * heads,
            0,
        )
        grad_heads_w = jnp.concatenate([grad_heads_w, spread], axis=1)
    heads_part = lax.all_to_all(grad_heads_w, "dp", 0, 0, tiled=True)
    tokens_wide = tokens.astype(f32)
    if chips == 4:
        first_sum, second_sum = corner_sums(grad_normeds[3].astype(bf16), grad_normeds)
        marks = (grad_tokens, first_sum)
        heads_part = after(heads_part, first_sum, second_sum)
    else:
        marks = (grad_tokens, grad_tokens)
    heads_sum = jnp.sum(heads_part.astype(f32), axis=0).astype(bf16)
    heads_part = lax.all_to_all(
        jnp.concatenate(
            [
                heads_sum[:all_rows].T.reshape(chain, shard, all_rows),
                gate_up_scattered.reshape(chain, shard, 2 * ff_own),
            ],
            axis=2,
        ),
        ("chip", "core"),
        0,
        0,
        tiled=True,
    )
    gate_up_part = heads_part[:, :, all_rows:]
    heads_part = heads_part[:, :, :all_rows]
    context_part = after(context_part, *marks)
    context_part = chip_sums(
        [
            lax.dynamic_index_in_dim(context_part, chip ^ step, 0, keepdims=False)
            for step in range(chips)
        ]
    ).astype(bf16)
    if chips == 4:
        grad_normed = side_sums(grad_normeds[0], first_sum, second_sum, heads_sum)
    else:
        grad_normed = chip_sums(grad_normeds)
    grad_tokens_one = norm_back(grad_normed, tokens_wide, inverse_rms(tokens_wide), gain_one)
    grad_inputs = (grad_middle + grad_tokens_one).astype(bf16)
    marks = (*marks, heads_sum, grad_normed, heads_part)

    def own_rows(part):
        mine = lax.dynamic_slice_in_dim(part, core * shard, shard, 0)
        other = core_swap(lax.dynamic_slice_in_dim(part, (1 - core) * shard, shard, 0))
        return mine, other

    mine, other = own_rows(context_part)
    persist_part = (mine.astype(f32) + other.astype(f32))[:, 2 * half : 2 * half + NP]
    by_side = by_core(core, mine[None], other[None])
    grad_keys_own, grad_values_own, grad_queries_own, grad_rates_own, gain_one_part = (
        unpack_weights(
            chips,
            heads,
            heads_part,
            by_side,
            key_weight,
            value_weight,
            query_weight,
            rate_weight,
            attn_gain[:, None],
        )
    )
    gate_part, up_part, gain_two_part = unpack_columns(
        gate_up_part, gate_weight, up_weight, ffn_gain[:, None]
    )
    parts = grad_output_w.reshape(groups, chips, shard, D)
    output_part = chip_sums(
        [
            lax.dynamic_index_in_dim(parts, chip ^ step, 1, keepdims=False)
            for step in range(chips)
        ]
    ).astype(bf16)
    output_part = lax.psum_scatter(
        output_part.reshape(groups * shard, D), "dp", scatter_dimension=0, tiled=True
    )
    if near and MH == D // groups:
        mem_sum = heads_sum[all_rows:]
        mem_sum = jnp.concatenate([mem_sum[: 2 * shard], mem_sum[2 * shard :]], axis=1)
        mine, other = own_rows(mem_sum)
        mem_part = mine.astype(f32) + other.astype(f32)
    elif near:
        spread = jnp.zeros((groups, 2 * shard, 2 * MH), bf16)
        spread = lax.dynamic_update_slice_in_dim(
            spread, grad_mem.reshape(heads, 2 * shard, 2 * MH), core * heads, 0
        )
        mem_line = lax.all_to_all(spread, "dp", 0, 0, tiled=True)
        mine, other = own_rows(jnp.sum(mem_line.astype(f32), axis=0).astype(bf16))
        mem_part = mine.astype(f32) + other.astype(f32)
    else:
        spread = jnp.zeros((heads, chips, HD, 2 * MH), bf16)
        spread = lax.dynamic_update_slice_in_dim(
            spread, grad_mem.reshape(heads, 1, HD, 2 * MH), chip, 1
        ).reshape(half, 2 * MH)
        spread = lax.dynamic_update_slice_in_dim(
            jnp.zeros((D, 2 * MH), bf16), spread, core * half, 0
        )
        mem_part = lax.psum_scatter(
            spread, ("dp", "chip", "core"), scatter_dimension=0, tiled=True
        ).astype(f32)
    scalar_sums = jnp.sum(grad_scalars, axis=1)[: 2 * heads].reshape(1, heads, 1, 2)
    spots = lax.dynamic_update_slice(
        jnp.zeros((core_count, heads, chips, 2), f32), scalar_sums, (core, 0, chip, 0)
    )
    sums = sum_everywhere(spots.reshape(H, 2), marks)
    grad_decay = sums[:, 0] * decay * (1.0 - decay)
    grad_momentum = sums[:, 1] * momentum * (1.0 - momentum)
    output_own = lax.ppermute(
        output_part, ("dp", "chip", "core"), [(d, s) for s, d in out_order]
    ).astype(f32)
    return (
        result[None],
        grad_inputs[None],
        gain_one_part[:, 0],
        grad_queries_own,
        grad_keys_own,
        grad_values_own,
        output_own,
        persist_part,
        mem_part[:, :MH],
        mem_part[:, MH:],
        grad_rates_own,
        grad_decay,
        grad_momentum,
        gain_two_part[:, 0],
        gate_part,
        up_part,
        down_part,
    )


def solution(mesh):
    split = jax.sharding.Mesh(
        mesh.devices.reshape(mesh.shape["dp"], mesh.shape["seq"] // 2, 2), ("dp", "chip", "core")
    )
    row = P("dp", ("chip", "core"), None)
    vector = P(("dp", "chip", "core"))
    matrix = P(("dp", "chip", "core"), None)
    in_specs = (
        row,
        P("dp", None),
        vector,
        matrix,
        matrix,
        matrix,
        matrix,
        matrix,
        matrix,
        matrix,
        matrix,
        P(),
        P(),
        vector,
        matrix,
        matrix,
        matrix,
        row,
    )
    out_specs = (
        row,
        row,
        vector,
        matrix,
        matrix,
        matrix,
        matrix,
        matrix,
        matrix,
        matrix,
        matrix,
        P(),
        P(),
        vector,
        matrix,
        matrix,
        matrix,
    )
    return jax.shard_map(
        on_device, mesh=split, in_specs=in_specs, out_specs=out_specs, check_vma=False
    )
```

```python
import jax
import jax.numpy as jnp
from jax import lax
from jax.experimental import pallas as pl
from jax.experimental.pallas import tpu as pltpu
from jax.sharding import PartitionSpec as P

D = 1536
H = 16
HD = 96
MH = 384
NP = 64
GROUP = 512
RATE_ROWS = 16
RATE_SCALE = 2.0 / 384
norm_epsilon = 1e-06
f32 = jnp.float32
bf16 = jnp.bfloat16


def dot_nn(left, right):
    return lax.dot_general(left, right, (((1,), (0,)), ((), ())), preferred_element_type=f32)


def dot_tn(left, right):
    return lax.dot_general(left, right, (((0,), (0,)), ((), ())), preferred_element_type=f32)


def dot_nt(left, right):
    return lax.dot_general(left, right, (((1,), (1,)), ((), ())), preferred_element_type=f32)


def inverse_root(values):
    return lax.rsqrt(jnp.mean(values * values, axis=0, keepdims=True) + norm_epsilon)


def spot(heads, head, which):
    at = 2 * head + which if which < 2 else 2 * heads + head
    return slice(at * HD, (at + 1) * HD)


def memory_forward_kernel(
    heads,
    blocks,
    flags,
    main_ref,
    retain_ref,
    update_ref,
    first_ref,
    second_ref,
    scalars_ref,
    recalled_ref,
    saved_ref,
    state,
):
    turn = pl.program_id(0)

    @pl.when(turn == 0)
    def blank():
        state[...] = jnp.zeros_like(state)

    saved_ref[0] = state[...]
    retain = retain_ref[0]

    def recall_with(first, second, head):
        rows = slice(head * HD, (head + 1) * HD)
        raw = main_ref[spot(heads, head, 2), :].astype(f32)
        probes = (raw * inverse_root(raw)).astype(bf16)
        inner = dot_tn(first[rows, :].astype(bf16), probes)
        return dot_nn(second[rows, :].astype(bf16), jax.nn.silu(inner).astype(bf16))

    only_state = flags[1, turn] * (1 - flags[2, turn])
    only_init = flags[2, turn] * (1 - flags[1, turn])

    @pl.when(only_state == 1)
    def from_state():
        for head in range(heads):
            recalled_ref[0, head * HD : (head + 1) * HD, :] = recall_with(
                state[0], state[1], head
            ).astype(bf16)

    @pl.when(only_init == 1)
    def from_init():
        for head in range(heads):
            recalled_ref[0, head * HD : (head + 1) * HD, :] = recall_with(
                first_ref[...], second_ref[...], head
            ).astype(bf16)

    @pl.when(only_state + only_init == 0)
    def from_both():
        for head in range(heads):
            recalled_ref[0, head * HD : (head + 1) * HD, :] = (
                retain * recall_with(state[0], state[1], head)
                + (1.0 - retain) * recall_with(first_ref[...], second_ref[...], head)
            ).astype(bf16)

    @pl.when(turn < blocks - 1)
    def step():
        carry = flags[0, turn].astype(f32)
        for head in range(heads):
            rows = slice(head * HD, (head + 1) * HD)
            keep = scalars_ref[0, head]
            push = scalars_ref[1, head] * carry
            base_first = jnp.where(carry > 0.5, state[0, rows, :], first_ref[rows, :])
            base_second = jnp.where(carry > 0.5, state[1, rows, :], second_ref[rows, :])
            raw = main_ref[spot(heads, head, 0), :].astype(f32)
            keys = (raw * inverse_root(raw)).astype(bf16)
            second_low = base_second.astype(bf16)
            inner = dot_tn(base_first.astype(bf16), keys)
            gate = jax.nn.sigmoid(inner)
            active = inner * gate
            slope = gate + active * (1.0 - gate)
            active_low = active.astype(bf16)
            at = 3 * heads * HD + head
            rate = RATE_SCALE * jax.nn.sigmoid(main_ref[at : at + 1, :].astype(f32))
            weight = rate * update_ref[0] * (1.0 / GROUP)
            error = dot_nn(second_low, active_low) - main_ref[spot(heads, head, 1), :].astype(f32)
            pull = (error * weight).astype(bf16)
            inner_pull = (dot_tn(second_low, pull) * slope).astype(bf16)
            speed_first = push * state[2, rows, :] - dot_nt(keys, inner_pull)
            speed_second = push * state[3, rows, :] - dot_nt(pull, active_low)
            state[0, rows, :] = keep * base_first + speed_first
            state[1, rows, :] = keep * base_second + speed_second
            state[2, rows, :] = speed_first
            state[3, rows, :] = speed_second


def memory_forward(flags, main, retain, update, first, second, scalars, chips):
    rows = (main.shape[0] - RATE_ROWS) // 3
    heads = rows // HD
    width = main.shape[1] // chips
    blocks = main.shape[1] // GROUP
    per = width // GROUP

    def block(turn, flags):
        return (0, ((turn // per) ^ flags[4, 0]) * per + ((turn % per) ^ flags[3, 0]))

    def by_chip(turn, flags):
        return (turn // per, 0, turn % per)

    def by_turn(turn, flags):
        return (turn, 0, 0)

    def whole(turn, flags):
        return (0, 0)

    line = pl.BlockSpec((1, 1, GROUP), by_turn)
    return pl.pallas_call(
        lambda *refs: memory_forward_kernel(heads, blocks, *refs),
        grid_spec=pltpu.PrefetchScalarGridSpec(
            num_scalar_prefetch=1,
            grid=(blocks,),
            in_specs=[
                pl.BlockSpec((3 * rows + RATE_ROWS, GROUP), block),
                line,
                line,
                pl.BlockSpec((rows, MH), whole),
                pl.BlockSpec((rows, MH), whole),
                pl.BlockSpec(memory_space=pltpu.SMEM),
            ],
            out_specs=[
                pl.BlockSpec((1, rows, GROUP), by_chip),
                pl.BlockSpec((1, 4, rows, MH), lambda turn, flags: (turn, 0, 0, 0)),
            ],
            scratch_shapes=[pltpu.VMEM((4, rows, MH), f32)],
        ),
        out_shape=[
            jax.ShapeDtypeStruct((chips, rows, width), bf16),
            jax.ShapeDtypeStruct((blocks, 4, rows, MH), f32),
        ],
        compiler_params=pltpu.CompilerParams(vmem_limit_bytes=50 * 2**20),
        cost_estimate=pl.CostEstimate(
            flops=blocks * heads * 7 * 2 * GROUP * HD * MH * 4,
            bytes_accessed=blocks * 6 * rows * MH * 4,
            transcendentals=blocks * heads * 2 * MH * GROUP,
        ),
    )(flags, main, retain, update, first, second, scalars)


def memory_backward_kernel(
    heads,
    blocks,
    flags,
    main_ref,
    retain_ref,
    update_ref,
    first_ref,
    second_ref,
    scalars_ref,
    saved_ref,
    pull_ref,
    grads_ref,
    grad_first_ref,
    grad_second_ref,
    grad_scalars_ref,
    message,
):
    count = pl.program_id(0)
    turn = blocks - 1 - count

    @pl.when(count == 0)
    def blank():
        message[...] = jnp.zeros_like(message)
        grad_first_ref[...] = jnp.zeros_like(grad_first_ref)
        grad_second_ref[...] = jnp.zeros_like(grad_second_ref)
        grad_scalars_ref[...] = jnp.zeros_like(grad_scalars_ref)

    rate_row = 3 * heads * HD

    @pl.when(count == 0)
    def last():
        for head in range(heads):
            grads_ref[spot(heads, head, 0), :] = jnp.zeros((HD, GROUP), bf16)
            grads_ref[spot(heads, head, 1), :] = jnp.zeros((HD, GROUP), bf16)
        grads_ref[rate_row:, :] = jnp.zeros((RATE_ROWS, GROUP), bf16)

    @pl.when(count > 0)
    def step():
        carry = flags[0, turn].astype(f32)
        grad_rates = []
        for head in range(heads):
            rows = slice(head * HD, (head + 1) * HD)
            keep = scalars_ref[0, head]
            push = scalars_ref[1, head] * carry
            base_first = jnp.where(carry > 0.5, saved_ref[0, 0, rows, :], first_ref[rows, :])
            base_second = jnp.where(carry > 0.5, saved_ref[0, 1, rows, :], second_ref[rows, :])
            grad_a = message[0, rows, :]
            grad_b = message[1, rows, :]
            grad_sa = message[2, rows, :] + grad_a
            grad_sb = message[3, rows, :] + grad_b
            momentum_part = carry * (
                jnp.sum(saved_ref[0, 2, rows, :] * grad_sa, axis=0, keepdims=True)
                + jnp.sum(saved_ref[0, 3, rows, :] * grad_sb, axis=0, keepdims=True)
            )
            decay_part = -(
                jnp.sum(base_first * grad_a, axis=0, keepdims=True)
                + jnp.sum(base_second * grad_b, axis=0, keepdims=True)
            )
            grad_scalars_ref[2 * head : 2 * head + 1, :] += decay_part
            grad_scalars_ref[2 * head + 1 : 2 * head + 2, :] += momentum_part
            back_a = (-grad_sa).astype(bf16)
            back_b = (-grad_sb).astype(bf16)
            raw = main_ref[spot(heads, head, 0), :].astype(f32)
            inverse = inverse_root(raw)
            normal = raw * inverse
            keys = normal.astype(bf16)
            first_low = base_first.astype(bf16)
            second_low = base_second.astype(bf16)
            inner = dot_tn(first_low, keys)
            gate = jax.nn.sigmoid(inner)
            active = inner * gate
            slope = gate + active * (1.0 - gate)
            bend = gate * (1.0 - gate) * (2.0 + inner - 2.0 * active)
            active_low = active.astype(bf16)
            weight = update_ref[0] * (1.0 / GROUP)
            at = rate_row + head
            rate_sigmoid = jax.nn.sigmoid(main_ref[at : at + 1, :].astype(f32))
            rate = RATE_SCALE * rate_sigmoid
            error = dot_nn(second_low, active_low) - main_ref[spot(heads, head, 1), :].astype(f32)
            pull = (error * (rate * weight)).astype(bf16)
            spread = dot_tn(second_low, pull)
            inner_pull = (spread * slope).astype(bf16)
            back_inner = dot_tn(back_a, keys)
            back_spread = (back_inner * slope).astype(bf16)
            grad_pull = dot_nn(back_b, active_low) + dot_nn(second_low, back_spread)
            grad_rates.append(
                jnp.sum(grad_pull * error, axis=0, keepdims=True)
                * weight
                * rate
                * (1.0 - rate_sigmoid)
            )
            grad_error = grad_pull * (rate * weight)
            grad_error_low = grad_error.astype(bf16)
            grads_ref[spot(heads, head, 1), :] = (-grad_error).astype(bf16)
            grad_active = dot_tn(back_b, pull) + dot_tn(second_low, grad_error_low)
            grad_inner = (back_inner * spread * bend + grad_active * slope).astype(bf16)
            grad_normal = dot_nn(back_a, inner_pull) + dot_nn(first_low, grad_inner)
            grads_ref[spot(heads, head, 0), :] = (
                inverse
                * (grad_normal - normal * jnp.mean(grad_normal * normal, axis=0, keepdims=True))
            ).astype(bf16)
            base_grad_a = keep * grad_a + dot_nt(keys, grad_inner)
            base_grad_b = (
                keep * grad_b + dot_nt(pull, back_spread) + dot_nt(grad_error_low, active_low)
            )
            message[0, rows, :] = carry * base_grad_a
            message[1, rows, :] = carry * base_grad_b
            message[2, rows, :] = push * grad_sa
            message[3, rows, :] = push * grad_sb
            grad_first_ref[rows, :] += (1.0 - carry) * base_grad_a
            grad_second_ref[rows, :] += (1.0 - carry) * base_grad_b
        grad_rates.append(jnp.zeros((RATE_ROWS - heads, GROUP), f32))
        grads_ref[rate_row:, :] = jnp.concatenate(
            grad_rates, axis=0
        ).astype(bf16)

    retain = retain_ref[0]

    def recall_back(first, second, grad_recalled, head):
        rows = slice(head * HD, (head + 1) * HD)
        raw = main_ref[spot(heads, head, 2), :].astype(f32)
        inverse = inverse_root(raw)
        normal = raw * inverse
        probes = normal.astype(bf16)
        first_low = first[rows, :].astype(bf16)
        inner = dot_tn(first_low, probes)
        gate = jax.nn.sigmoid(inner)
        active = inner * gate
        slope = gate + active * (1.0 - gate)
        grad_inner = (dot_tn(second[rows, :].astype(bf16), grad_recalled) * slope).astype(bf16)
        grad_second = dot_nt(grad_recalled, active.astype(bf16))
        grad_first = dot_nt(probes, grad_inner)
        grad_normal = dot_nn(first_low, grad_inner)
        grad_probes = inverse * (
            grad_normal - normal * jnp.mean(grad_normal * normal, axis=0, keepdims=True)
        )
        return grad_first, grad_second, grad_probes

    only_state = flags[1, turn] * (1 - flags[2, turn])
    only_init = flags[2, turn] * (1 - flags[1, turn])

    def from_state(whole):
        for head in range(heads):
            rows = slice(head * HD, (head + 1) * HD)
            grad_recalled = pull_ref[0, rows, :]
            if not whole:
                grad_recalled = (grad_recalled.astype(f32) * retain).astype(bf16)
            grad_first, grad_second, grad_probes = recall_back(
                saved_ref[0, 0], saved_ref[0, 1], grad_recalled, head
            )
            message[0, rows, :] += grad_first
            message[1, rows, :] += grad_second
            grads_ref[spot(heads, head, 2), :] = grad_probes.astype(bf16)

    def from_init(whole):
        for head in range(heads):
            rows = slice(head * HD, (head + 1) * HD)
            grad_recalled = pull_ref[0, rows, :]
            if not whole:
                grad_recalled = (grad_recalled.astype(f32) * (1.0 - retain)).astype(bf16)
            grad_first, grad_second, grad_probes = recall_back(
                first_ref[...], second_ref[...], grad_recalled, head
            )
            grad_first_ref[rows, :] += grad_first
            grad_second_ref[rows, :] += grad_second
            if not whole:
                grad_probes = grad_probes + grads_ref[spot(heads, head, 2), :].astype(f32)
            grads_ref[spot(heads, head, 2), :] = grad_probes.astype(bf16)

    @pl.when(only_state == 1)
    def state_alone():
        from_state(True)

    @pl.when(only_init == 1)
    def init_alone():
        from_init(True)

    @pl.when(only_state + only_init == 0)
    def both():
        from_state(False)
        from_init(False)


def memory_backward(
    flags, main, retain, update, first, second, scalars, saved, pull
):
    chips, rows, width = pull.shape
    heads = rows // HD
    blocks = chips * width // GROUP
    per = width // GROUP
    all_rows = 3 * rows + RATE_ROWS

    def block(count, flags):
        turn = blocks - 1 - count
        return (0, ((turn // per) ^ flags[4, 0]) * per + ((turn % per) ^ flags[3, 0]))

    def by_chip(count, flags):
        turn = blocks - 1 - count
        return (turn // per, 0, turn % per)

    def by_turn(count, flags):
        return (blocks - 1 - count, 0, 0)

    def whole(count, flags):
        return (0, 0)

    line = pl.BlockSpec((1, 1, GROUP), by_turn)
    matrix = pl.BlockSpec((rows, MH), whole)
    return pl.pallas_call(
        lambda *refs: memory_backward_kernel(heads, blocks, *refs),
        grid_spec=pltpu.PrefetchScalarGridSpec(
            num_scalar_prefetch=1,
            grid=(blocks,),
            in_specs=[
                pl.BlockSpec((3 * rows + RATE_ROWS, GROUP), block),
                line,
                line,
                matrix,
                matrix,
                pl.BlockSpec(memory_space=pltpu.SMEM),
                pl.BlockSpec(
                    (1, 4, rows, MH), lambda count, flags: (blocks - 1 - count, 0, 0, 0)
                ),
                pl.BlockSpec((1, rows, GROUP), by_chip),
            ],
            out_specs=[
                pl.BlockSpec((all_rows, GROUP), block),
                matrix,
                matrix,
                pl.BlockSpec((8, MH), whole),
            ],
            scratch_shapes=[pltpu.VMEM((4, rows, MH), f32)],
        ),
        out_shape=[
            jax.ShapeDtypeStruct((all_rows, chips * width), bf16),
            jax.ShapeDtypeStruct((rows, MH), f32),
            jax.ShapeDtypeStruct((rows, MH), f32),
            jax.ShapeDtypeStruct((8, MH), f32),
        ],
        compiler_params=pltpu.CompilerParams(vmem_limit_bytes=56 * 2**20),
        cost_estimate=pl.CostEstimate(
            flops=blocks * heads * 19 * 2 * GROUP * HD * MH * 4,
            bytes_accessed=blocks * 8 * rows * MH * 4,
            transcendentals=blocks * heads * 2 * MH * GROUP,
        ),
    )(flags, main, retain, update, first, second, scalars, saved, pull)


QUERIES = 256


def visible_bias(bias_ref, row_ref, col_ref):
    shape = bias_ref.shape[1:]
    key = lax.broadcasted_iota(jnp.int32, shape, 0)
    query = lax.broadcasted_iota(jnp.int32, shape, 1)
    for block in range(bias_ref.shape[0]):
        seen = jnp.logical_and(key <= query, col_ref[block] == row_ref[block])
        bias_ref[block] = jnp.where(seen, 0.0, -1e30)


def attention_forward_kernel(
    scale, core, low_ref, query_ref, far_ref, side_ref, row_ref, col_ref, mixed_ref, total_ref, bias_ref
):
    @pl.when(jnp.logical_and(pl.program_id(0) == 0, pl.program_id(1) == 0))
    def fill():
        visible_bias(bias_ref, row_ref, col_ref)

    block = pl.program_id(1)
    for part in range(GROUP // QUERIES):
        lanes = slice(part * QUERIES, (part + 1) * QUERIES)
        upto = (part + 1) * QUERIES
        query = query_ref[:, lanes]
        bias = bias_ref[block, :upto, lanes]
        s_p = dot_tn(side_ref[:HD], query) * scale
        s_r = dot_tn(far_ref[:HD, :upto], query) * scale + bias
        s_l = dot_tn(low_ref[:HD, :upto], query) * scale + bias
        top = jnp.maximum(
            jnp.max(s_p, axis=0, keepdims=True),
            jnp.maximum(
                jnp.max(s_r, axis=0, keepdims=True), jnp.max(s_l, axis=0, keepdims=True)
            ),
        )
        e_p = jnp.exp(s_p - top)
        e_r = jnp.exp(s_r - top)
        e_l = jnp.exp(s_l - top)
        total = (
            jnp.sum(e_p, axis=0, keepdims=True)
            + jnp.sum(e_r, axis=0, keepdims=True)
            + jnp.sum(e_l, axis=0, keepdims=True)
        )
        mixed = (
            dot_nn(side_ref[HD:], e_p.astype(bf16))
            + dot_nn(far_ref[HD:, :upto], e_r.astype(bf16))
            + dot_nn(low_ref[HD:, :upto], e_l.astype(bf16))
        )
        mixed_ref[:, lanes] = (mixed / total).astype(bf16)
        total_ref[0, :, lanes] = top + jnp.log(total)


def attention_specs(rows, width):
    count = width // GROUP
    heads = rows // HD
    low = pl.BlockSpec((2 * HD, GROUP), lambda head, block, core: (head, block))
    query = pl.BlockSpec((HD, GROUP), lambda head, block, core: (2 * heads + head, block))
    far = pl.BlockSpec((2 * HD, GROUP), lambda head, block, core: (head, block ^ core[0]))
    side = pl.BlockSpec((2 * HD, NP), lambda head, block, core: (head, 0))
    row = pl.BlockSpec((count, 1, GROUP), lambda head, block, core: (0, 0, 0))
    col = pl.BlockSpec((count, GROUP, 1), lambda head, block, core: (0, 0, 0))
    main = pl.BlockSpec((HD, GROUP), lambda head, block, core: (head, block))
    line = pl.BlockSpec((1, 1, GROUP), lambda head, block, core: (head, 0, block))
    return low, query, far, side, row, col, main, line


def attention_forward(scale, core, low, far, side, row, col):
    rows, width = low.shape[0] // 3, low.shape[1]
    low_spec, query_spec, far_spec, side_spec, row_spec, col_spec, main, line = attention_specs(
        rows, width
    )
    heads, count = rows // HD, width // GROUP
    return pl.pallas_call(
        lambda *refs: attention_forward_kernel(scale, *refs),
        grid_spec=pltpu.PrefetchScalarGridSpec(
            num_scalar_prefetch=1,
            grid=(heads, count),
            in_specs=[low_spec, query_spec, far_spec, side_spec, row_spec, col_spec],
            out_specs=[main, line],
            scratch_shapes=[pltpu.VMEM((count, GROUP, GROUP), f32)],
        ),
        out_shape=[
            jax.ShapeDtypeStruct((rows, width), bf16),
            jax.ShapeDtypeStruct((heads, 1, width), f32),
        ],
        compiler_params=pltpu.CompilerParams(vmem_limit_bytes=50 * 2**20),
        cost_estimate=pl.CostEstimate(
            flops=heads * count * 4 * GROUP * 1088 * HD * 4,
            bytes_accessed=6 * rows * width * 2,
            transcendentals=heads * count * GROUP * 1088,
        ),
    )(core, low, low, far, side, row, col)


def attention_backward_kernel(
    scale,
    core,
    low_ref,
    query_ref,
    far_ref,
    side_ref,
    row_ref,
    col_ref,
    mixed_ref,
    total_ref,
    grad_ref,
    grads_ref,
    grad_far_ref,
    grad_side_ref,
    bias_ref,
):
    @pl.when(jnp.logical_and(pl.program_id(0) == 0, pl.program_id(1) == 0))
    def fill():
        visible_bias(bias_ref, row_ref, col_ref)

    block = pl.program_id(1)

    @pl.when(block == 0)
    def blank():
        grad_side_ref[...] = jnp.zeros_like(grad_side_ref)

    parts = GROUP // QUERIES
    sums = {}
    for part in reversed(range(parts)):
        lanes = slice(part * QUERIES, (part + 1) * QUERIES)
        upto = (part + 1) * QUERIES
        query = query_ref[:, lanes]
        grad = grad_ref[:, lanes]
        bias = bias_ref[block, :upto, lanes] - total_ref[0, :, lanes]
        mean = jnp.sum(
            grad.astype(f32) * mixed_ref[:, lanes].astype(f32), axis=0, keepdims=True
        )
        grad_query = jnp.zeros((HD, QUERIES), f32)
        for name, keys, values, extra in (
            ("p", side_ref[:HD], side_ref[HD:], -total_ref[0, :, lanes]),
            ("r", far_ref[:HD, :upto], far_ref[HD:, :upto], bias),
            ("l", low_ref[:HD, :upto], low_ref[HD:, :upto], bias),
        ):
            chances = jnp.exp(dot_tn(keys, query) * scale + extra)
            slope = (chances * (dot_tn(values, grad) - mean)).astype(bf16)
            grad_query += dot_nn(keys, slope)
            grad_keys = dot_nt(query, slope)
            grad_values = dot_nt(grad, chances.astype(bf16))
            if name in sums:
                old_keys, old_values = sums[name]
                if name == "p":
                    sums[name] = (old_keys + grad_keys, old_values + grad_values)
                else:
                    sums[name] = (
                        jnp.concatenate([old_keys[:, :upto] + grad_keys, old_keys[:, upto:]], axis=1),
                        jnp.concatenate(
                            [old_values[:, :upto] + grad_values, old_values[:, upto:]], axis=1
                        ),
                    )
            else:
                sums[name] = (grad_keys, grad_values)
        grads_ref[2 * HD :, lanes] = (grad_query * scale).astype(bf16)
    grad_side_ref[:HD] += sums["p"][0] * scale
    grad_side_ref[HD:] += sums["p"][1]
    grad_far_ref[:HD] = (sums["r"][0] * scale).astype(bf16)
    grad_far_ref[HD:] = sums["r"][1].astype(bf16)
    grads_ref[:HD] = (sums["l"][0] * scale).astype(bf16)
    grads_ref[HD : 2 * HD] = sums["l"][1].astype(bf16)


def attention_backward(scale, core, low, far, side, row, col, mixed, total, grad):
    rows, width = low.shape[0] // 3, low.shape[1]
    low_spec, query_spec, far_spec, side_spec, row_spec, col_spec, main, line = attention_specs(
        rows, width
    )
    heads, count = rows // HD, width // GROUP
    return pl.pallas_call(
        lambda *refs: attention_backward_kernel(scale, *refs),
        grid_spec=pltpu.PrefetchScalarGridSpec(
            num_scalar_prefetch=1,
            grid=(heads, count),
            in_specs=[
                low_spec,
                query_spec,
                far_spec,
                side_spec,
                row_spec,
                col_spec,
                main,
                line,
                main,
            ],
            out_specs=[
                pl.BlockSpec((3 * HD, GROUP), lambda head, block, core: (head, block)),
                far_spec,
                side_spec,
            ],
            scratch_shapes=[pltpu.VMEM((count, GROUP, GROUP), f32)],
        ),
        out_shape=[
            jax.ShapeDtypeStruct((3 * rows, width), bf16),
            jax.ShapeDtypeStruct((2 * rows, width), bf16),
            jax.ShapeDtypeStruct((2 * rows, NP), f32),
        ],
        compiler_params=pltpu.CompilerParams(vmem_limit_bytes=50 * 2**20),
        cost_estimate=pl.CostEstimate(
            flops=heads * count * 10 * GROUP * 1088 * HD * 4,
            bytes_accessed=14 * rows * width * 2,
            transcendentals=heads * count * GROUP * 1088,
        ),
    )(core, low, low, far, side, row, col, mixed, total, grad)


def head_of(core, chip, turn, chips, heads):
    return core * chips * heads + turn * chips + chip


def pack_weights(chips, heads, key, value, query, rate, gains, side):
    shard = key.shape[0]

    def kernel(key_ref, value_ref, query_ref, rate_ref, gains_ref, side_ref, out_ref):
        for core in range(2):
            order = [
                head_of(core, chip, turn, chips, heads)
                for chip in range(chips)
                for turn in range(heads)
            ]
            end = 3 * D // 2
            out_ref[core, :, end:] = jnp.zeros((shard, 128), bf16)
            out_ref[core, :, end : end + NP] = side_ref[...]
            out_ref[core, :, end + NP : end + NP + 2] = gains_ref[...]
            for at, head in enumerate(order):
                columns = slice(head * HD, (head + 1) * HD)
                low = 2 * at * HD
                out_ref[core, :, low : low + HD] = key_ref[:, columns]
                out_ref[core, :, low + HD : low + 2 * HD] = value_ref[:, columns]
                low = D + at * HD
                out_ref[core, :, low : low + HD] = query_ref[:, columns]
                low = end + NP + 2 + at
                out_ref[core, :, low : low + 1] = rate_ref[:, head : head + 1]

    return pl.pallas_call(
        kernel, out_shape=jax.ShapeDtypeStruct((2, shard, 3 * D // 2 + 128), bf16)
    )(key, value, query, rate, gains, side)


def pack_columns(chain, gate, up):
    shard, whole = gate.shape
    own = whole // chain

    def kernel(gate_ref, up_ref, out_ref):
        groups = out_ref.shape[2] // (2 * size)
        for place in range(chain):
            for which, ref in enumerate((gate_ref, up_ref)):
                for group in range(groups):
                    at = which * own + group * size
                    start = (group * chain + place) * size
                    out_ref[place, :, at : at + size] = ref[:, start : start + size]

    size = whole // (D // shard)
    return pl.pallas_call(
        kernel, out_shape=jax.ShapeDtypeStruct((chain, shard, 2 * own), bf16)
    )(gate, up)


def unpack_columns(parts, gate, up, gain):
    chain, shard, both = parts.shape
    own = both // 2
    whole = gate.shape[1]
    size = whole // (D // shard)

    def kernel(parts_ref, gate_ref, up_ref, gain_ref, gate_out, up_out, gain_out):
        total = jnp.zeros((shard, 1), f32)
        for which, (ref, out) in enumerate(((gate_ref, gate_out), (up_ref, up_out))):
            for place in range(chain):
                for group in range(own // size):
                    at = which * own + group * size
                    start = (group * chain + place) * size
                    out[:, start : start + size] = parts_ref[place, :, at : at + size].astype(f32)
            total += jnp.sum(out[...] * ref[...].astype(f32), axis=1, keepdims=True)
        gain_out[...] = total / gain_ref[...].astype(f32)

    return pl.pallas_call(
        kernel,
        out_shape=[
            jax.ShapeDtypeStruct((shard, whole), f32),
            jax.ShapeDtypeStruct((shard, whole), f32),
            jax.ShapeDtypeStruct((shard, 1), f32),
        ],
    )(parts, gate, up, gain)


def unpack_weights(chips, heads, parts, context, key, value, query, rate, gain):
    shard = key.shape[0]

    def kernel(parts_ref, context_ref, key_ref, value_ref, query_ref, rate_ref, gain_ref, *outs):
        key_out, value_out, query_out, rate_out, gain_out = outs
        total = jnp.zeros((shard, 1), f32)
        for core in range(2):
            for chip in range(chips):
                place = chip * 2 + core
                for turn in range(heads):
                    head = head_of(core, chip, turn, chips, heads)
                    rate_out[:, head : head + 1] = parts_ref[
                        place, :, 3 * heads * HD + turn : 3 * heads * HD + turn + 1
                    ].astype(f32)
                    columns = slice(head * HD, (head + 1) * HD)
                    for which, (weight, out) in enumerate(
                        ((key_ref, key_out), (value_ref, value_out), (query_ref, query_out))
                    ):
                        grad = parts_ref[place, :, spot(heads, turn, which)].astype(f32)
                        total += jnp.sum(
                            grad * weight[:, columns].astype(f32), axis=1, keepdims=True
                        )
                        if which < 2:
                            near = (2 * (chip * heads + turn) + which) * HD
                            grad += context_ref[core, :, near : near + HD].astype(f32)
                        out[:, columns] = grad
        total += jnp.sum(rate_out[...] * rate_ref[...].astype(f32), axis=1, keepdims=True)
        gain_out[...] = total / gain_ref[...].astype(f32)

    wide = jax.ShapeDtypeStruct((shard, D), f32)
    return pl.pallas_call(
        kernel,
        out_shape=[
            wide,
            wide,
            wide,
            jax.ShapeDtypeStruct((shard, H), f32),
            jax.ShapeDtypeStruct((shard, 1), f32),
        ],
    )(parts, context, key, value, query, rate, gain)


def take_heads(chip, chips, heads, w_pair):
    rows = heads * HD
    size = 128
    span = 2 * rows
    tail_at = 3 * D // 2 // 128

    def kernel(chip_ref, low_ref, query_ref, tail_ref, out_ref, gains_ref):
        def turned(value):
            return value.astype(f32).T

        out_ref[:span] = turned(low_ref[...]).astype(bf16)
        query = turned(query_ref[...])
        odd = chip_ref[0] % 2 == 1
        out_ref[span : span + rows] = jnp.where(odd, query[rows:], query[:rows]).astype(bf16)
        tail = turned(tail_ref[...])
        gains_ref[...] = tail[NP : NP + 8]
        rates = jnp.zeros((heads, size), f32)
        for at in range(chips):
            low = NP + 2 + at * heads
            rates = jnp.where(chip_ref[0] == at, tail[low : low + heads], rates)
        out_ref[span + rows :] = jnp.concatenate(
            [rates, jnp.zeros((RATE_ROWS - heads, size), f32)], axis=0
        ).astype(bf16)

    return pl.pallas_call(
        kernel,
        grid_spec=pltpu.PrefetchScalarGridSpec(
            num_scalar_prefetch=1,
            grid=(D // size,),
            in_specs=[
                pl.BlockSpec((size, span), lambda at, chip_ref: (at, chip_ref[0])),
                pl.BlockSpec((size, span), lambda at, chip_ref: (at, chips + chip_ref[0] // 2)),
                pl.BlockSpec((size, 128), lambda at, chip_ref: (at, tail_at)),
            ],
            out_specs=[
                pl.BlockSpec((span + rows + RATE_ROWS, size), lambda at, chip_ref: (0, at)),
                pl.BlockSpec((8, size), lambda at, chip_ref: (0, at)),
            ],
        ),
        out_shape=[
            jax.ShapeDtypeStruct((span + rows + RATE_ROWS, D), bf16),
            jax.ShapeDtypeStruct((8, D), f32),
        ],
    )(chip, w_pair, w_pair, w_pair)


def project_blocks(first, blocks, tokens, gain, weight, old=()):
    columns = weight.shape[0]
    count = len(tokens)

    def kernel(*refs):
        gain_ref, weight_ref = refs[count : count + 2]
        normed_ref, main_ref = refs[-2:]
        for at in range(count):

            @pl.when(pl.program_id(0) == at)
            def one(tokens_ref=refs[at]):
                wide = tokens_ref[...].astype(f32)
                scale = lax.rsqrt(jnp.mean(wide * wide, axis=1, keepdims=True) + norm_epsilon)
                low = (wide * scale * gain_ref[...]).astype(bf16)
                normed_ref[...] = low
                main_ref[...] = dot_nt(weight_ref[...], low).astype(bf16)

    return pl.pallas_call(
        kernel,
        grid=(count,),
        in_specs=[pl.BlockSpec((GROUP, D), lambda i: (0, 0))] * count
        + [
            pl.BlockSpec((1, D), lambda i: (0, 0)),
            pl.BlockSpec((columns, D), lambda i: (0, 0)),
        ]
        + [pl.BlockSpec(memory_space=pl.ANY)] * len(old),
        out_specs=[
            pl.BlockSpec((GROUP, D), lambda i: (first + i, 0)),
            pl.BlockSpec((columns, GROUP), lambda i: (0, first + i)),
        ],
        out_shape=[
            jax.ShapeDtypeStruct((blocks * GROUP, D), bf16),
            jax.ShapeDtypeStruct((columns, blocks * GROUP), bf16),
        ],
        input_output_aliases={count + 2: 0, count + 3: 1} if old else {},
        compiler_params=pltpu.CompilerParams(vmem_limit_bytes=52 * 2**20),
        cost_estimate=pl.CostEstimate(
            flops=count * 2 * GROUP * D * columns * 2,
            bytes_accessed=count * (GROUP * D * 4 + columns * GROUP * 2) + columns * D * 2,
            transcendentals=0,
        ),
    )(*tokens, gain, weight, *old)


def merge_part(heads, grads_ref, part_ref, held):
    for head in range(heads):
        for which in range(3):
            low = (3 * head + which) * HD
            there = spot(heads, head, which)
            held[there, :] = (
                grads_ref[there, :].astype(f32) + part_ref[0, low : low + HD, :].astype(f32)
            ).astype(bf16)
    end = 3 * heads * HD
    held[end:, :] = grads_ref[end:, :]


def merge_blocks(chip, groups, grads, grad_part, normed):
    columns, tokens = grads.shape
    chips, part_rows, width = grad_part.shape
    heads = part_rows // (3 * HD)
    blocks = tokens // width
    cut = D // groups

    def kernel(chip_ref, grads_ref, part_ref, normed_ref, weight_out, total, held):
        at = pl.program_id(0)
        merge_part(heads, grads_ref, part_ref, held)
        part = dot_nn(held[...], normed_ref[...])

        @pl.when(at == 0)
        def begin():
            total[...] = part

        @pl.when(at > 0)
        def more():
            total[...] += part

        @pl.when(at == blocks - 1)
        def end():
            for group in range(groups):
                weight_out[group] = total[:, group * cut : (group + 1) * cut].astype(bf16)

    return pl.pallas_call(
        kernel,
        grid_spec=pltpu.PrefetchScalarGridSpec(
            num_scalar_prefetch=1,
            grid=(blocks,),
            in_specs=[
                pl.BlockSpec((columns, width), lambda at, chip_ref: (0, at)),
                pl.BlockSpec((1, part_rows, width), lambda at, chip_ref: (at ^ chip_ref[0], 0, 0)),
                pl.BlockSpec((width, D), lambda at, chip_ref: (at, 0)),
            ],
            out_specs=pl.BlockSpec((groups, columns, cut), lambda at, chip_ref: (0, 0, 0)),
            scratch_shapes=[pltpu.VMEM((columns, D), f32), pltpu.VMEM((columns, width), bf16)],
        ),
        out_shape=jax.ShapeDtypeStruct((groups, columns, cut), bf16),
        compiler_params=pltpu.CompilerParams(vmem_limit_bytes=44 * 2**20),
        cost_estimate=pl.CostEstimate(
            flops=2 * tokens * D * columns * 2,
            bytes_accessed=tokens * (D * 2 + columns * 4),
            transcendentals=0,
        ),
    )(chip, grads, grad_part, normed)


def back_blocks(chip, first, count, grads, grad_part, weight):
    columns = grads.shape[0]
    part_rows = grad_part.shape[1]
    heads = part_rows // (3 * HD)

    def kernel(chip_ref, grads_ref, part_ref, weight_ref, own_ref, other_ref, held):
        merge_part(heads, grads_ref, part_ref, held)
        out = dot_tn(held[...], weight_ref[...]).astype(bf16)

        @pl.when(pl.program_id(0) % 2 == 0)
        def own():
            own_ref[0] = out

        @pl.when(pl.program_id(0) % 2 == 1)
        def other():
            other_ref[0] = out

    block = pl.BlockSpec((1, GROUP, D), lambda at, chip_ref: (at // 2, 0, 0))
    blocks = jax.ShapeDtypeStruct((count, GROUP, D), bf16)
    return pl.pallas_call(
        kernel,
        grid_spec=pltpu.PrefetchScalarGridSpec(
            num_scalar_prefetch=1,
            grid=(2 * count,),
            in_specs=[
                pl.BlockSpec((columns, GROUP), lambda at, chip_ref: (0, 2 * first + at)),
                pl.BlockSpec(
                    (1, part_rows, GROUP),
                    lambda at, chip_ref: ((first + at // 2) ^ chip_ref[0], 0, at % 2),
                ),
                pl.BlockSpec(
                    (columns, D), lambda at, chip_ref: (0, 0), pipeline_mode=pl.Buffered(1)
                ),
            ],
            out_specs=[block, block],
            scratch_shapes=[pltpu.VMEM((columns, GROUP), bf16)],
        ),
        out_shape=[blocks, blocks],
        compiler_params=pltpu.CompilerParams(vmem_limit_bytes=32 * 2**20),
        cost_estimate=pl.CostEstimate(
            flops=count * 4 * GROUP * D * columns * 2,
            bytes_accessed=count * 2 * GROUP * (D * 2 + columns * 4),
            transcendentals=0,
        ),
    )(chip, grads, grad_part, weight)


def ffn_chunk(place, chunks, normed, grad, w_gate_up, w_down, old=()):
    own = w_down.shape[0]
    given = [piece for block in (*normed, *grad) for piece in block]
    spans, at = [], 0
    for block in (*normed, *grad):
        spans.append(slice(at, at + len(block)))
        at += len(block)
    count = len(given)

    def kernel(*refs):
        w_gate_up_ref, w_down_ref = refs[count : count + 2]
        all_normed, all_grad, all_hidden, all_grads, out_ref, back_ref = refs[-6:]
        for at in range(2):

            @pl.when(pl.program_id(0) == at)
            def one(normed_refs=refs[spans[at]], grad_refs=refs[spans[2 + at]]):
                low = jnp.concatenate([ref[...] for ref in normed_refs], axis=0)
                grad_low = jnp.concatenate([ref[...] for ref in grad_refs], axis=0)
                all_normed[...] = low
                all_grad[...] = grad_low
                gate = dot_nn(low, w_gate_up_ref[:, :own])
                up = dot_nn(low, w_gate_up_ref[:, own:])
                gate_sigmoid = jax.nn.sigmoid(gate)
                gate_silu = gate * gate_sigmoid
                hidden = (gate_silu * up).astype(bf16)
                all_hidden[...] = hidden
                out_ref[0] = dot_nn(hidden, w_down_ref[...]).astype(bf16)
                grad_hidden = dot_nt(grad_low, w_down_ref[...])
                slope = gate_sigmoid * (1.0 + gate * (1.0 - gate_sigmoid))
                all_grads[:, :own] = (grad_hidden * up * slope).astype(bf16)
                all_grads[:, own:] = (grad_hidden * gate_silu).astype(bf16)
                back_ref[0] = dot_nt(all_grads[...], w_gate_up_ref[...]).astype(bf16)

    tokens = chunks * 2 * GROUP
    once = pl.Buffered(1)
    return pl.pallas_call(
        kernel,
        grid=(2,),
        in_specs=[
            pl.BlockSpec(piece.shape, lambda i: (0, 0), pipeline_mode=once) for piece in given
        ]
        + [
            pl.BlockSpec((D, 2 * own), lambda i: (0, 0), pipeline_mode=once),
            pl.BlockSpec((own, D), lambda i: (0, 0), pipeline_mode=once),
        ]
        + [pl.BlockSpec(memory_space=pl.ANY)] * len(old),
        out_specs=[
            pl.BlockSpec((GROUP, D), lambda i: (2 * place + i, 0)),
            pl.BlockSpec((GROUP, D), lambda i: (2 * place + i, 0)),
            pl.BlockSpec((GROUP, own), lambda i: (2 * place + i, 0)),
            pl.BlockSpec((GROUP, 2 * own), lambda i: (2 * place + i, 0)),
            pl.BlockSpec((1, GROUP, D), lambda i: (i, 0, 0)),
            pl.BlockSpec((1, GROUP, D), lambda i: (i, 0, 0)),
        ],
        out_shape=[
            jax.ShapeDtypeStruct((tokens, D), bf16),
            jax.ShapeDtypeStruct((tokens, D), bf16),
            jax.ShapeDtypeStruct((tokens, own), bf16),
            jax.ShapeDtypeStruct((tokens, 2 * own), bf16),
            jax.ShapeDtypeStruct((2, GROUP, D), bf16),
            jax.ShapeDtypeStruct((2, GROUP, D), bf16),
        ],
        input_output_aliases={count + 2 + at: at for at in range(len(old))},
        compiler_params=pltpu.CompilerParams(vmem_limit_bytes=40 * 2**20),
        cost_estimate=pl.CostEstimate(
            flops=2 * GROUP * D * own * 12, bytes_accessed=20 * GROUP * D, transcendentals=2 * GROUP * own
        ),
    )(*given, w_gate_up, w_down, *old)


def context_product(context, grad_far, persist, grad_side, w_pair):
    size = 256
    columns = grad_far.shape[0]

    def kernel(context_ref, far_ref, persist_ref, side_ref, weight_ref, out_ref):
        out_ref[:, :columns] = (
            dot_nt(context_ref[...], far_ref[...]) + dot_nt(persist_ref[...], side_ref[...])
        ).astype(bf16)
        own = dot_nn(weight_ref[...], side_ref[...]).astype(bf16)
        out_ref[:, columns:] = jnp.concatenate([own, jnp.zeros((size, 128 - NP), bf16)], axis=1)

    once = pl.Buffered(1)
    return pl.pallas_call(
        kernel,
        grid=(D // size,),
        in_specs=[
            pl.BlockSpec((size, context.shape[1]), lambda at: (at, 0)),
            pl.BlockSpec(grad_far.shape, lambda at: (0, 0), pipeline_mode=once),
            pl.BlockSpec((size, NP), lambda at: (at, 0)),
            pl.BlockSpec(grad_side.shape, lambda at: (0, 0), pipeline_mode=once),
            pl.BlockSpec((size, columns), lambda at: (at, 0)),
        ],
        out_specs=pl.BlockSpec((size, columns + 128), lambda at: (at, 0)),
        out_shape=jax.ShapeDtypeStruct((D, columns + 128), bf16),
        compiler_params=pltpu.CompilerParams(vmem_limit_bytes=32 * 2**20),
        cost_estimate=pl.CostEstimate(
            flops=2 * D * columns * context.shape[1],
            bytes_accessed=4 * D * columns * 2,
            transcendentals=0,
        ),
    )(context, grad_far, persist, grad_side, w_pair)


def tokens_product(left, right):
    tokens, rows = left.shape
    columns = right.shape[1]
    size = 2 * GROUP
    steps = tokens // size

    def kernel(left_ref, right_ref, out_ref, total):
        at = pl.program_id(0)
        part = dot_tn(left_ref[...], right_ref[...])

        @pl.when(at == 0)
        def first():
            total[...] = part

        @pl.when(at > 0)
        def more():
            total[...] += part

        @pl.when(at == steps - 1)
        def last():
            out_ref[...] = total[...].astype(bf16)

    return pl.pallas_call(
        kernel,
        grid=(steps,),
        in_specs=[
            pl.BlockSpec((size, rows), lambda at: (at, 0)),
            pl.BlockSpec((size, columns), lambda at: (at, 0)),
        ],
        out_specs=pl.BlockSpec((rows, columns), lambda at: (0, 0)),
        out_shape=jax.ShapeDtypeStruct((rows, columns), bf16),
        scratch_shapes=[pltpu.VMEM((rows, columns), f32)],
        compiler_params=pltpu.CompilerParams(vmem_limit_bytes=50 * 2**20),
        cost_estimate=pl.CostEstimate(
            flops=2 * tokens * rows * columns,
            bytes_accessed=2 * tokens * (rows + columns),
            transcendentals=0,
        ),
    )(left, right)


def matmul(left, right, left_dim, right_dim, out=f32):
    return lax.dot_general(
        left, right, (((left_dim,), (right_dim,)), ((), ())), preferred_element_type=f32
    ).astype(out)


def core_swap(value):
    return lax.ppermute(value, "core", [(0, 1), (1, 0)])


def gather_chips(value):
    return lax.all_gather(value, ("dp", "chip"), axis=0, tiled=True)


def scatter_chips(value):
    return lax.psum_scatter(value, ("dp", "chip"), scatter_dimension=0, tiled=True)


def after(value, *events):
    return lax.optimization_barrier((value, *events))[0]


def together(*values):
    return lax.optimization_barrier(values)


def chip_swap(value, step):
    count = lax.axis_size("chip")
    return lax.ppermute(value, "chip", [(index, index ^ step) for index in range(count)])


def chip_parts(value):
    count = lax.axis_size("chip")
    if count != 4:
        return [value] + [chip_swap(value, step) for step in range(1, count)]
    middle = value.shape[0] // 2
    along = chip_swap(value, 1)
    across = chip_swap(value, 2)
    corner = jnp.concatenate([chip_swap(along[:middle], 2), chip_swap(across[middle:], 1)], axis=0)
    return [value, along, across, corner]


def corner_sums(corner, parts, *events):
    middle = corner.shape[0] // 2
    from_along = chip_swap(corner[:middle], 1)
    from_across = chip_swap(corner[middle:], 2)
    if events:
        from_along, from_across = after(from_along, *events), after(from_across, *events)
    from_along, from_across = from_along.astype(f32), from_across.astype(f32)
    first = jnp.concatenate(
        [parts[1][:middle].astype(f32), parts[1][middle:].astype(f32) + from_across], axis=0
    )
    second = jnp.concatenate(
        [parts[2][:middle].astype(f32) + from_along, parts[2][middle:].astype(f32)], axis=0
    )
    return first.astype(bf16), second.astype(bf16)


def side_sums(own, first, second, *events):
    first, second = chip_swap(first, 1), chip_swap(second, 2)
    if events:
        first, second = after(first, *events), after(second, *events)
    return own.astype(f32) + first.astype(f32) + second.astype(f32)


def chip_sums(parts):
    count = lax.axis_size("chip")
    if count != 4:
        total = parts[0].astype(f32)
        for step in range(1, count):
            total = total + chip_swap(parts[step].astype(bf16), step).astype(f32)
        return total
    return side_sums(parts[0], *corner_sums(parts[3].astype(bf16), parts))


def line_gather(value):
    count = lax.axis_size("dp")
    index = lax.axis_index("dp")
    up = down = value
    found = [value] * count
    for step in range(1, count):
        up = lax.ppermute(up, "dp", [(at, at + 1) for at in range(count - 1)])
        down = lax.ppermute(down, "dp", [(at + 1, at) for at in range(count - 1)])
        for at in range(count):
            found[at] = jnp.where(
                index - at == step, up, jnp.where(at - index == step, down, found[at])
            )
    return jnp.stack(found)


def sum_everywhere(value, marks):
    steps = [("core", 1)]
    for axis in ("chip", "dp"):
        step = 1
        while step < lax.axis_size(axis):
            steps.append((axis, step))
            step *= 2
    for at, (axis, step) in enumerate(steps):
        pairs = [(index, index ^ step) for index in range(lax.axis_size(axis))]
        other = lax.ppermute(value, axis, pairs)
        value = value + (after(other, marks[at]) if at < len(marks) else other)
    return value


def by_core(core, mine, other, axis=0):
    return jnp.where(
        core == 0,
        jnp.concatenate([mine, other], axis=axis),
        jnp.concatenate([other, mine], axis=axis),
    )


def inverse_rms(values):
    return lax.rsqrt(jnp.mean(values * values, axis=-1, keepdims=True) + norm_epsilon)


def norm_back(grad_normed, values, inverse, gain):
    normal = values * inverse
    scaled = grad_normed * gain
    return inverse * (scaled - normal * jnp.mean(scaled * normal, axis=-1, keepdims=True))


def on_device(
    inputs,
    segments,
    attn_gain,
    query_weight,
    key_weight,
    value_weight,
    output_weight,
    persistent,
    memory_first,
    memory_second,
    rate_weight,
    decay_logit,
    momentum_logit,
    ffn_gain,
    gate_weight,
    up_weight,
    down_weight,
    cotangent,
):
    groups, chips, core_count = (lax.axis_size("dp"), lax.axis_size("chip"), 2)
    core = lax.axis_index("core")
    chip = lax.axis_index("chip")
    position = chip * core_count + core
    chain = chips * core_count
    devices = groups * chain
    scale = HD ** (-0.5)
    half = D // 2
    core_heads = H // core_count
    heads = core_heads // chips
    rows = heads * HD
    width = 2 * GROUP
    all_rows = 3 * rows + RATE_ROWS
    shard = query_weight.shape[0]
    ff_own = gate_weight.shape[1] // chain
    pieces = devices // 2
    per_head = max(HD // shard, 1)
    near = 2 * shard == HD and core_heads == heads * chips

    tokens = inputs[0]
    grad_out = cotangent[0]

    if chips == 4:
        along, across = chip_swap(tokens, 1), chip_swap(tokens, 2)
    w_sides = pack_weights(
        chips,
        heads,
        key_weight,
        value_weight,
        query_weight,
        rate_weight,
        jnp.stack([attn_gain, ffn_gain], axis=1),
        persistent,
    )
    w_side = lax.dynamic_index_in_dim(w_sides, core, 0, keepdims=False)
    w_side_other = core_swap(lax.dynamic_index_in_dim(w_sides, 1 - core, 0, keepdims=False))
    w_pair = gather_chips(by_core(core, w_side, w_side_other))
    w_context = w_pair[:, : 2 * half]
    w_tail = w_pair[:, 3 * half :]
    persist = w_tail[:, :NP]
    if chips == 4:
        cut = GROUP // 2
        corner = jnp.concatenate(
            [chip_swap(along[:cut], 2), chip_swap(across[cut:], 1)], axis=0
        )
        token_halves = [tokens, along, across, corner]
    else:
        token_halves = chip_parts(tokens)
    mem_shard = jnp.concatenate([memory_first, memory_second], axis=1)
    if chips == 4:
        mem_shard = after(mem_shard, corner)
        gate_weight_, up_weight_ = after(gate_weight, corner), up_weight
    else:
        gate_weight_, up_weight_ = gate_weight, up_weight
    if near:
        mem_pair = by_core(core, mem_shard, core_swap(mem_shard))
        mem_line = line_gather(mem_pair).reshape(groups * 2 * shard, 2 * MH)
        mem_mine = lax.dynamic_slice_in_dim(mem_line, core * rows, rows, 0)
    else:
        mem_all = lax.all_gather(mem_shard, ("dp", "chip", "core"), axis=0, tiled=True)
        mem_all = lax.dynamic_slice_in_dim(mem_all, core * half, half, 0)
        mem_all = mem_all.reshape(heads, chips, HD, 2 * MH)
        mem_mine = lax.dynamic_index_in_dim(mem_all, chip, 1, keepdims=False).reshape(rows, 2 * MH)
    mem_mine = mem_mine.astype(f32)
    first_init, second_init = mem_mine[:, :MH], mem_mine[:, MH:]
    w_gate_up = lax.all_to_all(
        pack_columns(chain, gate_weight_, up_weight_), ("chip", "core"), 0, 0, tiled=True
    ).reshape(chain * shard, 2 * ff_own)
    chip_index = chip.astype(jnp.int32)[None]
    if chips == 4 and 2 * rows % 128 == 0:
        w_flat, gains = take_heads(chip_index, chips, heads, w_pair)
    else:
        w_main = jnp.concatenate(
            [
                lax.dynamic_slice_in_dim(w_pair, chip * 2 * rows, 2 * rows, 1),
                lax.dynamic_slice_in_dim(w_pair, 2 * half + chip * rows, rows, 1),
                lax.dynamic_slice_in_dim(w_tail, NP + 2 + chip * heads, heads, 1),
                jnp.zeros((D, RATE_ROWS - heads), bf16),
            ],
            axis=1,
        )
        w_flat = w_main.T
        gains = w_tail[:, NP : NP + 2].astype(f32).T
    w_flat = after(w_flat, w_gate_up)
    gain_one, gain_two = gains[:1], gains[1:2]

    out_order = []
    for side in range(2):
        for piece in range(pieces):
            spot_, part = divmod(piece, per_head)
            at_chip, turn = divmod(spot_, heads)
            source = side * pieces + (turn * chips + at_chip) * per_head + part
            out_order.append((source, 2 * piece + side))
    out_moved = lax.ppermute(output_weight, ("dp", "chip", "core"), out_order)
    if chips == 4:
        w_lines = lax.all_gather(
            jnp.concatenate([after(out_moved, w_pair), down_weight], axis=0), "dp", axis=0
        )
        out_lines = w_lines[:, :shard]
        w_down = w_lines[:, shard:].reshape(-1, D)
        w_gate_up = lax.all_gather(after(w_gate_up, w_pair), "dp", axis=0, tiled=True)
    else:
        w_gate_up = lax.all_gather(w_gate_up, "dp", axis=0, tiled=True)
        w_down = lax.all_gather(down_weight, "dp", axis=0, tiled=True)
        w_output = gather_chips(out_moved)

    ids = segments[0].reshape(chain, GROUP)
    first_id, last_id = ids[:, 0], ids[:, GROUP - 1]
    before = jnp.concatenate([first_id[:1], ids[:-1, GROUP - 1]])
    joined = jnp.logical_and(jnp.arange(chain) > 0, first_id == before)
    carry = jnp.logical_and(joined, first_id == last_id)
    kept = jnp.logical_and(joined[:, None], ids == first_id[:, None])
    retain = kept.astype(f32)[:, None, :]
    update = (ids == last_id[:, None]).astype(f32)[:, None, :]
    flags = jnp.stack(
        [
            carry.astype(jnp.int32),
            jnp.any(kept, axis=1).astype(jnp.int32),
            jnp.logical_not(jnp.all(kept, axis=1)).astype(jnp.int32),
            jnp.full((chain,), core, jnp.int32),
            jnp.full((chain,), chip, jnp.int32),
        ]
    )
    pair_ids = jnp.stack(
        [
            lax.dynamic_index_in_dim(ids, position, keepdims=False),
            lax.dynamic_index_in_dim(ids, chip * core_count + 1 - core, keepdims=False),
        ]
    )
    id_row, id_col = pair_ids[:, None, :], pair_ids[:, :, None]
    core_index = core.astype(jnp.int32)[None]
    decay = jax.nn.sigmoid(decay_logit)
    momentum = jax.nn.sigmoid(momentum_logit)

    def own_heads(value):
        return lax.dynamic_index_in_dim(
            value.reshape(core_count, heads, chips)[core], chip, 1, keepdims=False
        )

    scalars = jnp.stack([own_heads(1.0 - decay), own_heads(momentum)])

    if chips == 4:
        grad_low = after(grad_out, w_flat)
        along_low, across_high = chip_swap(grad_low[:cut], 1), chip_swap(grad_low[cut:], 2)
    token_blocks = []
    for part in token_halves:
        token_blocks += [part, core_swap(part)]
    placed = ()
    for start in range(0, chain, 8):
        placed = project_blocks(
            start, chain, token_blocks[start : start + 8], gain_one, w_flat, placed
        )
    normed_all, main = placed
    if chips == 4:
        main, along_low, across_high = together(main, along_low, across_high)


    def pair_rows(own):
        return jnp.concatenate([own, core_swap(own)], axis=0)

    if chips == 4:
        corner_along, corner_across = chip_swap(along_low, 2), chip_swap(across_high, 1)
    recalled, saved = memory_forward(
        flags, main, retain, update, first_init, second_init, scalars, chips
    )
    normed = normed_all[:width]
    low = matmul(w_pair[:, : 3 * half], normed, 0, 1, bf16)
    side = matmul(w_context, persist, 0, 0, bf16)
    if chips == 4:
        recalled, corner_along, corner_across, out_lines = together(
            recalled, corner_along, corner_across, out_lines
        )
        out_along, out_across = chip_swap(out_lines, 1), chip_swap(out_lines, 2)
    recalled = after(lax.all_to_all(recalled, "chip", 0, 0, tiled=True), low, side)
    if chips == 4:
        recalled, out_along, out_across = together(recalled, out_along, out_across)
    recalled = recalled.reshape(chips, heads, HD, width).swapaxes(0, 1).reshape(half, width)
    context = by_core(core, recalled, core_swap(recalled))
    if chips == 4:
        upper = groups // 2
        out_corner = (chip_swap(out_along[:upper], 2), chip_swap(out_across[upper:], 1))
        grad_low = after(grad_out, context)
        along_high, across_low = chip_swap(grad_low[cut:], 1), chip_swap(grad_low[:cut], 2)

    far = matmul(w_context, context, 0, 0, bf16)
    mixed, total = attention_forward(scale, core_index, low, far, side, id_row, id_col)

    if chips == 4:
        mixed, along_high, across_low, *out_corner = together(
            mixed, along_high, across_low, *out_corner
        )
        stacked = jnp.stack([out_lines, out_along, out_across, jnp.concatenate(out_corner, axis=0)])
        w_output = jnp.stack(
            [
                lax.dynamic_index_in_dim(stacked, chip ^ at, 0, keepdims=False)
                for at in range(chips)
            ],
            axis=1,
        ).reshape(half, D)

    def pair_sum(left, right, left_dim, right_dim):
        def block(which):
            return lax.slice_in_dim(
                left, which * GROUP, (which + 1) * GROUP, axis=1 - left_dim
            )

        other = core_swap(matmul(block(1), right, left_dim, right_dim, bf16))
        return matmul(block(0), right, left_dim, right_dim) + other.astype(f32)

    middle = tokens.astype(f32) + pair_sum(mixed, w_output, 0, 0)
    inverse_two = inverse_rms(middle)
    normed_own = (middle * inverse_two * gain_two).astype(bf16)
    def chunk(step, normed, grad, arrays):
        def both(pieces):
            return (tuple(pieces), tuple(core_swap(piece) for piece in pieces))

        *arrays, out, back = ffn_chunk(
            step, chips, both(normed), both(grad), w_gate_up, w_down, arrays
        )
        return tuple(arrays), out, back

    def over_cores(part):
        return part[0].astype(f32) + core_swap(part[1]).astype(f32)

    def halves(value, first, second):
        return chip_swap(value[:cut], first), chip_swap(value[cut:], second)

    if chips == 4:
        first = halves(normed_own, 1, 2)
        arrays, out_own, back_own = chunk(0, (normed_own,), (grad_out,), ())
        arrays, first = together(arrays, first)
        later = after(normed_own, arrays[0])
        second = (chip_swap(later[cut:], 1), chip_swap(later[:cut], 2))
        arrays, out_first, back_first = chunk(1, first, (along_low, across_high), arrays)
        arrays, second = together(arrays, second)
        corner = (
            chip_swap(after(first[0], arrays[0]), 2),
            chip_swap(after(first[1], arrays[0]), 1),
        )
        arrays, out_second, back_second = chunk(2, second, (along_high, across_low), arrays)
        arrays, corner = together(arrays, corner)
        sent = halves(after(over_cores(back_first), arrays[0]).astype(bf16), 1, 2)
        arrays, out_corner, back_corner = chunk(3, corner, (corner_along, corner_across), arrays)
        back_corner, sent = together(back_corner, sent)
        all_normed, all_grad, all_hidden, all_grad_gate_up = arrays
        corner_low = over_cores(back_corner).astype(bf16)
        from_corner = halves(corner_low, 1, 2)
        grad_down_w = tokens_product(after(all_hidden, corner_low), all_grad)
        grad_down_w, from_corner = together(grad_down_w, from_corner)

        def add_corner(part, from_corner):
            from_along, from_across = from_corner
            return (
                jnp.concatenate([part[:cut] + from_across, part[cut:] + from_along], axis=0)
            ).astype(bf16)

        last = add_corner(over_cores(back_second), from_corner)
        grad_gate_up_w = tokens_product(after(all_normed, last), all_grad_gate_up)
        grad_gate_up_w, last = together(grad_gate_up_w, halves(last, 1, 2))

        def all_parts(own, sent, last):
            low = own[:cut] + sent[0].astype(f32) + last[1].astype(f32)
            high = own[cut:] + sent[1].astype(f32) + last[0].astype(f32)
            return jnp.concatenate([low, high], axis=0)

        grad_normed_two = all_parts(over_cores(back_own), sent, last)
        out_corner = over_cores(after(out_corner, grad_gate_up_w)).astype(bf16)
        out_first = over_cores(after(out_first, grad_gate_up_w)).astype(bf16)
        out_second = over_cores(after(out_second, grad_gate_up_w))
        out_own = over_cores(after(out_own, grad_gate_up_w))
    else:
        grads_by_step, normeds_by_step = chip_parts(grad_out), chip_parts(normed_own)
        outs, backs, arrays = [], [], ()
        for step in range(chips):
            arrays, out, back = chunk(step, (normeds_by_step[step],), (grads_by_step[step],), arrays)
            outs.append(over_cores(out))
            backs.append(over_cores(back))
        all_normed, all_grad, all_hidden, all_grad_gate_up = arrays
        grad_normed_two = chip_sums(backs)
        grad_down_w = tokens_product(all_hidden, all_grad)
        grad_gate_up_w = tokens_product(all_normed, all_grad_gate_up)
    grad_middle = grad_out.astype(f32) + norm_back(grad_normed_two, middle, inverse_two, gain_two)
    down_part = lax.psum_scatter(grad_down_w, "dp", scatter_dimension=0, tiled=True).astype(f32)
    gate_up_scattered = lax.psum_scatter(grad_gate_up_w, "dp", scatter_dimension=0, tiled=True)

    grad_attended = pair_rows(grad_middle.astype(bf16))
    grad_output_w = matmul(mixed, grad_attended, 1, 0, bf16)
    output_part = lax.psum_scatter(grad_output_w, "dp", scatter_dimension=0, tiled=True)
    grad_mixed = matmul(w_output, grad_attended, 1, 1, bf16)
    events = ()
    if chips == 4:
        from_corner = halves(after(out_corner, grad_normed_two), 1, 2)
        out_last = add_corner(out_second, after(from_corner, grad_mixed))
        out_sent = halves(after(out_first, grad_normed_two), 1, 2)
        events = (out_last,)
    grad_part, grad_far, grad_side = attention_backward(
        scale,
        core_index,
        low,
        far,
        side,
        id_row,
        id_col,
        mixed,
        total,
        after(grad_mixed, *events),
    )
    grad_side = grad_side.astype(bf16)
    if chips == 4:
        grad_far, out_sent, out_last = together(grad_far, out_sent, halves(out_last, 1, 2))
        out_sum = all_parts(out_own, out_sent, out_last)
    else:
        out_sum = chip_sums(outs)
    result = (middle + out_sum).astype(bf16)

    def half_rows(which):
        return lax.dynamic_slice(w_pair, (which * half, 0), (half, 2 * half))

    pull_other = core_swap(matmul(half_rows(1 - core), grad_far, 1, 0, bf16))
    pull = (matmul(half_rows(core), grad_far, 1, 0) + pull_other.astype(f32)).astype(bf16)
    pull = pull.reshape(heads, chips, HD, width).swapaxes(0, 1).reshape(chips, rows, width)
    pull = after(lax.all_to_all(pull, "chip", 0, 0, tiled=True), result)
    grad_part = lax.all_to_all(
        after(grad_part.reshape(chips, 3 * rows, width), pull), "chip", 0, 0, tiled=True
    )
    grad_context_w = context_product(context, grad_far, persist, grad_side, w_pair)
    context_part = lax.psum_scatter(grad_context_w, "dp", scatter_dimension=0, tiled=True)
    context_part = context_part.reshape(chips, 2 * shard, 2 * half + 128)
    output_part = output_part.reshape(chips, shard, 2, half).swapaxes(1, 2)
    context_part = jnp.concatenate(
        [context_part, output_part.reshape(chips, 2 * shard, half)], axis=2
    )
    grads, grad_first, grad_second, grad_scalars = memory_backward(
        flags,
        main,
        retain,
        update,
        first_init,
        second_init,
        scalars,
        saved,
        after(pull, down_part, gate_up_scattered, grad_context_w),
    )
    grads, grad_part = together(grads, grad_part)
    gate_up_part = lax.all_to_all(
        after(gate_up_scattered, grad_part).reshape(chain, shard, 2 * ff_own),
        ("chip", "core"),
        0,
        0,
        tiled=True,
    )
    grad_mem = jnp.concatenate([grad_first, grad_second], axis=1).astype(bf16)
    corner_own, corner_other = back_blocks(chip_index, chips - 1, 1, grads, grad_part, w_flat)
    side_own, side_other = back_blocks(
        chip_index, 0, chips - 1, grads, after(grad_part, corner_own), w_flat
    )
    side_own, corner_other, gate_up_part = together(
        side_own, core_swap(corner_other), gate_up_part
    )
    corner_low = (corner_own[0].astype(f32) + corner_other[0].astype(f32)).astype(bf16)
    side_other = core_swap(side_other)
    grad_heads_w = merge_blocks(
        chip_index, groups, grads, after(grad_part, corner_low, side_own), normed_all
    )
    if near:
        spread = jnp.zeros((groups, 2 * shard, 2 * MH), bf16)
        spread = lax.dynamic_update_slice_in_dim(
            spread, grad_mem.reshape(heads, 2 * shard, 2 * MH), core * heads, 0
        )
        mem_line = lax.all_to_all(after(spread, gate_up_part), "dp", 0, 0, tiled=True)
        grad_heads_w, mem_line = together(grad_heads_w, mem_line)
    if chips == 4:
        grad_heads_w, side_other, from_corner = together(
            grad_heads_w, side_other, halves(corner_low, 1, 2)
        )
    heads_sum = lax.psum_scatter(grad_heads_w, "dp", scatter_dimension=0)
    grad_normeds = [
        side_own[step].astype(f32) + side_other[step].astype(f32) for step in range(chips - 1)
    ]
    grad_normeds.append(corner_low)
    tokens_wide = tokens.astype(f32)
    if chips == 4:
        from_along, from_across = (part.astype(f32) for part in from_corner)
        first_sum = jnp.concatenate(
            [grad_normeds[1][:cut], grad_normeds[1][cut:] + from_across], axis=0
        ).astype(bf16)
        second_sum = jnp.concatenate(
            [grad_normeds[2][:cut] + from_along, grad_normeds[2][cut:]], axis=0
        ).astype(bf16)
        heads_sum = after(heads_sum, first_sum, second_sum)
        marks = (corner_low, first_sum)
    else:
        marks = (corner_low, side_own)
    heads_part = lax.all_to_all(
        heads_sum.T.reshape(chain, shard, all_rows), ("chip", "core"), 0, 0, tiled=True
    )
    context_parts = [
        lax.dynamic_index_in_dim(after(context_part, *marks), chip ^ step, 0, keepdims=False)
        for step in range(chips)
    ]
    if chips == 4:
        context_first, context_second = corner_sums(
            context_parts[3].astype(bf16), context_parts, heads_sum
        )
        grad_normed = side_sums(grad_normeds[0], first_sum, second_sum, context_first)
        context_part = side_sums(
            context_parts[0], context_first, context_second, grad_normed
        ).astype(bf16)
    else:
        grad_normed = chip_sums(grad_normeds)
        context_part = chip_sums(context_parts).astype(bf16)
    grad_tokens_one = norm_back(grad_normed, tokens_wide, inverse_rms(tokens_wide), gain_one)
    grad_inputs = (grad_middle + grad_tokens_one).astype(bf16)
    marks = (*marks, heads_sum, grad_normed, heads_part)
    heads_part = after(heads_part, grad_inputs)

    def own_rows(part):
        mine = lax.dynamic_slice_in_dim(part, core * shard, shard, 0)
        other = core_swap(lax.dynamic_slice_in_dim(part, (1 - core) * shard, shard, 0))
        return mine, other

    output_part = jnp.concatenate(
        [context_part[:shard, 2 * half + 128 :], context_part[shard:, 2 * half + 128 :]], axis=1
    )
    mine, other = own_rows(context_part[:, : 2 * half + 128])
    persist_part = (mine.astype(f32) + other.astype(f32))[:, 2 * half : 2 * half + NP]
    by_side = by_core(core, mine[None], other[None])
    grad_keys_own, grad_values_own, grad_queries_own, grad_rates_own, gain_one_part = (
        unpack_weights(
            chips,
            heads,
            heads_part,
            by_side,
            key_weight,
            value_weight,
            query_weight,
            rate_weight,
            attn_gain[:, None],
        )
    )
    gate_part, up_part, gain_two_part = unpack_columns(
        gate_up_part, gate_weight, up_weight, ffn_gain[:, None]
    )
    if near:
        mine, other = own_rows(
            jnp.sum(after(mem_line, *marks).astype(f32), axis=0).astype(bf16)
        )
        mem_part = mine.astype(f32) + other.astype(f32)
    else:
        spread = jnp.zeros((heads, chips, HD, 2 * MH), bf16)
        spread = lax.dynamic_update_slice_in_dim(
            spread, grad_mem.reshape(heads, 1, HD, 2 * MH), chip, 1
        ).reshape(half, 2 * MH)
        spread = lax.dynamic_update_slice_in_dim(
            jnp.zeros((D, 2 * MH), bf16), spread, core * half, 0
        )
        mem_part = lax.psum_scatter(
            spread, ("dp", "chip", "core"), scatter_dimension=0, tiled=True
        ).astype(f32)
    scalar_sums = jnp.sum(grad_scalars, axis=1)[: 2 * heads].reshape(1, heads, 1, 2)
    spots = lax.dynamic_update_slice(
        jnp.zeros((core_count, heads, chips, 2), f32), scalar_sums, (core, 0, chip, 0)
    )
    sums = sum_everywhere(spots.reshape(H, 2), marks)
    grad_decay = sums[:, 0] * decay * (1.0 - decay)
    grad_momentum = sums[:, 1] * momentum * (1.0 - momentum)
    output_own = lax.ppermute(
        output_part, ("dp", "chip", "core"), [(d, s) for s, d in out_order]
    ).astype(f32)
    return (
        result[None],
        grad_inputs[None],
        gain_one_part[:, 0],
        grad_queries_own,
        grad_keys_own,
        grad_values_own,
        output_own,
        persist_part,
        mem_part[:, :MH],
        mem_part[:, MH:],
        grad_rates_own,
        grad_decay,
        grad_momentum,
        gain_two_part[:, 0],
        gate_part,
        up_part,
        down_part,
    )


def solution(mesh):
    split = jax.sharding.Mesh(
        mesh.devices.reshape(mesh.shape["dp"], mesh.shape["seq"] // 2, 2), ("dp", "chip", "core")
    )
    row = P("dp", ("chip", "core"), None)
    vector = P(("dp", "chip", "core"))
    matrix = P(("dp", "chip", "core"), None)
    in_specs = (
        row,
        P("dp", None),
        vector,
        matrix,
        matrix,
        matrix,
        matrix,
        matrix,
        matrix,
        matrix,
        matrix,
        P(),
        P(),
        vector,
        matrix,
        matrix,
        matrix,
        row,
    )
    out_specs = (
        row,
        row,
        vector,
        matrix,
        matrix,
        matrix,
        matrix,
        matrix,
        matrix,
        matrix,
        matrix,
        P(),
        P(),
        vector,
        matrix,
        matrix,
        matrix,
    )
    return jax.shard_map(
        on_device, mesh=split, in_specs=in_specs, out_specs=out_specs, check_vma=False
    )
```

```python
import jax
import jax.numpy as jnp
from jax import lax
from jax.experimental import pallas as pl
from jax.experimental.pallas import tpu as pltpu
from jax.sharding import PartitionSpec as P

D = 1536
H = 16
HD = 96
MH = 384
NP = 64
GROUP = 512
RATE_ROWS = 16
RATE_SCALE = 2.0 / 384
norm_epsilon = 1e-06
f32 = jnp.float32
bf16 = jnp.bfloat16


def dot_nn(left, right):
    return lax.dot_general(left, right, (((1,), (0,)), ((), ())), preferred_element_type=f32)


def dot_tn(left, right):
    return lax.dot_general(left, right, (((0,), (0,)), ((), ())), preferred_element_type=f32)


def dot_nt(left, right):
    return lax.dot_general(left, right, (((1,), (1,)), ((), ())), preferred_element_type=f32)


def inverse_root(values):
    return lax.rsqrt(jnp.mean(values * values, axis=0, keepdims=True) + norm_epsilon)


def spot(heads, head, which):
    at = 2 * head + which if which < 2 else 2 * heads + head
    return slice(at * HD, (at + 1) * HD)


def memory_forward_kernel(
    heads,
    blocks,
    flags,
    main_ref,
    retain_ref,
    update_ref,
    first_ref,
    second_ref,
    scalars_ref,
    recalled_ref,
    saved_ref,
    state,
):
    turn = pl.program_id(0)

    @pl.when(turn == 0)
    def blank():
        state[...] = jnp.zeros_like(state)

    saved_ref[0] = state[...]
    retain = retain_ref[0]

    def recall_with(first, second, head):
        rows = slice(head * HD, (head + 1) * HD)
        raw = main_ref[spot(heads, head, 2), :].astype(f32)
        probes = (raw * inverse_root(raw)).astype(bf16)
        inner = dot_tn(first[rows, :].astype(bf16), probes)
        return dot_nn(second[rows, :].astype(bf16), jax.nn.silu(inner).astype(bf16))

    only_state = flags[1, turn] * (1 - flags[2, turn])
    only_init = flags[2, turn] * (1 - flags[1, turn])

    @pl.when(only_state == 1)
    def from_state():
        for head in range(heads):
            recalled_ref[0, head * HD : (head + 1) * HD, :] = recall_with(
                state[0], state[1], head
            ).astype(bf16)

    @pl.when(only_init == 1)
    def from_init():
        for head in range(heads):
            recalled_ref[0, head * HD : (head + 1) * HD, :] = recall_with(
                first_ref[...], second_ref[...], head
            ).astype(bf16)

    @pl.when(only_state + only_init == 0)
    def from_both():
        for head in range(heads):
            recalled_ref[0, head * HD : (head + 1) * HD, :] = (
                retain * recall_with(state[0], state[1], head)
                + (1.0 - retain) * recall_with(first_ref[...], second_ref[...], head)
            ).astype(bf16)

    @pl.when(turn < blocks - 1)
    def step():
        carry = flags[0, turn].astype(f32)
        for head in range(heads):
            rows = slice(head * HD, (head + 1) * HD)
            keep = scalars_ref[0, head]
            push = scalars_ref[1, head] * carry
            base_first = jnp.where(carry > 0.5, state[0, rows, :], first_ref[rows, :])
            base_second = jnp.where(carry > 0.5, state[1, rows, :], second_ref[rows, :])
            raw = main_ref[spot(heads, head, 0), :].astype(f32)
            keys = (raw * inverse_root(raw)).astype(bf16)
            second_low = base_second.astype(bf16)
            inner = dot_tn(base_first.astype(bf16), keys)
            gate = jax.nn.sigmoid(inner)
            active = inner * gate
            slope = gate + active * (1.0 - gate)
            active_low = active.astype(bf16)
            at = 3 * heads * HD + head
            rate = RATE_SCALE * jax.nn.sigmoid(main_ref[at : at + 1, :].astype(f32))
            weight = rate * update_ref[0] * (1.0 / GROUP)
            error = dot_nn(second_low, active_low) - main_ref[spot(heads, head, 1), :].astype(f32)
            pull = (error * weight).astype(bf16)
            inner_pull = (dot_tn(second_low, pull) * slope).astype(bf16)
            speed_first = push * state[2, rows, :] - dot_nt(keys, inner_pull)
            speed_second = push * state[3, rows, :] - dot_nt(pull, active_low)
            state[0, rows, :] = keep * base_first + speed_first
            state[1, rows, :] = keep * base_second + speed_second
            state[2, rows, :] = speed_first
            state[3, rows, :] = speed_second


def memory_forward(flags, main, retain, update, first, second, scalars, chips):
    rows = (main.shape[0] - RATE_ROWS) // 3
    heads = rows // HD
    width = main.shape[1] // chips
    blocks = main.shape[1] // GROUP
    per = width // GROUP

    def block(turn, flags):
        return (0, ((turn // per) ^ flags[4, 0]) * per + ((turn % per) ^ flags[3, 0]))

    def by_chip(turn, flags):
        return (turn // per, 0, turn % per)

    def by_turn(turn, flags):
        return (turn, 0, 0)

    def whole(turn, flags):
        return (0, 0)

    line = pl.BlockSpec((1, 1, GROUP), by_turn)
    return pl.pallas_call(
        lambda *refs: memory_forward_kernel(heads, blocks, *refs),
        grid_spec=pltpu.PrefetchScalarGridSpec(
            num_scalar_prefetch=1,
            grid=(blocks,),
            in_specs=[
                pl.BlockSpec((3 * rows + RATE_ROWS, GROUP), block),
                line,
                line,
                pl.BlockSpec((rows, MH), whole),
                pl.BlockSpec((rows, MH), whole),
                pl.BlockSpec(memory_space=pltpu.SMEM),
            ],
            out_specs=[
                pl.BlockSpec((1, rows, GROUP), by_chip),
                pl.BlockSpec((1, 4, rows, MH), lambda turn, flags: (turn, 0, 0, 0)),
            ],
            scratch_shapes=[pltpu.VMEM((4, rows, MH), f32)],
        ),
        out_shape=[
            jax.ShapeDtypeStruct((chips, rows, width), bf16),
            jax.ShapeDtypeStruct((blocks, 4, rows, MH), f32),
        ],
        compiler_params=pltpu.CompilerParams(vmem_limit_bytes=50 * 2**20),
        cost_estimate=pl.CostEstimate(
            flops=blocks * heads * 7 * 2 * GROUP * HD * MH * 4,
            bytes_accessed=blocks * 6 * rows * MH * 4,
            transcendentals=blocks * heads * 2 * MH * GROUP,
        ),
    )(flags, main, retain, update, first, second, scalars)


def memory_backward_kernel(
    heads,
    blocks,
    flags,
    main_ref,
    retain_ref,
    update_ref,
    first_ref,
    second_ref,
    scalars_ref,
    saved_ref,
    pull_ref,
    grads_ref,
    grad_first_ref,
    grad_second_ref,
    grad_scalars_ref,
    message,
):
    count = pl.program_id(0)
    turn = blocks - 1 - count

    @pl.when(count == 0)
    def blank():
        message[...] = jnp.zeros_like(message)
        grad_first_ref[...] = jnp.zeros_like(grad_first_ref)
        grad_second_ref[...] = jnp.zeros_like(grad_second_ref)
        grad_scalars_ref[...] = jnp.zeros_like(grad_scalars_ref)

    rate_row = 3 * heads * HD

    @pl.when(count == 0)
    def last():
        for head in range(heads):
            grads_ref[spot(heads, head, 0), :] = jnp.zeros((HD, GROUP), bf16)
            grads_ref[spot(heads, head, 1), :] = jnp.zeros((HD, GROUP), bf16)
        grads_ref[rate_row:, :] = jnp.zeros((RATE_ROWS, GROUP), bf16)

    @pl.when(count > 0)
    def step():
        carry = flags[0, turn].astype(f32)
        grad_rates = []
        for head in range(heads):
            rows = slice(head * HD, (head + 1) * HD)
            keep = scalars_ref[0, head]
            push = scalars_ref[1, head] * carry
            base_first = jnp.where(carry > 0.5, saved_ref[0, 0, rows, :], first_ref[rows, :])
            base_second = jnp.where(carry > 0.5, saved_ref[0, 1, rows, :], second_ref[rows, :])
            grad_a = message[0, rows, :]
            grad_b = message[1, rows, :]
            grad_sa = message[2, rows, :] + grad_a
            grad_sb = message[3, rows, :] + grad_b
            momentum_part = carry * (
                jnp.sum(saved_ref[0, 2, rows, :] * grad_sa, axis=0, keepdims=True)
                + jnp.sum(saved_ref[0, 3, rows, :] * grad_sb, axis=0, keepdims=True)
            )
            decay_part = -(
                jnp.sum(base_first * grad_a, axis=0, keepdims=True)
                + jnp.sum(base_second * grad_b, axis=0, keepdims=True)
            )
            grad_scalars_ref[2 * head : 2 * head + 1, :] += decay_part
            grad_scalars_ref[2 * head + 1 : 2 * head + 2, :] += momentum_part
            back_a = (-grad_sa).astype(bf16)
            back_b = (-grad_sb).astype(bf16)
            raw = main_ref[spot(heads, head, 0), :].astype(f32)
            inverse = inverse_root(raw)
            normal = raw * inverse
            keys = normal.astype(bf16)
            first_low = base_first.astype(bf16)
            second_low = base_second.astype(bf16)
            inner = dot_tn(first_low, keys)
            gate = jax.nn.sigmoid(inner)
            active = inner * gate
            slope = gate + active * (1.0 - gate)
            bend = gate * (1.0 - gate) * (2.0 + inner - 2.0 * active)
            active_low = active.astype(bf16)
            weight = update_ref[0] * (1.0 / GROUP)
            at = rate_row + head
            rate_sigmoid = jax.nn.sigmoid(main_ref[at : at + 1, :].astype(f32))
            rate = RATE_SCALE * rate_sigmoid
            error = dot_nn(second_low, active_low) - main_ref[spot(heads, head, 1), :].astype(f32)
            pull = (error * (rate * weight)).astype(bf16)
            spread = dot_tn(second_low, pull)
            inner_pull = (spread * slope).astype(bf16)
            back_inner = dot_tn(back_a, keys)
            back_spread = (back_inner * slope).astype(bf16)
            grad_pull = dot_nn(back_b, active_low) + dot_nn(second_low, back_spread)
            grad_rates.append(
                jnp.sum(grad_pull * error, axis=0, keepdims=True)
                * weight
                * rate
                * (1.0 - rate_sigmoid)
            )
            grad_error = grad_pull * (rate * weight)
            grad_error_low = grad_error.astype(bf16)
            grads_ref[spot(heads, head, 1), :] = (-grad_error).astype(bf16)
            grad_active = dot_tn(back_b, pull) + dot_tn(second_low, grad_error_low)
            grad_inner = (back_inner * spread * bend + grad_active * slope).astype(bf16)
            grad_normal = dot_nn(back_a, inner_pull) + dot_nn(first_low, grad_inner)
            grads_ref[spot(heads, head, 0), :] = (
                inverse
                * (grad_normal - normal * jnp.mean(grad_normal * normal, axis=0, keepdims=True))
            ).astype(bf16)
            base_grad_a = keep * grad_a + dot_nt(keys, grad_inner)
            base_grad_b = (
                keep * grad_b + dot_nt(pull, back_spread) + dot_nt(grad_error_low, active_low)
            )
            message[0, rows, :] = carry * base_grad_a
            message[1, rows, :] = carry * base_grad_b
            message[2, rows, :] = push * grad_sa
            message[3, rows, :] = push * grad_sb
            grad_first_ref[rows, :] += (1.0 - carry) * base_grad_a
            grad_second_ref[rows, :] += (1.0 - carry) * base_grad_b
        grad_rates.append(jnp.zeros((RATE_ROWS - heads, GROUP), f32))
        grads_ref[rate_row:, :] = jnp.concatenate(
            grad_rates, axis=0
        ).astype(bf16)

    retain = retain_ref[0]

    def recall_back(first, second, grad_recalled, head):
        rows = slice(head * HD, (head + 1) * HD)
        raw = main_ref[spot(heads, head, 2), :].astype(f32)
        inverse = inverse_root(raw)
        normal = raw * inverse
        probes = normal.astype(bf16)
        first_low = first[rows, :].astype(bf16)
        inner = dot_tn(first_low, probes)
        gate = jax.nn.sigmoid(inner)
        active = inner * gate
        slope = gate + active * (1.0 - gate)
        grad_inner = (dot_tn(second[rows, :].astype(bf16), grad_recalled) * slope).astype(bf16)
        grad_second = dot_nt(grad_recalled, active.astype(bf16))
        grad_first = dot_nt(probes, grad_inner)
        grad_normal = dot_nn(first_low, grad_inner)
        grad_probes = inverse * (
            grad_normal - normal * jnp.mean(grad_normal * normal, axis=0, keepdims=True)
        )
        return grad_first, grad_second, grad_probes

    only_state = flags[1, turn] * (1 - flags[2, turn])
    only_init = flags[2, turn] * (1 - flags[1, turn])

    def from_state(whole):
        for head in range(heads):
            rows = slice(head * HD, (head + 1) * HD)
            grad_recalled = pull_ref[0, rows, :]
            if not whole:
                grad_recalled = (grad_recalled.astype(f32) * retain).astype(bf16)
            grad_first, grad_second, grad_probes = recall_back(
                saved_ref[0, 0], saved_ref[0, 1], grad_recalled, head
            )
            message[0, rows, :] += grad_first
            message[1, rows, :] += grad_second
            grads_ref[spot(heads, head, 2), :] = grad_probes.astype(bf16)

    def from_init(whole):
        for head in range(heads):
            rows = slice(head * HD, (head + 1) * HD)
            grad_recalled = pull_ref[0, rows, :]
            if not whole:
                grad_recalled = (grad_recalled.astype(f32) * (1.0 - retain)).astype(bf16)
            grad_first, grad_second, grad_probes = recall_back(
                first_ref[...], second_ref[...], grad_recalled, head
            )
            grad_first_ref[rows, :] += grad_first
            grad_second_ref[rows, :] += grad_second
            if not whole:
                grad_probes = grad_probes + grads_ref[spot(heads, head, 2), :].astype(f32)
            grads_ref[spot(heads, head, 2), :] = grad_probes.astype(bf16)

    @pl.when(only_state == 1)
    def state_alone():
        from_state(True)

    @pl.when(only_init == 1)
    def init_alone():
        from_init(True)

    @pl.when(only_state + only_init == 0)
    def both():
        from_state(False)
        from_init(False)


def memory_backward(
    flags, main, retain, update, first, second, scalars, saved, pull
):
    chips, rows, width = pull.shape
    heads = rows // HD
    blocks = chips * width // GROUP
    per = width // GROUP
    all_rows = 3 * rows + RATE_ROWS

    def block(count, flags):
        turn = blocks - 1 - count
        return (0, ((turn // per) ^ flags[4, 0]) * per + ((turn % per) ^ flags[3, 0]))

    def by_chip(count, flags):
        turn = blocks - 1 - count
        return (turn // per, 0, turn % per)

    def by_turn(count, flags):
        return (blocks - 1 - count, 0, 0)

    def whole(count, flags):
        return (0, 0)

    line = pl.BlockSpec((1, 1, GROUP), by_turn)
    matrix = pl.BlockSpec((rows, MH), whole)
    return pl.pallas_call(
        lambda *refs: memory_backward_kernel(heads, blocks, *refs),
        grid_spec=pltpu.PrefetchScalarGridSpec(
            num_scalar_prefetch=1,
            grid=(blocks,),
            in_specs=[
                pl.BlockSpec((3 * rows + RATE_ROWS, GROUP), block),
                line,
                line,
                matrix,
                matrix,
                pl.BlockSpec(memory_space=pltpu.SMEM),
                pl.BlockSpec(
                    (1, 4, rows, MH), lambda count, flags: (blocks - 1 - count, 0, 0, 0)
                ),
                pl.BlockSpec((1, rows, GROUP), by_chip),
            ],
            out_specs=[
                pl.BlockSpec((all_rows, GROUP), block),
                matrix,
                matrix,
                pl.BlockSpec((8, MH), whole),
            ],
            scratch_shapes=[pltpu.VMEM((4, rows, MH), f32)],
        ),
        out_shape=[
            jax.ShapeDtypeStruct((all_rows, chips * width), bf16),
            jax.ShapeDtypeStruct((rows, MH), f32),
            jax.ShapeDtypeStruct((rows, MH), f32),
            jax.ShapeDtypeStruct((8, MH), f32),
        ],
        compiler_params=pltpu.CompilerParams(vmem_limit_bytes=56 * 2**20),
        cost_estimate=pl.CostEstimate(
            flops=blocks * heads * 19 * 2 * GROUP * HD * MH * 4,
            bytes_accessed=blocks * 8 * rows * MH * 4,
            transcendentals=blocks * heads * 2 * MH * GROUP,
        ),
    )(flags, main, retain, update, first, second, scalars, saved, pull)


QUERIES = 256


def visible_bias(bias_ref, row_ref, col_ref):
    shape = bias_ref.shape[1:]
    key = lax.broadcasted_iota(jnp.int32, shape, 0)
    query = lax.broadcasted_iota(jnp.int32, shape, 1)
    for block in range(bias_ref.shape[0]):
        seen = jnp.logical_and(key <= query, col_ref[block] == row_ref[block])
        bias_ref[block] = jnp.where(seen, 0.0, -1e30)


def attention_forward_kernel(
    scale, core, low_ref, query_ref, far_ref, side_ref, row_ref, col_ref, mixed_ref, total_ref, bias_ref
):
    @pl.when(jnp.logical_and(pl.program_id(0) == 0, pl.program_id(1) == 0))
    def fill():
        visible_bias(bias_ref, row_ref, col_ref)

    block = pl.program_id(1)
    for part in range(GROUP // QUERIES):
        lanes = slice(part * QUERIES, (part + 1) * QUERIES)
        upto = (part + 1) * QUERIES
        query = query_ref[:, lanes]
        bias = bias_ref[block, :upto, lanes]
        s_p = dot_tn(side_ref[:HD], query) * scale
        s_r = dot_tn(far_ref[:HD, :upto], query) * scale + bias
        s_l = dot_tn(low_ref[:HD, :upto], query) * scale + bias
        top = jnp.maximum(
            jnp.max(s_p, axis=0, keepdims=True),
            jnp.maximum(
                jnp.max(s_r, axis=0, keepdims=True), jnp.max(s_l, axis=0, keepdims=True)
            ),
        )
        e_p = jnp.exp(s_p - top)
        e_r = jnp.exp(s_r - top)
        e_l = jnp.exp(s_l - top)
        total = (
            jnp.sum(e_p, axis=0, keepdims=True)
            + jnp.sum(e_r, axis=0, keepdims=True)
            + jnp.sum(e_l, axis=0, keepdims=True)
        )
        mixed = (
            dot_nn(side_ref[HD:], e_p.astype(bf16))
            + dot_nn(far_ref[HD:, :upto], e_r.astype(bf16))
            + dot_nn(low_ref[HD:, :upto], e_l.astype(bf16))
        )
        mixed_ref[:, lanes] = (mixed / total).astype(bf16)
        total_ref[0, :, lanes] = top + jnp.log(total)


def attention_specs(rows, width):
    count = width // GROUP
    heads = rows // HD
    low = pl.BlockSpec((2 * HD, GROUP), lambda head, block, core: (head, block))
    query = pl.BlockSpec((HD, GROUP), lambda head, block, core: (2 * heads + head, block))
    far = pl.BlockSpec((2 * HD, GROUP), lambda head, block, core: (head, block ^ core[0]))
    side = pl.BlockSpec((2 * HD, NP), lambda head, block, core: (head, 0))
    row = pl.BlockSpec((count, 1, GROUP), lambda head, block, core: (0, 0, 0))
    col = pl.BlockSpec((count, GROUP, 1), lambda head, block, core: (0, 0, 0))
    main = pl.BlockSpec((HD, GROUP), lambda head, block, core: (head, block))
    line = pl.BlockSpec((1, 1, GROUP), lambda head, block, core: (head, 0, block))
    return low, query, far, side, row, col, main, line


def attention_forward(scale, core, low, far, side, row, col):
    rows, width = low.shape[0] // 3, low.shape[1]
    low_spec, query_spec, far_spec, side_spec, row_spec, col_spec, main, line = attention_specs(
        rows, width
    )
    heads, count = rows // HD, width // GROUP
    return pl.pallas_call(
        lambda *refs: attention_forward_kernel(scale, *refs),
        grid_spec=pltpu.PrefetchScalarGridSpec(
            num_scalar_prefetch=1,
            grid=(heads, count),
            in_specs=[low_spec, query_spec, far_spec, side_spec, row_spec, col_spec],
            out_specs=[main, line],
            scratch_shapes=[pltpu.VMEM((count, GROUP, GROUP), f32)],
        ),
        out_shape=[
            jax.ShapeDtypeStruct((rows, width), bf16),
            jax.ShapeDtypeStruct((heads, 1, width), f32),
        ],
        compiler_params=pltpu.CompilerParams(vmem_limit_bytes=50 * 2**20),
        cost_estimate=pl.CostEstimate(
            flops=heads * count * 4 * GROUP * 1088 * HD * 4,
            bytes_accessed=6 * rows * width * 2,
            transcendentals=heads * count * GROUP * 1088,
        ),
    )(core, low, low, far, side, row, col)


def attention_backward_kernel(
    scale,
    core,
    low_ref,
    query_ref,
    far_ref,
    side_ref,
    row_ref,
    col_ref,
    mixed_ref,
    total_ref,
    grad_ref,
    grads_ref,
    grad_far_ref,
    grad_side_ref,
    bias_ref,
):
    @pl.when(jnp.logical_and(pl.program_id(0) == 0, pl.program_id(1) == 0))
    def fill():
        visible_bias(bias_ref, row_ref, col_ref)

    block = pl.program_id(1)

    @pl.when(block == 0)
    def blank():
        grad_side_ref[...] = jnp.zeros_like(grad_side_ref)

    parts = GROUP // QUERIES
    sums = {}
    for part in reversed(range(parts)):
        lanes = slice(part * QUERIES, (part + 1) * QUERIES)
        upto = (part + 1) * QUERIES
        query = query_ref[:, lanes]
        grad = grad_ref[:, lanes]
        bias = bias_ref[block, :upto, lanes] - total_ref[0, :, lanes]
        mean = jnp.sum(
            grad.astype(f32) * mixed_ref[:, lanes].astype(f32), axis=0, keepdims=True
        )
        grad_query = jnp.zeros((HD, QUERIES), f32)
        for name, keys, values, extra in (
            ("p", side_ref[:HD], side_ref[HD:], -total_ref[0, :, lanes]),
            ("r", far_ref[:HD, :upto], far_ref[HD:, :upto], bias),
            ("l", low_ref[:HD, :upto], low_ref[HD:, :upto], bias),
        ):
            chances = jnp.exp(dot_tn(keys, query) * scale + extra)
            slope = (chances * (dot_tn(values, grad) - mean)).astype(bf16)
            grad_query += dot_nn(keys, slope)
            grad_keys = dot_nt(query, slope)
            grad_values = dot_nt(grad, chances.astype(bf16))
            if name in sums:
                old_keys, old_values = sums[name]
                if name == "p":
                    sums[name] = (old_keys + grad_keys, old_values + grad_values)
                else:
                    sums[name] = (
                        jnp.concatenate([old_keys[:, :upto] + grad_keys, old_keys[:, upto:]], axis=1),
                        jnp.concatenate(
                            [old_values[:, :upto] + grad_values, old_values[:, upto:]], axis=1
                        ),
                    )
            else:
                sums[name] = (grad_keys, grad_values)
        grads_ref[2 * HD :, lanes] = (grad_query * scale).astype(bf16)
    grad_side_ref[:HD] += sums["p"][0] * scale
    grad_side_ref[HD:] += sums["p"][1]
    grad_far_ref[:HD] = (sums["r"][0] * scale).astype(bf16)
    grad_far_ref[HD:] = sums["r"][1].astype(bf16)
    grads_ref[:HD] = (sums["l"][0] * scale).astype(bf16)
    grads_ref[HD : 2 * HD] = sums["l"][1].astype(bf16)


def attention_backward(scale, core, low, far, side, row, col, mixed, total, grad):
    rows, width = low.shape[0] // 3, low.shape[1]
    low_spec, query_spec, far_spec, side_spec, row_spec, col_spec, main, line = attention_specs(
        rows, width
    )
    heads, count = rows // HD, width // GROUP
    return pl.pallas_call(
        lambda *refs: attention_backward_kernel(scale, *refs),
        grid_spec=pltpu.PrefetchScalarGridSpec(
            num_scalar_prefetch=1,
            grid=(heads, count),
            in_specs=[
                low_spec,
                query_spec,
                far_spec,
                side_spec,
                row_spec,
                col_spec,
                main,
                line,
                main,
            ],
            out_specs=[
                pl.BlockSpec((3 * HD, GROUP), lambda head, block, core: (head, block)),
                far_spec,
                side_spec,
            ],
            scratch_shapes=[pltpu.VMEM((count, GROUP, GROUP), f32)],
        ),
        out_shape=[
            jax.ShapeDtypeStruct((3 * rows, width), bf16),
            jax.ShapeDtypeStruct((2 * rows, width), bf16),
            jax.ShapeDtypeStruct((2 * rows, NP), f32),
        ],
        compiler_params=pltpu.CompilerParams(vmem_limit_bytes=50 * 2**20),
        cost_estimate=pl.CostEstimate(
            flops=heads * count * 10 * GROUP * 1088 * HD * 4,
            bytes_accessed=14 * rows * width * 2,
            transcendentals=heads * count * GROUP * 1088,
        ),
    )(core, low, low, far, side, row, col, mixed, total, grad)


def head_of(core, chip, turn, chips, heads):
    return core * chips * heads + turn * chips + chip


def pack_weights(chips, heads, key, value, query, rate, gains, side):
    shard = key.shape[0]

    def kernel(key_ref, value_ref, query_ref, rate_ref, gains_ref, side_ref, out_ref):
        for core in range(2):
            order = [
                head_of(core, chip, turn, chips, heads)
                for chip in range(chips)
                for turn in range(heads)
            ]
            end = 3 * D // 2
            out_ref[core, :, end:] = jnp.zeros((shard, 128), bf16)
            out_ref[core, :, end : end + NP] = side_ref[...]
            out_ref[core, :, end + NP : end + NP + 2] = gains_ref[...]
            for at, head in enumerate(order):
                columns = slice(head * HD, (head + 1) * HD)
                low = 2 * at * HD
                out_ref[core, :, low : low + HD] = key_ref[:, columns]
                out_ref[core, :, low + HD : low + 2 * HD] = value_ref[:, columns]
                low = D + at * HD
                out_ref[core, :, low : low + HD] = query_ref[:, columns]
                low = end + NP + 2 + at
                out_ref[core, :, low : low + 1] = rate_ref[:, head : head + 1]

    return pl.pallas_call(
        kernel, out_shape=jax.ShapeDtypeStruct((2, shard, 3 * D // 2 + 128), bf16)
    )(key, value, query, rate, gains, side)


def pack_columns(chain, gate, up):
    shard, whole = gate.shape
    own = whole // chain

    def kernel(gate_ref, up_ref, out_ref):
        groups = out_ref.shape[2] // (2 * size)
        for place in range(chain):
            for which, ref in enumerate((gate_ref, up_ref)):
                for group in range(groups):
                    at = which * own + group * size
                    start = (group * chain + place) * size
                    out_ref[place, :, at : at + size] = ref[:, start : start + size]

    size = whole // (D // shard)
    return pl.pallas_call(
        kernel, out_shape=jax.ShapeDtypeStruct((chain, shard, 2 * own), bf16)
    )(gate, up)


def unpack_columns(parts, gate, up, gain):
    chain, shard = parts.shape[:2]
    whole = gate.shape[1]
    own = whole // chain
    size = whole // (D // shard)

    def kernel(parts_ref, gate_ref, up_ref, gain_ref, gate_out, up_out, gain_out):
        total = jnp.zeros((shard, 1), f32)
        for which, (ref, out) in enumerate(((gate_ref, gate_out), (up_ref, up_out))):
            for place in range(chain):
                for group in range(own // size):
                    at = which * own + group * size
                    start = (group * chain + place) * size
                    out[:, start : start + size] = parts_ref[place, :, at : at + size].astype(f32)
            total += jnp.sum(out[...] * ref[...].astype(f32), axis=1, keepdims=True)
        gain_out[...] = total / gain_ref[...].astype(f32)

    return pl.pallas_call(
        kernel,
        out_shape=[
            jax.ShapeDtypeStruct((shard, whole), f32),
            jax.ShapeDtypeStruct((shard, whole), f32),
            jax.ShapeDtypeStruct((shard, 1), f32),
        ],
    )(parts, gate, up, gain)


def unpack_weights(chips, heads, start, parts, context, key, value, query, rate, gain):
    shard = key.shape[0]

    def kernel(parts_ref, context_ref, key_ref, value_ref, query_ref, rate_ref, gain_ref, *outs):
        key_out, value_out, query_out, rate_out, gain_out = outs
        total = jnp.zeros((shard, 1), f32)
        for core in range(2):
            for chip in range(chips):
                place = chip * 2 + core
                for turn in range(heads):
                    head = head_of(core, chip, turn, chips, heads)
                    at = start + 3 * heads * HD + turn
                    rate_out[:, head : head + 1] = parts_ref[place, :, at : at + 1].astype(f32)
                    columns = slice(head * HD, (head + 1) * HD)
                    for which, (weight, out) in enumerate(
                        ((key_ref, key_out), (value_ref, value_out), (query_ref, query_out))
                    ):
                        there = spot(heads, turn, which)
                        there = slice(start + there.start, start + there.stop)
                        grad = parts_ref[place, :, there].astype(f32)
                        total += jnp.sum(
                            grad * weight[:, columns].astype(f32), axis=1, keepdims=True
                        )
                        if which < 2:
                            near = (2 * (chip * heads + turn) + which) * HD
                            grad += context_ref[core, :, near : near + HD].astype(f32)
                        out[:, columns] = grad
        total += jnp.sum(rate_out[...] * rate_ref[...].astype(f32), axis=1, keepdims=True)
        gain_out[...] = total / gain_ref[...].astype(f32)

    wide = jax.ShapeDtypeStruct((shard, D), f32)
    return pl.pallas_call(
        kernel,
        out_shape=[
            wide,
            wide,
            wide,
            jax.ShapeDtypeStruct((shard, H), f32),
            jax.ShapeDtypeStruct((shard, 1), f32),
        ],
    )(parts, context, key, value, query, rate, gain)


def take_heads(chip, chips, heads, w_pair):
    rows = heads * HD
    size = 128
    span = 2 * rows
    tail_at = 3 * D // 2 // 128

    def kernel(chip_ref, low_ref, query_ref, tail_ref, out_ref, gains_ref):
        def turned(value):
            return value.astype(f32).T

        out_ref[:span] = turned(low_ref[...]).astype(bf16)
        query = turned(query_ref[...])
        odd = chip_ref[0] % 2 == 1
        out_ref[span : span + rows] = jnp.where(odd, query[rows:], query[:rows]).astype(bf16)
        tail = turned(tail_ref[...])
        gains_ref[...] = tail[NP : NP + 8]
        rates = jnp.zeros((heads, size), f32)
        for at in range(chips):
            low = NP + 2 + at * heads
            rates = jnp.where(chip_ref[0] == at, tail[low : low + heads], rates)
        out_ref[span + rows :] = jnp.concatenate(
            [rates, jnp.zeros((RATE_ROWS - heads, size), f32)], axis=0
        ).astype(bf16)

    return pl.pallas_call(
        kernel,
        grid_spec=pltpu.PrefetchScalarGridSpec(
            num_scalar_prefetch=1,
            grid=(D // size,),
            in_specs=[
                pl.BlockSpec((size, span), lambda at, chip_ref: (at, chip_ref[0])),
                pl.BlockSpec((size, span), lambda at, chip_ref: (at, chips + chip_ref[0] // 2)),
                pl.BlockSpec((size, 128), lambda at, chip_ref: (at, tail_at)),
            ],
            out_specs=[
                pl.BlockSpec((span + rows + RATE_ROWS, size), lambda at, chip_ref: (0, at)),
                pl.BlockSpec((8, size), lambda at, chip_ref: (0, at)),
            ],
        ),
        out_shape=[
            jax.ShapeDtypeStruct((span + rows + RATE_ROWS, D), bf16),
            jax.ShapeDtypeStruct((8, D), f32),
        ],
    )(chip, w_pair, w_pair, w_pair)


def project_blocks(first, blocks, tokens, gain, weight, old=()):
    columns = weight.shape[0]
    count = len(tokens)

    def kernel(*refs):
        gain_ref, weight_ref = refs[count : count + 2]
        normed_ref, main_ref = refs[-2:]
        for at in range(count):

            @pl.when(pl.program_id(0) == at)
            def one(tokens_ref=refs[at]):
                wide = tokens_ref[...].astype(f32)
                scale = lax.rsqrt(jnp.mean(wide * wide, axis=1, keepdims=True) + norm_epsilon)
                low = (wide * scale * gain_ref[...]).astype(bf16)
                normed_ref[...] = low
                main_ref[...] = dot_nt(weight_ref[...], low).astype(bf16)

    return pl.pallas_call(
        kernel,
        grid=(count,),
        in_specs=[pl.BlockSpec((GROUP, D), lambda i: (0, 0))] * count
        + [
            pl.BlockSpec((1, D), lambda i: (0, 0)),
            pl.BlockSpec((columns, D), lambda i: (0, 0)),
        ]
        + [pl.BlockSpec(memory_space=pl.ANY)] * len(old),
        out_specs=[
            pl.BlockSpec((GROUP, D), lambda i: (first + i, 0)),
            pl.BlockSpec((columns, GROUP), lambda i: (0, first + i)),
        ],
        out_shape=[
            jax.ShapeDtypeStruct((blocks * GROUP, D), bf16),
            jax.ShapeDtypeStruct((columns, blocks * GROUP), bf16),
        ],
        input_output_aliases={count + 2: 0, count + 3: 1} if old else {},
        compiler_params=pltpu.CompilerParams(vmem_limit_bytes=52 * 2**20),
        cost_estimate=pl.CostEstimate(
            flops=count * 2 * GROUP * D * columns * 2,
            bytes_accessed=count * (GROUP * D * 4 + columns * GROUP * 2) + columns * D * 2,
            transcendentals=0,
        ),
    )(*tokens, gain, weight, *old)


def merge_part(heads, grads_ref, part_ref, held):
    for head in range(heads):
        for which in range(3):
            low = (3 * head + which) * HD
            there = spot(heads, head, which)
            held[there, :] = (
                grads_ref[there, :].astype(f32) + part_ref[0, low : low + HD, :].astype(f32)
            ).astype(bf16)
    end = 3 * heads * HD
    held[end:, :] = grads_ref[end:, :]


def merge_blocks(chip, groups, grads, grad_part, normed):
    columns, tokens = grads.shape
    chips, part_rows, width = grad_part.shape
    heads = part_rows // (3 * HD)
    blocks = tokens // width
    cut = D // groups

    def kernel(chip_ref, grads_ref, part_ref, normed_ref, weight_out, total, held):
        at = pl.program_id(0)
        merge_part(heads, grads_ref, part_ref, held)
        part = dot_nn(held[...], normed_ref[...])

        @pl.when(at == 0)
        def begin():
            total[...] = part

        @pl.when(at > 0)
        def more():
            total[...] += part

        @pl.when(at == blocks - 1)
        def end():
            for group in range(groups):
                weight_out[group] = total[:, group * cut : (group + 1) * cut].astype(bf16)

    return pl.pallas_call(
        kernel,
        grid_spec=pltpu.PrefetchScalarGridSpec(
            num_scalar_prefetch=1,
            grid=(blocks,),
            in_specs=[
                pl.BlockSpec((columns, width), lambda at, chip_ref: (0, at)),
                pl.BlockSpec((1, part_rows, width), lambda at, chip_ref: (at ^ chip_ref[0], 0, 0)),
                pl.BlockSpec((width, D), lambda at, chip_ref: (at, 0)),
            ],
            out_specs=pl.BlockSpec((groups, columns, cut), lambda at, chip_ref: (0, 0, 0)),
            scratch_shapes=[pltpu.VMEM((columns, D), f32), pltpu.VMEM((columns, width), bf16)],
        ),
        out_shape=jax.ShapeDtypeStruct((groups, columns, cut), bf16),
        compiler_params=pltpu.CompilerParams(vmem_limit_bytes=44 * 2**20),
        cost_estimate=pl.CostEstimate(
            flops=2 * tokens * D * columns * 2,
            bytes_accessed=tokens * (D * 2 + columns * 4),
            transcendentals=0,
        ),
    )(chip, grads, grad_part, normed)


def back_blocks(chip, first, count, grads, grad_part, weight):
    columns = grads.shape[0]
    part_rows = grad_part.shape[1]
    heads = part_rows // (3 * HD)

    def kernel(chip_ref, grads_ref, part_ref, weight_ref, own_ref, other_ref, held):
        merge_part(heads, grads_ref, part_ref, held)
        out = dot_tn(held[...], weight_ref[...]).astype(bf16)

        @pl.when(pl.program_id(0) % 2 == 0)
        def own():
            own_ref[0] = out

        @pl.when(pl.program_id(0) % 2 == 1)
        def other():
            other_ref[0] = out

    block = pl.BlockSpec((1, GROUP, D), lambda at, chip_ref: (at // 2, 0, 0))
    blocks = jax.ShapeDtypeStruct((count, GROUP, D), bf16)
    return pl.pallas_call(
        kernel,
        grid_spec=pltpu.PrefetchScalarGridSpec(
            num_scalar_prefetch=1,
            grid=(2 * count,),
            in_specs=[
                pl.BlockSpec((columns, GROUP), lambda at, chip_ref: (0, 2 * first + at)),
                pl.BlockSpec(
                    (1, part_rows, GROUP),
                    lambda at, chip_ref: ((first + at // 2) ^ chip_ref[0], 0, at % 2),
                ),
                pl.BlockSpec(
                    (columns, D), lambda at, chip_ref: (0, 0), pipeline_mode=pl.Buffered(1)
                ),
            ],
            out_specs=[block, block],
            scratch_shapes=[pltpu.VMEM((columns, GROUP), bf16)],
        ),
        out_shape=[blocks, blocks],
        compiler_params=pltpu.CompilerParams(vmem_limit_bytes=32 * 2**20),
        cost_estimate=pl.CostEstimate(
            flops=count * 4 * GROUP * D * columns * 2,
            bytes_accessed=count * 2 * GROUP * (D * 2 + columns * 4),
            transcendentals=0,
        ),
    )(chip, grads, grad_part, weight)


def ffn_chunk(place, chunks, normed, grad, w_gate_up, w_down, old=()):
    own = w_down.shape[0]
    given = [piece for block in (*normed, *grad) for piece in block]
    spans, at = [], 0
    for block in (*normed, *grad):
        spans.append(slice(at, at + len(block)))
        at += len(block)
    count = len(given)

    def kernel(*refs):
        w_gate_up_ref, w_down_ref = refs[count : count + 2]
        all_normed, all_grad, all_hidden, all_grads, out_ref, back_ref = refs[-6:]
        for at in range(2):

            @pl.when(pl.program_id(0) == at)
            def one(normed_refs=refs[spans[at]], grad_refs=refs[spans[2 + at]]):
                low = jnp.concatenate([ref[...] for ref in normed_refs], axis=0)
                grad_low = jnp.concatenate([ref[...] for ref in grad_refs], axis=0)
                all_normed[...] = low
                all_grad[...] = grad_low
                gate = dot_nn(low, w_gate_up_ref[:, :own])
                up = dot_nn(low, w_gate_up_ref[:, own:])
                gate_sigmoid = jax.nn.sigmoid(gate)
                gate_silu = gate * gate_sigmoid
                hidden = (gate_silu * up).astype(bf16)
                all_hidden[...] = hidden
                out_ref[0] = dot_nn(hidden, w_down_ref[...]).astype(bf16)
                grad_hidden = dot_nt(grad_low, w_down_ref[...])
                slope = gate_sigmoid * (1.0 + gate * (1.0 - gate_sigmoid))
                all_grads[:, :own] = (grad_hidden * up * slope).astype(bf16)
                all_grads[:, own:] = (grad_hidden * gate_silu).astype(bf16)
                back_ref[0] = dot_nt(all_grads[...], w_gate_up_ref[...]).astype(bf16)

    tokens = chunks * 2 * GROUP
    once = pl.Buffered(1)
    return pl.pallas_call(
        kernel,
        grid=(2,),
        in_specs=[
            pl.BlockSpec(piece.shape, lambda i: (0, 0), pipeline_mode=once) for piece in given
        ]
        + [
            pl.BlockSpec((D, 2 * own), lambda i: (0, 0), pipeline_mode=once),
            pl.BlockSpec((own, D), lambda i: (0, 0), pipeline_mode=once),
        ]
        + [pl.BlockSpec(memory_space=pl.ANY)] * len(old),
        out_specs=[
            pl.BlockSpec((GROUP, D), lambda i: (2 * place + i, 0)),
            pl.BlockSpec((GROUP, D), lambda i: (2 * place + i, 0)),
            pl.BlockSpec((GROUP, own), lambda i: (2 * place + i, 0)),
            pl.BlockSpec((GROUP, 2 * own), lambda i: (2 * place + i, 0)),
            pl.BlockSpec((1, GROUP, D), lambda i: (i, 0, 0)),
            pl.BlockSpec((1, GROUP, D), lambda i: (i, 0, 0)),
        ],
        out_shape=[
            jax.ShapeDtypeStruct((tokens, D), bf16),
            jax.ShapeDtypeStruct((tokens, D), bf16),
            jax.ShapeDtypeStruct((tokens, own), bf16),
            jax.ShapeDtypeStruct((tokens, 2 * own), bf16),
            jax.ShapeDtypeStruct((2, GROUP, D), bf16),
            jax.ShapeDtypeStruct((2, GROUP, D), bf16),
        ],
        input_output_aliases={count + 2 + at: at for at in range(len(old))},
        compiler_params=pltpu.CompilerParams(vmem_limit_bytes=58 * 2**20),
        cost_estimate=pl.CostEstimate(
            flops=2 * GROUP * D * own * 12, bytes_accessed=20 * GROUP * D, transcendentals=2 * GROUP * own
        ),
    )(*given, w_gate_up, w_down, *old)


def context_product(context, grad_far, persist, grad_side, w_pair):
    size = 256
    columns = grad_far.shape[0]

    def kernel(context_ref, far_ref, persist_ref, side_ref, weight_ref, out_ref):
        out_ref[:, :columns] = (
            dot_nt(context_ref[...], far_ref[...]) + dot_nt(persist_ref[...], side_ref[...])
        ).astype(bf16)
        own = dot_nn(weight_ref[...], side_ref[...]).astype(bf16)
        out_ref[:, columns:] = jnp.concatenate([own, jnp.zeros((size, 128 - NP), bf16)], axis=1)

    once = pl.Buffered(1)
    return pl.pallas_call(
        kernel,
        grid=(D // size,),
        in_specs=[
            pl.BlockSpec((size, context.shape[1]), lambda at: (at, 0)),
            pl.BlockSpec(grad_far.shape, lambda at: (0, 0), pipeline_mode=once),
            pl.BlockSpec((size, NP), lambda at: (at, 0)),
            pl.BlockSpec(grad_side.shape, lambda at: (0, 0), pipeline_mode=once),
            pl.BlockSpec((size, columns), lambda at: (at, 0)),
        ],
        out_specs=pl.BlockSpec((size, columns + 128), lambda at: (at, 0)),
        out_shape=jax.ShapeDtypeStruct((D, columns + 128), bf16),
        compiler_params=pltpu.CompilerParams(vmem_limit_bytes=32 * 2**20),
        cost_estimate=pl.CostEstimate(
            flops=2 * D * columns * context.shape[1],
            bytes_accessed=4 * D * columns * 2,
            transcendentals=0,
        ),
    )(context, grad_far, persist, grad_side, w_pair)


def tokens_product(left, right):
    tokens, rows = left.shape
    columns = right.shape[1]
    size = 2 * GROUP
    steps = tokens // size

    def kernel(left_ref, right_ref, out_ref, total):
        at = pl.program_id(0)
        part = dot_tn(left_ref[...], right_ref[...])

        @pl.when(at == 0)
        def first():
            total[...] = part

        @pl.when(at > 0)
        def more():
            total[...] += part

        @pl.when(at == steps - 1)
        def last():
            out_ref[...] = total[...].astype(bf16)

    return pl.pallas_call(
        kernel,
        grid=(steps,),
        in_specs=[
            pl.BlockSpec((size, rows), lambda at: (at, 0)),
            pl.BlockSpec((size, columns), lambda at: (at, 0)),
        ],
        out_specs=pl.BlockSpec((rows, columns), lambda at: (0, 0)),
        out_shape=jax.ShapeDtypeStruct((rows, columns), bf16),
        scratch_shapes=[pltpu.VMEM((rows, columns), f32)],
        compiler_params=pltpu.CompilerParams(vmem_limit_bytes=50 * 2**20),
        cost_estimate=pl.CostEstimate(
            flops=2 * tokens * rows * columns,
            bytes_accessed=2 * tokens * (rows + columns),
            transcendentals=0,
        ),
    )(left, right)


def matmul(left, right, left_dim, right_dim, out=f32):
    return lax.dot_general(
        left, right, (((left_dim,), (right_dim,)), ((), ())), preferred_element_type=f32
    ).astype(out)


def core_swap(value):
    return lax.ppermute(value, "core", [(0, 1), (1, 0)])


def gather_chips(value):
    return lax.all_gather(value, ("dp", "chip"), axis=0, tiled=True)


def scatter_chips(value):
    return lax.psum_scatter(value, ("dp", "chip"), scatter_dimension=0, tiled=True)


def after(value, *events):
    return lax.optimization_barrier((value, *events))[0]


def together(*values):
    return lax.optimization_barrier(values)


def chip_swap(value, step):
    count = lax.axis_size("chip")
    return lax.ppermute(value, "chip", [(index, index ^ step) for index in range(count)])


def chip_parts(value):
    count = lax.axis_size("chip")
    if count != 4:
        return [value] + [chip_swap(value, step) for step in range(1, count)]
    middle = value.shape[0] // 2
    along = chip_swap(value, 1)
    across = chip_swap(value, 2)
    corner = jnp.concatenate([chip_swap(along[:middle], 2), chip_swap(across[middle:], 1)], axis=0)
    return [value, along, across, corner]


def corner_sums(corner, parts, *events):
    middle = corner.shape[0] // 2
    from_along = chip_swap(corner[:middle], 1)
    from_across = chip_swap(corner[middle:], 2)
    if events:
        from_along, from_across = after(from_along, *events), after(from_across, *events)
    from_along, from_across = from_along.astype(f32), from_across.astype(f32)
    first = jnp.concatenate(
        [parts[1][:middle].astype(f32), parts[1][middle:].astype(f32) + from_across], axis=0
    )
    second = jnp.concatenate(
        [parts[2][:middle].astype(f32) + from_along, parts[2][middle:].astype(f32)], axis=0
    )
    return first.astype(bf16), second.astype(bf16)


def side_sums(own, first, second, *events):
    first, second = chip_swap(first, 1), chip_swap(second, 2)
    if events:
        first, second = after(first, *events), after(second, *events)
    return own.astype(f32) + first.astype(f32) + second.astype(f32)


def chip_sums(parts):
    count = lax.axis_size("chip")
    if count != 4:
        total = parts[0].astype(f32)
        for step in range(1, count):
            total = total + chip_swap(parts[step].astype(bf16), step).astype(f32)
        return total
    return side_sums(parts[0], *corner_sums(parts[3].astype(bf16), parts))


def line_gather(value):
    count = lax.axis_size("dp")
    index = lax.axis_index("dp")
    up = down = value
    found = [value] * count
    for step in range(1, count):
        up = lax.ppermute(up, "dp", [(at, at + 1) for at in range(count - 1)])
        down = lax.ppermute(down, "dp", [(at + 1, at) for at in range(count - 1)])
        for at in range(count):
            found[at] = jnp.where(
                index - at == step, up, jnp.where(at - index == step, down, found[at])
            )
    return jnp.stack(found)


def sum_everywhere(value, marks):
    steps = []
    for axis in ("dp", "core", "chip"):
        step = 1
        while step < lax.axis_size(axis):
            steps.append((axis, step))
            step *= 2
    for at, (axis, step) in enumerate(steps):
        pairs = [(index, index ^ step) for index in range(lax.axis_size(axis))]
        other = lax.ppermute(value, axis, pairs)
        value = value + (after(other, marks[at]) if at < len(marks) else other)
    return value


def by_core(core, mine, other, axis=0):
    return jnp.where(
        core == 0,
        jnp.concatenate([mine, other], axis=axis),
        jnp.concatenate([other, mine], axis=axis),
    )


def inverse_rms(values):
    return lax.rsqrt(jnp.mean(values * values, axis=-1, keepdims=True) + norm_epsilon)


def norm_back(grad_normed, values, inverse, gain):
    normal = values * inverse
    scaled = grad_normed * gain
    return inverse * (scaled - normal * jnp.mean(scaled * normal, axis=-1, keepdims=True))


def on_device(
    inputs,
    segments,
    attn_gain,
    query_weight,
    key_weight,
    value_weight,
    output_weight,
    persistent,
    memory_first,
    memory_second,
    rate_weight,
    decay_logit,
    momentum_logit,
    ffn_gain,
    gate_weight,
    up_weight,
    down_weight,
    cotangent,
):
    groups, chips, core_count = (lax.axis_size("dp"), lax.axis_size("chip"), 2)
    core = lax.axis_index("core")
    chip = lax.axis_index("chip")
    position = chip * core_count + core
    chain = chips * core_count
    devices = groups * chain
    scale = HD ** (-0.5)
    half = D // 2
    core_heads = H // core_count
    heads = core_heads // chips
    rows = heads * HD
    width = 2 * GROUP
    all_rows = 3 * rows + RATE_ROWS
    shard = query_weight.shape[0]
    ff_own = gate_weight.shape[1] // chain
    pieces = devices // 2
    per_head = max(HD // shard, 1)
    near = 2 * shard == HD and core_heads == heads * chips

    tokens = inputs[0]
    grad_out = cotangent[0]

    if chips == 4:
        along, across = chip_swap(tokens, 1), chip_swap(tokens, 2)
    w_sides = pack_weights(
        chips,
        heads,
        key_weight,
        value_weight,
        query_weight,
        rate_weight,
        jnp.stack([attn_gain, ffn_gain], axis=1),
        persistent,
    )
    w_side = lax.dynamic_index_in_dim(w_sides, core, 0, keepdims=False)
    w_side_other = core_swap(lax.dynamic_index_in_dim(w_sides, 1 - core, 0, keepdims=False))
    w_pair = gather_chips(by_core(core, w_side, w_side_other))
    w_context = w_pair[:, : 2 * half]
    w_tail = w_pair[:, 3 * half :]
    persist = w_tail[:, :NP]
    if chips == 4:
        cut = GROUP // 2
        corner = jnp.concatenate(
            [chip_swap(along[:cut], 2), chip_swap(across[cut:], 1)], axis=0
        )
        token_halves = [tokens, along, across, corner]
    else:
        token_halves = chip_parts(tokens)
    mem_shard = jnp.concatenate([memory_first, memory_second], axis=1)
    if chips == 4:
        mem_shard = after(mem_shard, corner)
        gate_weight_, up_weight_ = after(gate_weight, corner), up_weight
    else:
        gate_weight_, up_weight_ = gate_weight, up_weight
    if near:
        mem_pair = by_core(core, mem_shard, core_swap(mem_shard))
        mem_line = line_gather(mem_pair).reshape(groups * 2 * shard, 2 * MH)
        mem_mine = lax.dynamic_slice_in_dim(mem_line, core * rows, rows, 0)
    else:
        mem_all = lax.all_gather(mem_shard, ("dp", "chip", "core"), axis=0, tiled=True)
        mem_all = lax.dynamic_slice_in_dim(mem_all, core * half, half, 0)
        mem_all = mem_all.reshape(heads, chips, HD, 2 * MH)
        mem_mine = lax.dynamic_index_in_dim(mem_all, chip, 1, keepdims=False).reshape(rows, 2 * MH)
    mem_mine = mem_mine.astype(f32)
    first_init, second_init = mem_mine[:, :MH], mem_mine[:, MH:]
    w_gate_up = lax.all_to_all(
        pack_columns(chain, gate_weight_, up_weight_), ("chip", "core"), 0, 0, tiled=True
    ).reshape(chain * shard, 2 * ff_own)
    chip_index = chip.astype(jnp.int32)[None]
    if chips == 4 and 2 * rows % 128 == 0:
        w_flat, gains = take_heads(chip_index, chips, heads, w_pair)
    else:
        w_main = jnp.concatenate(
            [
                lax.dynamic_slice_in_dim(w_pair, chip * 2 * rows, 2 * rows, 1),
                lax.dynamic_slice_in_dim(w_pair, 2 * half + chip * rows, rows, 1),
                lax.dynamic_slice_in_dim(w_tail, NP + 2 + chip * heads, heads, 1),
                jnp.zeros((D, RATE_ROWS - heads), bf16),
            ],
            axis=1,
        )
        w_flat = w_main.T
        gains = w_tail[:, NP : NP + 2].astype(f32).T
    w_flat = after(w_flat, w_gate_up)
    gain_one, gain_two = gains[:1], gains[1:2]

    out_order = []
    for side in range(2):
        for piece in range(pieces):
            spot_, part = divmod(piece, per_head)
            at_chip, turn = divmod(spot_, heads)
            source = side * pieces + (turn * chips + at_chip) * per_head + part
            out_order.append((source, 2 * piece + side))
    out_moved = lax.ppermute(output_weight, ("dp", "chip", "core"), out_order)
    if chips == 4:
        w_lines = lax.all_gather(
            jnp.concatenate([after(out_moved, w_pair), down_weight], axis=0), "dp", axis=0
        )
        out_lines = w_lines[:, :shard]
        w_down = w_lines[:, shard:].reshape(-1, D)
        w_gate_up = lax.all_gather(after(w_gate_up, w_pair), "dp", axis=0, tiled=True)
    else:
        w_gate_up = lax.all_gather(w_gate_up, "dp", axis=0, tiled=True)
        w_down = lax.all_gather(down_weight, "dp", axis=0, tiled=True)
        w_output = gather_chips(out_moved)

    ids = segments[0].reshape(chain, GROUP)
    first_id, last_id = ids[:, 0], ids[:, GROUP - 1]
    before = jnp.concatenate([first_id[:1], ids[:-1, GROUP - 1]])
    joined = jnp.logical_and(jnp.arange(chain) > 0, first_id == before)
    carry = jnp.logical_and(joined, first_id == last_id)
    kept = jnp.logical_and(joined[:, None], ids == first_id[:, None])
    retain = kept.astype(f32)[:, None, :]
    update = (ids == last_id[:, None]).astype(f32)[:, None, :]
    flags = jnp.stack(
        [
            carry.astype(jnp.int32),
            jnp.any(kept, axis=1).astype(jnp.int32),
            jnp.logical_not(jnp.all(kept, axis=1)).astype(jnp.int32),
            jnp.full((chain,), core, jnp.int32),
            jnp.full((chain,), chip, jnp.int32),
        ]
    )
    pair_ids = jnp.stack(
        [
            lax.dynamic_index_in_dim(ids, position, keepdims=False),
            lax.dynamic_index_in_dim(ids, chip * core_count + 1 - core, keepdims=False),
        ]
    )
    id_row, id_col = pair_ids[:, None, :], pair_ids[:, :, None]
    core_index = core.astype(jnp.int32)[None]
    decay = jax.nn.sigmoid(decay_logit)
    momentum = jax.nn.sigmoid(momentum_logit)

    def own_heads(value):
        return lax.dynamic_index_in_dim(
            value.reshape(core_count, heads, chips)[core], chip, 1, keepdims=False
        )

    scalars = jnp.stack([own_heads(1.0 - decay), own_heads(momentum)])

    if chips == 4:
        grad_low = after(grad_out, w_flat)
        along_low, across_high = chip_swap(grad_low[:cut], 1), chip_swap(grad_low[cut:], 2)
    token_blocks = []
    for part in token_halves:
        token_blocks += [part, core_swap(part)]
    placed = ()
    for start in range(0, chain, 8):
        placed = project_blocks(
            start, chain, token_blocks[start : start + 8], gain_one, w_flat, placed
        )
    normed_all, main = placed
    if chips == 4:
        main, along_low, across_high = together(main, along_low, across_high)


    def pair_rows(own):
        return jnp.concatenate([own, core_swap(own)], axis=0)

    if chips == 4:
        corner_along, corner_across = chip_swap(along_low, 2), chip_swap(across_high, 1)
    recalled, saved = memory_forward(
        flags, main, retain, update, first_init, second_init, scalars, chips
    )
    normed = normed_all[:width]
    low = matmul(w_pair[:, : 3 * half], normed, 0, 1, bf16)
    side = matmul(w_context, persist, 0, 0, bf16)
    if chips == 4:
        recalled, corner_along, corner_across, out_lines = together(
            recalled, corner_along, corner_across, out_lines
        )
        out_along, out_across = chip_swap(out_lines, 1), chip_swap(out_lines, 2)
    recalled = after(lax.all_to_all(recalled, "chip", 0, 0, tiled=True), low, side)
    if chips == 4:
        recalled, out_along, out_across = together(recalled, out_along, out_across)
    recalled = recalled.reshape(chips, heads, HD, width).swapaxes(0, 1).reshape(half, width)
    context = by_core(core, recalled, core_swap(recalled))
    if chips == 4:
        upper = groups // 2
        out_corner = (chip_swap(out_along[:upper], 2), chip_swap(out_across[upper:], 1))
        grad_low = after(grad_out, context)
        along_high, across_low = chip_swap(grad_low[cut:], 1), chip_swap(grad_low[:cut], 2)

    far = matmul(w_context, context, 0, 0, bf16)
    mixed, total = attention_forward(scale, core_index, low, far, side, id_row, id_col)

    if chips == 4:
        mixed, along_high, across_low, *out_corner = together(
            mixed, along_high, across_low, *out_corner
        )
        stacked = jnp.stack([out_lines, out_along, out_across, jnp.concatenate(out_corner, axis=0)])
        w_output = jnp.stack(
            [
                lax.dynamic_index_in_dim(stacked, chip ^ at, 0, keepdims=False)
                for at in range(chips)
            ],
            axis=1,
        ).reshape(half, D)

    def pair_sum(left, right, left_dim, right_dim):
        def block(which):
            return lax.slice_in_dim(
                left, which * GROUP, (which + 1) * GROUP, axis=1 - left_dim
            )

        other = core_swap(matmul(block(1), right, left_dim, right_dim, bf16))
        return matmul(block(0), right, left_dim, right_dim) + other.astype(f32)

    middle = tokens.astype(f32) + pair_sum(mixed, w_output, 0, 0)
    inverse_two = inverse_rms(middle)
    normed_own = (middle * inverse_two * gain_two).astype(bf16)
    def chunk(step, normed, grad, arrays):
        def both(pieces):
            return (tuple(pieces), tuple(core_swap(piece) for piece in pieces))

        *arrays, out, back = ffn_chunk(
            step, chips, both(normed), both(grad), w_gate_up, w_down, arrays
        )
        return tuple(arrays), out, back

    def over_cores(part):
        return part[0].astype(f32) + core_swap(part[1]).astype(f32)

    def halves(value, first, second):
        return chip_swap(value[:cut], first), chip_swap(value[cut:], second)

    if chips == 4:
        first = halves(normed_own, 1, 2)
        arrays, out_own, back_own = chunk(0, (normed_own,), (grad_out,), ())
        arrays, first = together(arrays, first)
        later = after(normed_own, arrays[0])
        second = (chip_swap(later[cut:], 1), chip_swap(later[:cut], 2))
        arrays, out_first, back_first = chunk(1, first, (along_low, across_high), arrays)
        arrays, second = together(arrays, second)
        corner = (
            chip_swap(after(first[0], arrays[0]), 2),
            chip_swap(after(first[1], arrays[0]), 1),
        )
        arrays, out_second, back_second = chunk(2, second, (along_high, across_low), arrays)
        arrays, corner = together(arrays, corner)
        sent = halves(after(over_cores(back_first), arrays[0]).astype(bf16), 1, 2)
        arrays, out_corner, back_corner = chunk(3, corner, (corner_along, corner_across), arrays)
        back_corner, sent = together(back_corner, sent)
        all_normed, all_grad, all_hidden, all_grad_gate_up = arrays
        corner_low = over_cores(back_corner).astype(bf16)
        from_corner = halves(corner_low, 1, 2)
        grad_down_w = tokens_product(after(all_hidden, corner_low), all_grad)
        grad_down_w, from_corner = together(grad_down_w, from_corner)

        def add_corner(part, from_corner):
            from_along, from_across = from_corner
            return (
                jnp.concatenate([part[:cut] + from_across, part[cut:] + from_along], axis=0)
            ).astype(bf16)

        last = add_corner(over_cores(back_second), from_corner)
        grad_gate_up_w = tokens_product(after(all_normed, last), all_grad_gate_up)
        grad_gate_up_w, last = together(grad_gate_up_w, halves(last, 1, 2))

        def all_parts(own, sent, last):
            low = own[:cut] + sent[0].astype(f32) + last[1].astype(f32)
            high = own[cut:] + sent[1].astype(f32) + last[0].astype(f32)
            return jnp.concatenate([low, high], axis=0)

        grad_normed_two = all_parts(over_cores(back_own), sent, last)
        out_corner = over_cores(after(out_corner, grad_gate_up_w)).astype(bf16)
        out_first = over_cores(after(out_first, grad_gate_up_w)).astype(bf16)
        out_second = over_cores(after(out_second, grad_gate_up_w))
        out_own = over_cores(after(out_own, grad_gate_up_w))
    else:
        grads_by_step, normeds_by_step = chip_parts(grad_out), chip_parts(normed_own)
        outs, backs, arrays = [], [], ()
        for step in range(chips):
            arrays, out, back = chunk(step, (normeds_by_step[step],), (grads_by_step[step],), arrays)
            outs.append(over_cores(out))
            backs.append(over_cores(back))
        all_normed, all_grad, all_hidden, all_grad_gate_up = arrays
        grad_normed_two = chip_sums(backs)
        grad_down_w = tokens_product(all_hidden, all_grad)
        grad_gate_up_w = tokens_product(all_normed, all_grad_gate_up)
    grad_middle = grad_out.astype(f32) + norm_back(grad_normed_two, middle, inverse_two, gain_two)
    down_part = lax.psum_scatter(grad_down_w, "dp", scatter_dimension=0, tiled=True).astype(f32)
    gate_up_scattered = lax.psum_scatter(grad_gate_up_w, "dp", scatter_dimension=0, tiled=True)

    grad_attended = pair_rows(grad_middle.astype(bf16))
    grad_mixed = matmul(w_output, grad_attended, 1, 1, bf16)
    grad_output_w = matmul(mixed, grad_attended, 1, 0, bf16)
    output_part = lax.psum_scatter(grad_output_w, "dp", scatter_dimension=0, tiled=True)
    events = ()
    if chips == 4:
        from_corner = halves(after(out_corner, grad_normed_two), 1, 2)
        out_last = add_corner(out_second, after(from_corner, grad_mixed))
        out_sent = halves(after(out_first, grad_normed_two), 1, 2)
        events = (out_last,)
    grad_part, grad_far, grad_side = attention_backward(
        scale,
        core_index,
        low,
        far,
        side,
        id_row,
        id_col,
        mixed,
        total,
        after(grad_mixed, grad_output_w, *events),
    )
    grad_side = grad_side.astype(bf16)
    if chips == 4:
        grad_far, out_sent, out_last = together(grad_far, out_sent, halves(out_last, 1, 2))

    def half_rows(which):
        return lax.dynamic_slice(w_pair, (which * half, 0), (half, 2 * half))

    pull_other = core_swap(matmul(half_rows(1 - core), grad_far, 1, 0, bf16))
    pull = (matmul(half_rows(core), grad_far, 1, 0) + pull_other.astype(f32)).astype(bf16)
    pull = pull.reshape(heads, chips, HD, width).swapaxes(0, 1).reshape(chips, rows, width)
    ready = pull
    pull = lax.all_to_all(pull, "chip", 0, 0, tiled=True)
    grad_part = lax.all_to_all(
        after(grad_part.reshape(chips, 3 * rows, width), pull), "chip", 0, 0, tiled=True
    )
    grad_context_w = context_product(
        context, after(grad_far, ready), persist, grad_side, w_pair
    )
    grad_context_w, pull = together(grad_context_w, pull)
    context_part = lax.psum_scatter(grad_context_w, "dp", scatter_dimension=0, tiled=True)
    context_part = context_part.reshape(chips, 2 * shard, 2 * half + 128)
    grads, grad_first, grad_second, grad_scalars = memory_backward(
        flags,
        main,
        retain,
        update,
        first_init,
        second_init,
        scalars,
        saved,
        after(pull, down_part, gate_up_scattered, grad_context_w),
    )
    if chips == 4:
        out_sum = all_parts(after(out_own, grads), out_sent, out_last)
    else:
        out_sum = chip_sums(outs)
    result = (middle + out_sum).astype(bf16)
    grads, grad_part, result = together(grads, grad_part, result)
    grad_mem = jnp.concatenate([grad_first, grad_second], axis=1).astype(bf16)
    corner_own, corner_other = back_blocks(chip_index, chips - 1, 1, grads, grad_part, w_flat)
    corner_other = core_swap(corner_other)
    side_own, side_other = back_blocks(
        chip_index, 0, chips - 1, grads, after(grad_part, corner_other), w_flat
    )
    corner_low = (corner_own[0].astype(f32) + corner_other[0].astype(f32)).astype(bf16)
    side_other = core_swap(side_other)
    grad_heads_w = merge_blocks(
        chip_index, groups, grads, after(grad_part, corner_low, side_own), normed_all
    )
    if chips == 4:
        grad_heads_w, side_other, from_corner = together(
            grad_heads_w, side_other, halves(corner_low, 1, 2)
        )
    heads_sum = lax.psum_scatter(grad_heads_w, "dp", scatter_dimension=0)
    if near:
        spread = jnp.zeros((groups, 2 * shard, 2 * MH), bf16)
        spread = lax.dynamic_update_slice_in_dim(
            spread, after(grad_mem, grad_heads_w).reshape(heads, 2 * shard, 2 * MH), core * heads, 0
        )
        mem_line = lax.psum_scatter(
            spread.reshape(groups * 2 * shard, 2 * MH), "dp", scatter_dimension=0, tiled=True
        )
    else:
        mem_line = grad_mem
    grad_normeds = [
        side_own[step].astype(f32) + side_other[step].astype(f32) for step in range(chips - 1)
    ]
    grad_normeds.append(corner_low)
    tokens_wide = tokens.astype(f32)
    if chips == 4:
        from_along, from_across = (part.astype(f32) for part in from_corner)
        first_sum = jnp.concatenate(
            [grad_normeds[1][:cut], grad_normeds[1][cut:] + from_across], axis=0
        ).astype(bf16)
        second_sum = jnp.concatenate(
            [grad_normeds[2][:cut] + from_along, grad_normeds[2][cut:]], axis=0
        ).astype(bf16)
        heads_sum = after(heads_sum, first_sum, second_sum)
        marks = (corner_low, first_sum)
    else:
        marks = (corner_low, side_own)
    heads_sum = heads_sum.T
    heads_part = lax.all_to_all(
        jnp.concatenate(
            [
                gate_up_scattered.reshape(chain, shard, 2 * ff_own),
                heads_sum.reshape(chain, shard, all_rows),
            ],
            axis=2,
        ),
        ("chip", "core"),
        0,
        0,
        tiled=True,
    )
    output_part = output_part.reshape(chips, shard, 2, half).swapaxes(1, 2)
    context_part = jnp.concatenate(
        [context_part, output_part.reshape(chips, 2 * shard, half)], axis=2
    )
    context_parts = [
        lax.dynamic_index_in_dim(after(context_part, grad_heads_w), chip ^ step, 0, keepdims=False)
        for step in range(chips)
    ]
    if chips == 4:
        context_first, context_second = corner_sums(
            context_parts[3].astype(bf16), context_parts, heads_sum
        )
        grad_normed = side_sums(grad_normeds[0], first_sum, second_sum, heads_sum)
        context_part = side_sums(context_parts[0], context_first, context_second).astype(bf16)
    else:
        grad_normed = chip_sums(grad_normeds)
        context_part = chip_sums(context_parts).astype(bf16)
    grad_tokens_one = norm_back(grad_normed, tokens_wide, inverse_rms(tokens_wide), gain_one)
    grad_inputs = (grad_middle + grad_tokens_one).astype(bf16)
    marks = (corner_own, side_own, grad_heads_w, grad_inputs, grad_inputs)
    grad_inputs, heads_part = together(grad_inputs, heads_part)

    def own_rows(part):
        mine = lax.dynamic_slice_in_dim(part, core * shard, shard, 0)
        other = core_swap(lax.dynamic_slice_in_dim(part, (1 - core) * shard, shard, 0))
        return mine, other

    output_part = jnp.concatenate(
        [context_part[:shard, 2 * half + 128 :], context_part[shard:, 2 * half + 128 :]], axis=1
    )
    mine, other = own_rows(context_part[:, : 2 * half + 128])
    persist_part = (mine.astype(f32) + other.astype(f32))[:, 2 * half : 2 * half + NP]
    by_side = by_core(core, mine[None], other[None])
    grad_keys_own, grad_values_own, grad_queries_own, grad_rates_own, gain_one_part = (
        unpack_weights(
            chips,
            heads,
            2 * ff_own,
            heads_part,
            by_side,
            key_weight,
            value_weight,
            query_weight,
            rate_weight,
            attn_gain[:, None],
        )
    )
    gate_part, up_part, gain_two_part = unpack_columns(
        heads_part, gate_weight, up_weight, ffn_gain[:, None]
    )
    if near:
        mine, other = own_rows(after(mem_line, heads_sum))
        mem_part = mine.astype(f32) + other.astype(f32)
    else:
        spread = jnp.zeros((heads, chips, HD, 2 * MH), bf16)
        spread = lax.dynamic_update_slice_in_dim(
            spread, grad_mem.reshape(heads, 1, HD, 2 * MH), chip, 1
        ).reshape(half, 2 * MH)
        spread = lax.dynamic_update_slice_in_dim(
            jnp.zeros((D, 2 * MH), bf16), spread, core * half, 0
        )
        mem_part = lax.psum_scatter(
            spread, ("dp", "chip", "core"), scatter_dimension=0, tiled=True
        ).astype(f32)
    scalar_sums = jnp.sum(grad_scalars, axis=1)[: 2 * heads].reshape(1, heads, 1, 2)
    spots = lax.dynamic_update_slice(
        jnp.zeros((core_count, heads, chips, 2), f32), scalar_sums, (core, 0, chip, 0)
    )
    sums = sum_everywhere(spots.reshape(H, 2), marks)
    grad_decay = sums[:, 0] * decay * (1.0 - decay)
    grad_momentum = sums[:, 1] * momentum * (1.0 - momentum)
    output_own = lax.ppermute(
        output_part, ("dp", "chip", "core"), [(d, s) for s, d in out_order]
    ).astype(f32)
    return (
        result[None],
        grad_inputs[None],
        gain_one_part[:, 0],
        grad_queries_own,
        grad_keys_own,
        grad_values_own,
        output_own,
        persist_part,
        mem_part[:, :MH],
        mem_part[:, MH:],
        grad_rates_own,
        grad_decay,
        grad_momentum,
        gain_two_part[:, 0],
        gate_part,
        up_part,
        down_part,
    )


def solution(mesh):
    split = jax.sharding.Mesh(
        mesh.devices.reshape(mesh.shape["dp"], mesh.shape["seq"] // 2, 2), ("dp", "chip", "core")
    )
    row = P("dp", ("chip", "core"), None)
    vector = P(("dp", "chip", "core"))
    matrix = P(("dp", "chip", "core"), None)
    in_specs = (
        row,
        P("dp", None),
        vector,
        matrix,
        matrix,
        matrix,
        matrix,
        matrix,
        matrix,
        matrix,
        matrix,
        P(),
        P(),
        vector,
        matrix,
        matrix,
        matrix,
        row,
    )
    out_specs = (
        row,
        row,
        vector,
        matrix,
        matrix,
        matrix,
        matrix,
        matrix,
        matrix,
        matrix,
        matrix,
        P(),
        P(),
        vector,
        matrix,
        matrix,
        matrix,
    )
    return jax.shard_map(
        on_device, mesh=split, in_specs=in_specs, out_specs=out_specs, check_vma=False
    )
```
